256 devices in a mesh: group: 4 (over x), sub: 8 (over y, core), leaf: 8 (over z).
Axes of the slice: x: 4, y: 4, z: 8, core: 2. Of those that a mesh axis runs over, the one named last changes fastest.
Arguments:
- points: bfloat16 [524288, 256], P(('group', 'sub', 'leaf')), may hold values from -17 to 17
- right_side: float32 [64, 524288], P(None, ('group', 'sub', 'leaf')), may hold values from -26 to 26
- skel_sub: bfloat16 [8192, 256], P(('group', 'sub')), may hold values from -14 to 14
- skel_group: bfloat16 [1024, 256], P('group'), may hold values from -11 to 11
- skel_top: bfloat16 [256, 256], replicated, may hold values from -9 to 9
- neighbors: int32 [512, 2], P(('group', 'sub', 'leaf')), may hold values from 0 to 511, as said below
- counts: int32 [512], P(('group', 'sub', 'leaf')), may hold values from 0 to 2, as said below
Outputs:
- solution: float32 [64, 524288], P(None, ('group', 'sub', 'leaf'))
- residual: float32 [64, 524288], P(None, ('group', 'sub', 'leaf'))
The draws below stay inside these ranges and needn't reach their ends.
Inputs may be any that keep to these rules, and one draw needn't show every extreme that they name: `neighbors`: row i lists, in its first counts[i] entries, only leaves i - 1 and i + 1, i - 1 first; leaf i lists i + 1 exactly when leaf i + 1 lists i; entries from counts[i] on equal i. `counts`: the number of live entries in the leaf's list; 2 is reached.
All inputs are finite; a program needn't handle non-finite values.
Results may differ from the reference program's by a relative error of at most 0.0045.
Values may be sent and summed in bfloat16 or wider, within the bound.
No kernel may reach another device: no remote copies, remote signals or barrier semaphores. Data moves between devices by JAX's collectives and lax.ppermute only.
A program may use at most 64 MiB of HBM per device.

```python
import math
import jax
import jax.numpy as jnp
from jax import lax

DIM = 256
RHS = 64
LEAF = 1024
SKEL = 256
NB = 2
ITERS = 2
LPD = 2
NLEAVES = 512
NPTS = 524288
SUBPTS = 16384
SUBNODES = 32
GROUPS = 4
N_SUB = 8


latent_dims = 16


centre_scale = 0.7071


def edge_lists(key):
    drawn = (jax.random.randint(key, (NLEAVES - 1,), 0, 5) < 3).astype(jnp.int32)
    between = jnp.arange(NLEAVES - 1, dtype=jnp.int32)
    forced = (between + 1) % (2 * LPD) == LPD
    linked = jnp.where(forced, 1, drawn).astype(jnp.int32)
    lower = jnp.concatenate([jnp.zeros((1,), jnp.int32), linked])
    upper = jnp.concatenate([linked, jnp.zeros((1,), jnp.int32)])
    position = jnp.arange(NLEAVES, dtype=jnp.int32)
    first_entry = jnp.where(lower == 1, position - 1, jnp.where(upper == 1, position + 1, position))
    second_entry = jnp.where((lower == 1) & (upper == 1), position + 1, position)
    return (jnp.stack([first_entry, second_entry], axis=1), lower + upper)


def tree_centres(key):
    keys = jax.random.split(jax.random.fold_in(key, 101), 3)
    coarse = centre_scale * jax.random.truncated_normal(keys[0], -4.0, 4.0, (GROUPS, latent_dims), jnp.float32)
    fine = centre_scale * jax.random.truncated_normal(keys[1], -4.0, 4.0, (SUBNODES, latent_dims), jnp.float32)
    leaves = centre_scale * jax.random.truncated_normal(keys[2], -4.0, 4.0, (NLEAVES, latent_dims), jnp.float32)
    return (coarse, fine, leaves)


def embed(latent):
    return latent[:, jnp.arange(DIM, dtype=jnp.int32) % latent_dims]


def draw_neighbors(key, part):
    listed, tally = edge_lists(key)
    return listed


def draw_counts(key, part):
    listed, tally = edge_lists(key)
    return tally


def draw_points(key, part):
    coarse, fine, leaves = tree_centres(key)
    key = jax.random.fold_in(key, 41)
    keys = jax.random.split(key, 3)
    centre = jnp.repeat(coarse, NLEAVES // GROUPS, axis=0) + jnp.repeat(fine, NLEAVES // SUBNODES, axis=0) + leaves
    spread = jnp.exp(jax.random.uniform(keys[0], (NLEAVES, 1), jnp.float32, math.log(0.8), math.log(1.25)))
    within = 1.2247 * jax.random.truncated_normal(keys[1], -4.0, 4.0, (NPTS, latent_dims), jnp.float32)
    jitter = 0.5 * jax.random.truncated_normal(keys[2], -4.0, 4.0, (NPTS, DIM), jnp.float32)
    latent = jnp.repeat(centre, LEAF, axis=0) + within * jnp.repeat(spread, LEAF, axis=0)
    return (embed(latent) + jitter).astype(jnp.bfloat16)


def draw_right_side(key, part):
    key = jax.random.fold_in(key, 11)
    keys = jax.random.split(key, 3)
    spread = jnp.exp(jax.random.uniform(keys[0], (NLEAVES,), jnp.float32, math.log(0.3), math.log(3.0)))
    ramp = jnp.exp(math.log(3.0) * (jnp.arange(NPTS, dtype=jnp.float32) / NPTS - 0.5))
    offsets = jax.random.uniform(keys[1], (RHS, NLEAVES), jnp.float32, -1.0, 1.0)
    noise = jax.random.truncated_normal(keys[2], -4.0, 4.0, (RHS, NPTS), jnp.float32)
    shifted = noise + jnp.repeat(offsets, LEAF, axis=1)
    return shifted * jnp.repeat(spread, LEAF)[None, :] * ramp[None, :]


def draw_skel_sub(key, part):
    coarse, fine, leaves = tree_centres(key)
    key = jax.random.fold_in(key, 23)
    keys = jax.random.split(key, 3)
    centre = jnp.repeat(coarse, SUBNODES // GROUPS, axis=0) + fine
    rows = SUBNODES * SKEL
    spread = jnp.exp(jax.random.uniform(keys[0], (rows, 1), jnp.float32, math.log(0.7), math.log(1.4)))
    within = jax.random.truncated_normal(keys[1], -4.0, 4.0, (rows, latent_dims), jnp.float32)
    jitter = 0.5 * jax.random.truncated_normal(keys[2], -4.0, 4.0, (rows, DIM), jnp.float32)
    latent = jnp.repeat(centre, SKEL, axis=0) + within * spread
    return (embed(latent) + jitter).astype(jnp.bfloat16)


def draw_skel_group(key, part):
    coarse, fine, leaves = tree_centres(key)
    key = jax.random.fold_in(key, 29)
    keys = jax.random.split(key, 3)
    rows = GROUPS * SKEL
    spread = jnp.exp(jax.random.uniform(keys[0], (rows, 1), jnp.float32, math.log(0.7), math.log(1.4)))
    within = jax.random.truncated_normal(keys[1], -4.0, 4.0, (rows, latent_dims), jnp.float32)
    jitter = 0.5 * jax.random.truncated_normal(keys[2], -4.0, 4.0, (rows, DIM), jnp.float32)
    latent = jnp.repeat(coarse, SKEL, axis=0) + within * spread
    return (embed(latent) + jitter).astype(jnp.bfloat16)


def draw_skel_top(key, part):
    key = jax.random.fold_in(key, 31)
    keys = jax.random.split(key, 3)
    spread = jnp.exp(jax.random.uniform(keys[0], (SKEL, 1), jnp.float32, math.log(0.7), math.log(1.4)))
    within = 1.2247 * jax.random.truncated_normal(keys[1], -4.0, 4.0, (SKEL, latent_dims), jnp.float32)
    jitter = 0.5 * jax.random.truncated_normal(keys[2], -4.0, 4.0, (SKEL, DIM), jnp.float32)
    return (embed(within * spread) + jitter).astype(jnp.bfloat16)


def setup_inputs(seed: int = 0) -> dict:
    key_list = jax.random.split(jax.random.key(seed), 8)
    return {
        "points": draw_points(jax.random.fold_in(key_list[7], 71), 0),
        "right_side": draw_right_side(jax.random.fold_in(key_list[7], 71), 0),
        "skel_sub": draw_skel_sub(jax.random.fold_in(key_list[7], 71), 0),
        "skel_group": draw_skel_group(jax.random.fold_in(key_list[7], 71), 0),
        "skel_top": draw_skel_top(jax.random.fold_in(key_list[7], 71), 0),
        "neighbors": draw_neighbors(jax.random.fold_in(key_list[7], 71), 0),
        "counts": draw_counts(jax.random.fold_in(key_list[7], 71), 0),
    }


ridge_term = 3.0
level_one = 0.5
level_two = 0.25
level_top = 0.3
highest = lax.Precision.HIGHEST


def gauss_block(left_rows, right_rows):
    cross = lax.dot_general(left_rows, right_rows, (((1,), (1,)), ((), ())), precision=highest, preferred_element_type=jnp.float32)
    left_sq = jnp.sum(left_rows * left_rows, axis=1)
    right_sq = jnp.sum(right_rows * right_rows, axis=1)
    return jnp.exp((2.0 * cross - left_sq[:, None] - right_sq[None, :]) * (0.25 / left_rows.shape[1]))


def dot_plain(values, table):
    return jnp.dot(values, table, precision=highest, preferred_element_type=jnp.float32)


def dot_last(values, table):
    return lax.dot_general(values, table, (((1,), (1,)), ((), ())), precision=highest, preferred_element_type=jnp.float32)


def apply_near(coords, rounded, neighbors, counts):
    def one_leaf(leaf_index):
        start = (leaf_index * LEAF).astype(jnp.int32)
        own_points = lax.dynamic_slice_in_dim(coords, start, LEAF, 0)
        own_dirs = lax.dynamic_slice_in_dim(rounded, start, LEAF, 1)
        self_table = gauss_block(own_points, own_points).astype(jnp.bfloat16)
        running = jnp.dot(own_dirs, self_table, preferred_element_type=jnp.float32)
        for column in range(NB):
            other_start = (neighbors[leaf_index, column] * LEAF).astype(jnp.int32)
            other_points = lax.dynamic_slice_in_dim(coords, other_start, LEAF, 0)
            other_dirs = lax.dynamic_slice_in_dim(rounded, other_start, LEAF, 1)
            weight = (column < counts[leaf_index]).astype(jnp.float32)
            table = (gauss_block(other_points, own_points) * weight).astype(jnp.bfloat16)
            running = running + jnp.dot(other_dirs, table, preferred_element_type=jnp.float32)
        return running * (1.0 / LEAF)

    stacked = lax.map(one_leaf, jnp.arange(NLEAVES, dtype=jnp.int32))
    return jnp.transpose(stacked, (1, 0, 2)).reshape(rounded.shape[0], rounded.shape[1])


def apply_far(coords, field, skel_sub, skel_group, skel_top):
    sub_points = coords.reshape(SUBNODES, SUBPTS, DIM)
    sub_skel = skel_sub.reshape(SUBNODES, SKEL, DIM)
    group_skel = skel_group.reshape(GROUPS, SKEL, DIM)
    sub_field = jnp.transpose(field.reshape(field.shape[0], SUBNODES, SUBPTS), (1, 0, 2))

    def upward(index):
        return dot_plain(sub_field[index], gauss_block(sub_points[index], sub_skel[index])) * (1.0 / LEAF)

    up_one = lax.map(upward, jnp.arange(SUBNODES, dtype=jnp.int32))
    owner = jnp.arange(SUBNODES, dtype=jnp.int32) // N_SUB
    low_tables = jax.vmap(gauss_block)(sub_skel, group_skel[owner])
    high_tables = jax.vmap(lambda group_rows: gauss_block(group_rows, skel_top))(group_skel)
    terms_two = jnp.einsum("src,scd->srd", up_one, low_tables, precision=highest) * (1.0 / SKEL)
    up_two = jnp.sum(terms_two.reshape(GROUPS, N_SUB, field.shape[0], SKEL), axis=1)
    up_top = jnp.einsum("grc,gcd->rd", up_two, high_tables, precision=highest) * (1.0 / SKEL)
    down_top = level_top * up_top
    down_two = level_two * up_two + jnp.einsum("rd,gcd->grc", down_top, high_tables, precision=highest) * (1.0 / SKEL)
    down_one = level_one * up_one + jnp.einsum("srd,scd->src", down_two[owner], low_tables, precision=highest) * (1.0 / SKEL)

    def downward(index):
        return dot_last(down_one[index], gauss_block(sub_points[index], sub_skel[index])) * (1.0 / LEAF)

    pieces = lax.map(downward, jnp.arange(SUBNODES, dtype=jnp.int32))
    return jnp.transpose(pieces, (1, 0, 2)).reshape(field.shape[0], field.shape[1])


def reference(points, right_side, skel_sub, skel_group, skel_top, neighbors, counts):
    coords = points.astype(jnp.float32)
    sub_coords = skel_sub.astype(jnp.float32)
    group_coords = skel_group.astype(jnp.float32)
    top_coords = skel_top.astype(jnp.float32)

    def operate(field):
        near_part = apply_near(coords, field.astype(jnp.bfloat16), neighbors, counts)
        far_part = apply_far(coords, field, sub_coords, group_coords, top_coords)
        return ridge_term * field + near_part + far_part

    solution = jnp.zeros_like(right_side)
    residual = right_side
    direction = right_side
    norm_now = jnp.sum(residual * residual, axis=1)
    for iteration in range(ITERS):
        applied = operate(direction)
        step_size = norm_now / jnp.sum(direction * applied, axis=1)
        solution = solution + step_size[:, None] * direction
        residual = residual - step_size[:, None] * applied
        if iteration + 1 < ITERS:
            norm_next = jnp.sum(residual * residual, axis=1)
            direction = residual + (norm_next / norm_now)[:, None] * direction
            norm_now = norm_next
    return solution, residual
```

```python
import jax
import jax.numpy as jnp
from jax import lax
from jax.sharding import PartitionSpec as P

LEAF = 1024
SKEL = 256
ALL = ("group", "sub", "leaf")

ridge_term = 3.0
level_one = 0.5
level_two = 0.25
level_top = 0.3

bf16 = jnp.bfloat16
f32 = jnp.float32


def gauss_block(left_rows, right_rows):
    cross = lax.dot_general(
        left_rows, right_rows, (((1,), (1,)), ((), ())), preferred_element_type=f32
    )
    left_sq = jnp.sum(jnp.square(left_rows.astype(f32)), axis=1)
    right_sq = jnp.sum(jnp.square(right_rows.astype(f32)), axis=1)
    return jnp.exp(
        (2.0 * cross - left_sq[:, None] - right_sq[None, :]) * (0.25 / left_rows.shape[1])
    )


def dot_plain(values, table):
    return jnp.dot(values, table, precision=lax.Precision.HIGHEST, preferred_element_type=f32)


def dot_last(values, table):
    return lax.dot_general(
        values,
        table,
        (((1,), (1,)), ((), ())),
        precision=lax.Precision.HIGHEST,
        preferred_element_type=f32,
    )


def dot_near(values, table):
    return jnp.dot(values, table, preferred_element_type=f32)


def dot_near_last(values, table):
    return lax.dot_general(
        values, table, (((1,), (1,)), ((), ())), preferred_element_type=f32
    )


def axis_sum(value, axis):
    count = lax.axis_size(axis)
    sent = jnp.broadcast_to(value[None], (count,) + value.shape)
    got = lax.all_to_all(sent, axis, 0, 0)
    return jnp.sum(got.astype(f32), axis=0)


def pieces_of(value):
    high = lax.reduce_precision(value, 8, 7)
    rest = value - high
    middle = lax.reduce_precision(rest, 8, 7)
    low = rest - middle
    return jnp.concatenate([high, middle, low], axis=1)


def with_scalars(weights, scalars):
    rows = jnp.pad(pieces_of(scalars), ((0, 4), (0, 64)))
    return jnp.concatenate([weights, rows], axis=0).astype(bf16)


def without_scalars(total):
    rows = total[64:68]
    return total[:64], rows[:, :64] + (rows[:, 64:128] + rows[:, 128:192])


def shift_up(value):
    count = lax.axis_size(ALL)
    return lax.ppermute(value, ALL, [(i, i + 1) for i in range(count - 1)])


def shift_down(value):
    count = lax.axis_size(ALL)
    return lax.ppermute(value, ALL, [(i + 1, i) for i in range(count - 1)])


def shards(points, right_side, skel_sub, skel_group, skel_top, neighbors, counts):
    first_leaf = lax.axis_index(ALL) * 2
    live = jnp.arange(2)[None, :] < counts[:, None]

    def listed(position, target):
        return jnp.sum((live[position] & (neighbors[position] == target)).astype(f32))

    with_before = listed(0, first_leaf - 1)
    with_inner = listed(0, first_leaf + 1)
    with_inner_back = listed(1, first_leaf)

    points_a, points_b = points[:LEAF], points[LEAF:]
    points_before = shift_up(points_b)
    table_a = gauss_block(points_a, points_a).astype(bf16)
    table_b = gauss_block(points_b, points_b).astype(bf16)
    table_ab = gauss_block(points_a, points_b).astype(bf16)
    table_before = gauss_block(points_before, points_a).astype(bf16)

    point_table = gauss_block(points, skel_sub)
    low_table = gauss_block(skel_sub, skel_group)
    high_table = gauss_block(skel_group, skel_top)

    def near(rounded):
        field_a, field_b = rounded[:, :LEAF], rounded[:, LEAF:]
        field_before = shift_up(field_b)
        from_before = with_before * dot_near(field_before, table_before)
        back = with_before * dot_near_last(field_a, table_before)
        own_a = dot_near(field_a, table_a) + with_inner * dot_near_last(field_b, table_ab)
        own_b = dot_near(field_b, table_b) + with_inner_back * dot_near(field_a, table_ab)
        after = shift_down(back)
        own = jnp.concatenate([own_a, own_b], axis=1) * (1.0 / LEAF)
        cross_a = from_before * (1.0 / LEAF)
        return own, cross_a, after * (1.0 / LEAF)

    def down(up_one, up_two, up_top):
        down_top = level_top * up_top
        down_two = level_two * up_two + dot_last(down_top, high_table) * (1.0 / SKEL)
        down_one = level_one * up_one + dot_last(down_two, low_table) * (1.0 / SKEL)
        return dot_last(down_one, point_table) * (1.0 / LEAF)

    first = right_side
    terms = dot_plain(first, point_table) * (1.0 / LEAF)
    up_one = axis_sum(terms.astype(bf16), "leaf")
    up_two = axis_sum((dot_plain(up_one, low_table) * (1.0 / SKEL)).astype(bf16), "sub")
    up_top = axis_sum((dot_plain(up_two, high_table) * (1.0 / SKEL)).astype(bf16), "group")
    own, cross_a, after = near(first.astype(bf16))
    far = down(up_one, up_two, up_top)
    second_a = own[:, :LEAF] + cross_a + far[:, :LEAF]
    second_b = own[:, LEAF:] + after + far[:, LEAF:]
    second = jnp.concatenate([second_a, second_b], axis=1)

    terms = dot_plain(second, point_table) * (1.0 / LEAF)
    own, cross_a, after = near(second.astype(bf16))
    scalars = jnp.stack(
        [
            jnp.sum(first * first, axis=1),
            jnp.sum(first * second, axis=1),
            jnp.sum(second * second, axis=1),
            jnp.sum(second * own, axis=1) + 2.0 * jnp.sum(second_a * cross_a, axis=1),
        ]
    )
    up_one, scalars = without_scalars(axis_sum(with_scalars(terms, scalars), "leaf"))
    scalars = scalars.at[3].add(level_one * jnp.sum(up_one * up_one, axis=1))
    terms = dot_plain(up_one, low_table) * (1.0 / SKEL)
    up_two, scalars = without_scalars(axis_sum(with_scalars(terms, scalars), "sub"))
    scalars = scalars.at[3].add(level_two * jnp.sum(up_two * up_two, axis=1))
    terms = dot_plain(up_two, high_table) * (1.0 / SKEL)
    up_top, scalars = without_scalars(axis_sum(with_scalars(terms, scalars), "group"))
    scalars = scalars.at[3].add(level_top * jnp.sum(up_top * up_top, axis=1))
    far = down(up_one, up_two, up_top)
    third_a = own[:, :LEAF] + cross_a + far[:, :LEAF]
    third_b = own[:, LEAF:] + after + far[:, LEAF:]
    third = jnp.concatenate([third_a, third_b], axis=1)

    bb, bu, uu, uv = scalars[0], scalars[1], scalars[2], scalars[3]
    step_one = bb / (ridge_term * bb + bu)
    ratio = bu / bb
    norm_one = step_one * step_one * (uu - ratio * bu)
    beta = norm_one / bb
    bend_rr = step_one * step_one * (ratio * ratio * bu - 2.0 * ratio * uu + uv)
    bend_rb = step_one * (ratio * bu - uu)
    bending = (
        ridge_term * (norm_one + beta * beta * bb)
        + bend_rr
        + 2.0 * beta * bend_rb
        + beta * beta * bu
    )
    step_two = norm_one / bending

    def column(value):
        return value[:, None]

    residual_one = column(step_one * ratio) * first - column(step_one) * second
    direction = residual_one + column(beta) * first
    applied = (
        ridge_term * direction
        + column(step_one * ratio + beta) * second
        - column(step_one) * third
    )
    solution = column(step_one) * first + column(step_two) * direction
    residual = residual_one - column(step_two) * applied
    return (solution, residual)


def solution(mesh):
    return jax.shard_map(
        shards,
        mesh=mesh,
        in_specs=(
            P(ALL, None),
            P(None, ALL),
            P(("group", "sub"), None),
            P("group", None),
            P(),
            P(ALL, None),
            P(ALL),
        ),
        out_specs=(P(None, ALL), P(None, ALL)),
        check_vma=False,
    )
```

```python
import math

import jax
import jax.numpy as jnp
from jax import lax
from jax.experimental import pallas as pl
from jax.experimental.pallas import tpu as pltpu
from jax.sharding import PartitionSpec as P

LEAF = 1024
SKEL = 256
RHS = 64
DIM = 256
ROWS = 256
STEPS = LEAF // ROWS
WIDE = 512
ALL = ("group", "sub", "leaf")

ridge_term = 3.0
level_one = 0.5
level_two = 0.25
level_top = 0.3

bf16 = jnp.bfloat16
f32 = jnp.float32
per_unit = 0.25 / DIM * math.log2(math.e)
vmem_bytes = 40 * 1024 * 1024


def shape_of(shape, dtype):
    return jax.ShapeDtypeStruct(shape, dtype)


def cost(flops, moved, exps=0):
    return pl.CostEstimate(flops=flops, bytes_accessed=moved, transcendentals=exps)


params = pltpu.CompilerParams(vmem_limit_bytes=vmem_bytes)


def nn(left, right, precision=None):
    return lax.dot_general(
        left, right, (((1,), (0,)), ((), ())), precision=precision, preferred_element_type=f32
    )


def nt(left, right, precision=None):
    return lax.dot_general(
        left, right, (((1,), (1,)), ((), ())), precision=precision, preferred_element_type=f32
    )


highest = lax.Precision.HIGHEST


def squares(rows):
    wide = rows.astype(f32)
    return wide * wide


def left_column(rows):
    return jnp.sum(squares(rows), axis=1, keepdims=True) * per_unit


def right_row(rows):
    square = squares(rows)
    high = square.astype(bf16)
    low = (square - high.astype(f32)).astype(bf16)
    ones = jnp.ones((8, rows.shape[1]), bf16)
    return (nt(ones, high) + nt(ones, low))[0:1] * per_unit


def gauss(left, column, right, row):
    return jnp.exp2(nt(left, right) * (2.0 * per_unit) - column - row)


def split(value):
    high = value.astype(bf16)
    low = (value - high.astype(f32)).astype(bf16)
    return high, low


def up_dot(field, table_high, table_low):
    high, low = split(field)
    both = nn(jnp.concatenate([high, low], axis=0), table_high)
    return both[:RHS] + both[RHS:] + nn(high, table_low)


def down_dot(weights, table_high, table_low):
    high, low = split(weights)
    both = nt(jnp.concatenate([high, low], axis=0), table_high)
    return both[:RHS] + both[RHS:] + nt(high, table_low)


def start_kernel(
    x_ref, z1_ref, z2_ref, z3_ref, b_ref, sent_ref, gh_ref, gl_ref, t1_ref, t2_ref, halo_ref
):
    z1 = z1_ref[...]
    row = right_row(z1)
    total = jnp.zeros((RHS, SKEL), f32)
    for k in range(0, x_ref.shape[0], WIDE):
        part = x_ref[k : k + WIDE, :]
        table = gauss(part, left_column(part), z1, row)
        high, low = split(table)
        gh_ref[k : k + WIDE, :] = high
        gl_ref[k : k + WIDE, :] = low
        total += up_dot(b_ref[:, k : k + WIDE], high, low)
    value = (total * (1.0 / LEAF)).astype(bf16)
    for k in range(sent_ref.shape[0]):
        sent_ref[k] = value
    halo_ref[0:LEAF, :] = x_ref[LEAF:, :]
    for k in range(STEPS):
        first = LEAF + k * RHS
        halo_ref[first : first + RHS, :] = b_ref[
            :, LEAF + k * ROWS : LEAF + (k + 1) * ROWS
        ].astype(bf16)
    z2, z3 = z2_ref[...], z3_ref[...]
    t1_ref[...] = gauss(z1, left_column(z1), z2, right_row(z2))
    t2_ref[...] = gauss(z2, left_column(z2), z3, right_row(z3))


def start_call(points, z1, z2, z3, field, peers):
    count = points.shape[0]
    return pl.pallas_call(
        start_kernel,
        out_shape=(
            shape_of((peers, RHS, SKEL), bf16),
            shape_of((count, SKEL), bf16),
            shape_of((count, SKEL), bf16),
            shape_of((SKEL, SKEL), f32),
            shape_of((SKEL, SKEL), f32),
            shape_of((LEAF + STEPS * RHS, DIM), bf16),
        ),
        compiler_params=params,
        cost_estimate=cost(600_000_000, 5_000_000, 655_360),
        name="start",
    )(points, z1, z2, z3, field)


def listed(nb_ref, ct_ref, position, target):
    found = 0.0
    for k in range(nb_ref.shape[1]):
        hit = (k < ct_ref[position]) & (nb_ref[position, k] == target)
        found = found + jnp.where(hit, 1.0, 0.0)
    return found


def first_leaf_of():
    return lax.axis_index(ALL) * 2


def chunk(step):
    return pl.ds(pl.multiple_of(step * ROWS, ROWS), ROWS)


def near_own(step, b_a, b_b, b_a_part, b_b_part, t_a, t_b, t_ab, nb_ref, ct_ref, out_ref):
    first = first_leaf_of()
    inner = listed(nb_ref, ct_ref, 0, first + 1)
    inner_back = listed(nb_ref, ct_ref, 1, first)
    add_a = nn(b_a_part, t_a)
    add_b = nn(b_b_part, t_b) + inner_back * nn(b_a_part, t_ab)
    cross = inner * nt(b_b, t_ab)

    @pl.when(step == 0)
    def _():
        out_ref[:, :LEAF] = add_a
        out_ref[:, LEAF:] = add_b

    @pl.when(step > 0)
    def _():
        out_ref[:, :LEAF] += add_a
        out_ref[:, LEAF:] += add_b

    out_ref[:, chunk(step)] += cross


def tables_kernel(
    nb_ref, ct_ref, x_ref, b_ref, after_ref, tabs_ref, out_ref, row_ref
):
    del after_ref
    step = pl.program_id(0)

    @pl.when(step == 0)
    def _():
        row_ref[...] = right_row(x_ref[...])

    x_a, x_b = x_ref[:LEAF, :], x_ref[LEAF:, :]
    rows_a = x_ref[chunk(step), :]
    rows_b = x_ref[pl.ds(pl.multiple_of(LEAF + step * ROWS, ROWS), ROWS), :]
    row_a, row_b = row_ref[:, :LEAF], row_ref[:, LEAF:]
    col_a, col_b = left_column(rows_a), left_column(rows_b)
    t_a = gauss(rows_a, col_a, x_a, row_a).astype(bf16)
    t_b = gauss(rows_b, col_b, x_b, row_b).astype(bf16)
    t_ab = gauss(rows_a, col_a, x_b, row_b).astype(bf16)
    tabs_ref[0] = t_a
    tabs_ref[1] = t_b
    tabs_ref[2] = t_ab
    b_b = b_ref[:, LEAF:].astype(bf16)
    b_a_part = b_ref[:, chunk(step)].astype(bf16)
    b_b_part = b_ref[:, pl.ds(pl.multiple_of(LEAF + step * ROWS, ROWS), ROWS)].astype(bf16)
    near_own(step, None, b_b, b_a_part, b_b_part, t_a, t_b, t_ab, nb_ref, ct_ref, out_ref)


def smem():
    return pl.BlockSpec(memory_space=pltpu.SMEM)


def whole(*shape):
    return pl.BlockSpec(shape, lambda i: (0,) * len(shape))


def anywhere():
    return pl.BlockSpec(memory_space=pl.ANY)


def tables_call(neighbors, counts, points, field, after):
    return pl.pallas_call(
        tables_kernel,
        grid=(STEPS,),
        in_specs=[
            smem(),
            smem(),
            whole(2 * LEAF, DIM),
            whole(RHS, 2 * LEAF),
            anywhere(),
        ],
        out_specs=(
            pl.BlockSpec((3, ROWS, LEAF), lambda i: (0, i, 0)),
            whole(RHS, 2 * LEAF),
        ),
        out_shape=(
            shape_of((3, LEAF, LEAF), bf16),
            shape_of((RHS, 2 * LEAF), f32),
        ),
        scratch_shapes=[pltpu.VMEM((1, 2 * LEAF), f32)],
        compiler_params=params,
        cost_estimate=cost(2_200_000_000, 8_000_000, 3_145_728),
        name="tables",
    )(neighbors, counts, points, field, after)


def before_kernel(nb_ref, ct_ref, hx_ref, hb_ref, x_ref, b_ref, after_ref, tab_ref, out_ref, back_ref, row_ref):
    del after_ref
    step = pl.program_id(0)
    x_a = x_ref[...]

    @pl.when(step == 0)
    def _():
        row_ref[...] = right_row(x_a)

    rows = hx_ref[...]
    table = gauss(rows, left_column(rows), x_a, row_ref[...]).astype(bf16)
    tab_ref[...] = table
    weight = listed(nb_ref, ct_ref, 0, first_leaf_of() - 1)
    add = weight * nn(hb_ref[...], table)

    @pl.when(step == 0)
    def _():
        out_ref[...] = add

    @pl.when(step > 0)
    def _():
        out_ref[...] += add

    back_ref[...] = weight * nt(b_ref[...].astype(bf16), table)


def before_call(neighbors, counts, halo, points, field, after):
    return pl.pallas_call(
        before_kernel,
        grid=(STEPS,),
        in_specs=[
            smem(),
            smem(),
            pl.BlockSpec((ROWS, DIM), lambda i: (i, 0)),
            pl.BlockSpec((RHS, DIM), lambda i: (LEAF // RHS + i, 0)),
            whole(LEAF, DIM),
            whole(RHS, LEAF),
            anywhere(),
        ],
        out_specs=(
            pl.BlockSpec((ROWS, LEAF), lambda i: (i, 0)),
            whole(RHS, LEAF),
            pl.BlockSpec((RHS, ROWS), lambda i: (0, i)),
        ),
        out_shape=(
            shape_of((LEAF, LEAF), bf16),
            shape_of((RHS, LEAF), f32),
            shape_of((RHS, LEAF), f32),
        ),
        scratch_shapes=[pltpu.VMEM((1, LEAF), f32)],
        compiler_params=params,
        cost_estimate=cost(800_000_000, 4_000_000, 1_048_576),
        name="before",
    )(neighbors, counts, halo, halo, points, field, after)


def total_of(got_ref):
    total = got_ref[0].astype(f32)
    for k in range(1, got_ref.shape[0]):
        total += got_ref[k].astype(f32)
    return total


def climb_kernel(got_ref, table_ref, up_ref, sent_ref):
    total = total_of(got_ref)
    up_ref[...] = total
    value = (nn(total, table_ref[...], highest) * (1.0 / SKEL)).astype(bf16)
    for k in range(sent_ref.shape[0]):
        sent_ref[k] = value


def climb_call(got, table, peers):
    return pl.pallas_call(
        climb_kernel,
        out_shape=(shape_of((RHS, SKEL), f32), shape_of((peers, RHS, SKEL), bf16)),
        compiler_params=params,
        cost_estimate=cost(50_000_000, 900_000),
        name="climb",
    )(got, table)


def down_weights(up_one, up_two, up_top, low_table, high_table):
    down_top = level_top * up_top
    down_two = level_two * up_two + nt(down_top, high_table, highest) * (1.0 / SKEL)
    return level_one * up_one + nt(down_two, low_table, highest) * (1.0 / SKEL)


def second_kernel(
    got_ref, p1_ref, p2_ref, t1_ref, t2_ref, gh_ref, gl_ref, own_ref, cross_ref, after_ref,
    u_ref, edge_ref, d1_ref
):
    step = pl.program_id(0)

    @pl.when(step == 0)
    def _():
        d1_ref[...] = down_weights(
            p1_ref[...], p2_ref[...], total_of(got_ref), t1_ref[...], t2_ref[...]
        )

    far = down_dot(d1_ref[...], gh_ref[...], gl_ref[...])
    side = jnp.where(step < 2, cross_ref[...], after_ref[...])
    value = (own_ref[...] + side + far) * (1.0 / LEAF)
    u_ref[...] = value
    edge_ref[...] = value.astype(bf16)


def tail_block(i):
    return (0, jnp.maximum(i - 2, 0))


def head_block(i):
    return (0, jnp.minimum(i, 1))


def second_call(got, p1, p2, t1, t2, gh, gl, own, cross, after):
    small = whole(RHS, SKEL)
    square = whole(SKEL, SKEL)
    return pl.pallas_call(
        second_kernel,
        grid=(4,),
        in_specs=[
            whole(*got.shape),
            small,
            small,
            square,
            square,
            pl.BlockSpec((WIDE, SKEL), lambda i: (i, 0)),
            pl.BlockSpec((WIDE, SKEL), lambda i: (i, 0)),
            pl.BlockSpec((RHS, WIDE), lambda i: (0, i)),
            pl.BlockSpec((RHS, WIDE), head_block),
            pl.BlockSpec((RHS, WIDE), tail_block),
        ],
        out_specs=(
            pl.BlockSpec((RHS, WIDE), lambda i: (0, i)),
            pl.BlockSpec((RHS, WIDE), tail_block),
        ),
        out_shape=(shape_of((RHS, 2 * LEAF), f32), shape_of((RHS, LEAF), bf16)),
        scratch_shapes=[pltpu.VMEM((RHS, SKEL), f32)],
        compiler_params=params,
        cost_estimate=cost(250_000_000, 5_000_000),
        name="second",
    )(got, p1, p2, t1, t2, gh, gl, own, cross, after)


def row_sum(value):
    return jnp.sum(value, axis=1, keepdims=True)


def third_kernel(
    nb_ref, ct_ref, u_ref, b_ref, tabs_ref, gha_ref, gla_ref, ghb_ref, glb_ref,
    out_ref, up_ref, sums_ref
):
    step = pl.program_id(0)
    part_a = chunk(step)
    part_b = pl.ds(pl.multiple_of(LEAF + step * ROWS, ROWS), ROWS)
    u_a, u_b = u_ref[:, part_a], u_ref[:, part_b]
    up = up_dot(u_a, gha_ref[...], gla_ref[...]) + up_dot(u_b, ghb_ref[...], glb_ref[...])

    @pl.when(step == 0)
    def _():
        up_ref[...] = up

    @pl.when(step > 0)
    def _():
        up_ref[...] += up

    near_own(
        step, None, u_ref[:, LEAF:].astype(bf16), u_a.astype(bf16), u_b.astype(bf16),
        tabs_ref[0], tabs_ref[1], tabs_ref[2], nb_ref, ct_ref, out_ref,
    )

    @pl.when(step == STEPS - 1)
    def _():
        b, u = b_ref[...], u_ref[...]
        lane = lax.broadcasted_iota(jnp.int32, (RHS, 128), 1)
        sums = (row_sum(b * b), row_sum(b * u), row_sum(u * u), row_sum(u * out_ref[...]))
        total = jnp.zeros((RHS, 128), f32)
        for k in range(4):
            total = jnp.where(lane == k, sums[k], total)
        sums_ref[...] = total


def third_call(neighbors, counts, u, field, tabs, gh, gl):
    near_rows = pl.BlockSpec((ROWS, SKEL), lambda i: (i, 0))
    far_rows = pl.BlockSpec((ROWS, SKEL), lambda i: (STEPS + i, 0))
    return pl.pallas_call(
        third_kernel,
        grid=(STEPS,),
        in_specs=[
            smem(),
            smem(),
            whole(RHS, 2 * LEAF),
            whole(RHS, 2 * LEAF),
            pl.BlockSpec((3, ROWS, LEAF), lambda i: (0, i, 0)),
            near_rows,
            near_rows,
            far_rows,
            far_rows,
        ],
        out_specs=(whole(RHS, 2 * LEAF), whole(RHS, SKEL), whole(RHS, 128)),
        out_shape=(
            shape_of((RHS, 2 * LEAF), f32),
            shape_of((RHS, SKEL), f32),
            shape_of((RHS, 128), f32),
        ),
        compiler_params=params,
        cost_estimate=cost(700_000_000, 10_000_000),
        name="third",
    )(neighbors, counts, u, field, tabs, gh, gl, gh, gl)


def rows_of(sums):
    high = sums.astype(bf16).astype(f32)
    rest = sums - high
    middle = rest.astype(bf16).astype(f32)
    low = rest - middle
    lane = lax.broadcasted_iota(jnp.int32, (RHS, 128), 1)
    packed = jnp.where(lane < 4, high, 0.0)
    packed += jnp.where((lane >= 4) & (lane < 8), pltpu.roll(middle, 4, 1), 0.0)
    packed += jnp.where((lane >= 8) & (lane < 12), pltpu.roll(low, 8, 1), 0.0)
    turned = packed.T[:16]
    return jnp.concatenate([turned, jnp.zeros((16, SKEL - RHS), f32)], axis=1)


def sums_of(rows):
    turned = jnp.concatenate([rows[:, :RHS], jnp.zeros((112, RHS), f32)], axis=0).T
    total = turned + (pltpu.roll(turned, 124, 1) + pltpu.roll(turned, 120, 1))
    lane = lax.broadcasted_iota(jnp.int32, (RHS, 128), 1)
    return jnp.where(lane < 4, total, 0.0)


def put_all(sent_ref, value, sums):
    message = jnp.concatenate([value, rows_of(sums)], axis=0).astype(bf16)
    for k in range(sent_ref.shape[0]):
        sent_ref[k] = message


def add_last(sums, column):
    lane = lax.broadcasted_iota(jnp.int32, (RHS, 128), 1)
    return sums + jnp.where(lane == 3, column, 0.0)


def finish_kernel(
    nb_ref, ct_ref, edge_ref, tab_ref, u_ref, up_ref, sums_ref, sent_ref, out_ref, back_ref
):
    weight = listed(nb_ref, ct_ref, 0, first_leaf_of() - 1)
    u_a = u_ref[...]
    table = tab_ref[...]
    cross = weight * nn(edge_ref[...], table)
    out_ref[...] = cross
    back_ref[...] = weight * nt(u_a.astype(bf16), table)
    sums = add_last(sums_ref[...], 2.0 * row_sum(u_a * cross))
    lane = lax.broadcasted_iota(jnp.int32, (RHS, 128), 1)
    sums = jnp.where(lane == 3, sums * (1.0 / LEAF), sums)
    put_all(sent_ref, up_ref[...] * (1.0 / LEAF), sums)


def finish_call(neighbors, counts, edge, tab, u, up, sums, peers):
    return pl.pallas_call(
        finish_kernel,
        grid=(1,),
        in_specs=[
            smem(),
            smem(),
            whole(RHS, LEAF),
            whole(LEAF, LEAF),
            whole(RHS, LEAF),
            whole(RHS, SKEL),
            whole(RHS, 128),
        ],
        out_specs=(whole(peers, RHS + 16, SKEL), whole(RHS, LEAF), whole(RHS, LEAF)),
        out_shape=(
            shape_of((peers, RHS + 16, SKEL), bf16),
            shape_of((RHS, LEAF), f32),
            shape_of((RHS, LEAF), f32),
        ),
        compiler_params=params,
        cost_estimate=cost(270_000_000, 4_000_000),
        name="finish",
    )(neighbors, counts, edge, tab, u, up, sums)


def climb_sums_kernel(level, got_ref, table_ref, up_ref, sent_ref):
    total = total_of(got_ref)
    up = total[:RHS]
    up_ref[...] = up
    sums = add_last(sums_of(total[RHS:]), level * row_sum(up * up))
    put_all(sent_ref, nn(up, table_ref[...], highest) * (1.0 / SKEL), sums)


def climb_sums_call(got, table, level, peers):
    return pl.pallas_call(
        lambda *refs: climb_sums_kernel(level, *refs),
        out_shape=(shape_of((RHS, SKEL), f32), shape_of((peers, RHS + 16, SKEL), bf16)),
        compiler_params=params,
        cost_estimate=cost(50_000_000, 900_000),
        name="climb_sums",
    )(got, table)


def last_kernel(
    got_ref, p1_ref, p2_ref, t1_ref, t2_ref, gh_ref, gl_ref, own_ref, cross_ref, after_ref,
    b_ref, u_ref, x_ref, r_ref, d1_ref, coef_ref
):
    step = pl.program_id(0)

    @pl.when(step == 0)
    def _():
        total = total_of(got_ref)
        top = total[:RHS]
        d1_ref[...] = down_weights(p1_ref[...], p2_ref[...], top, t1_ref[...], t2_ref[...])
        sums = add_last(sums_of(total[RHS:]), level_top * row_sum(top * top))
        bb, bu, uu, uv = sums[:, 0:1], sums[:, 1:2], sums[:, 2:3], sums[:, 3:4]
        step_one = bb / (ridge_term * bb + bu)
        ratio = bu / bb
        norm_one = step_one * step_one * (uu - ratio * bu)
        beta = norm_one / bb
        bend_rr = step_one * step_one * (ratio * ratio * bu - 2.0 * ratio * uu + uv)
        bend_rb = step_one * (ratio * bu - uu)
        bending = (
            ridge_term * (norm_one + beta * beta * bb)
            + bend_rr
            + 2.0 * beta * bend_rb
            + beta * beta * bu
        )
        step_two = norm_one / bending
        lane = lax.broadcasted_iota(jnp.int32, (RHS, 128), 1)
        coefs = jnp.where(lane == 0, step_one, jnp.where(lane == 1, ratio, 0.0))
        coef_ref[...] = jnp.where(lane == 2, beta, jnp.where(lane == 3, step_two, coefs))

    coefs = coef_ref[...]
    step_one, ratio, beta, step_two = (coefs[:, k : k + 1] for k in range(4))
    far = down_dot(d1_ref[...], gh_ref[...], gl_ref[...])
    side = jnp.where(step < 2, cross_ref[...], after_ref[...])
    third = (own_ref[...] + side + far) * (1.0 / LEAF)
    first, second = b_ref[...], u_ref[...]
    residual_one = (step_one * ratio) * first - step_one * second
    direction = residual_one + beta * first
    applied = (
        ridge_term * direction + (step_one * ratio + beta) * second - step_one * third
    )
    x_ref[...] = step_one * first + step_two * direction
    r_ref[...] = residual_one - step_two * applied


def last_call(got, p1, p2, t1, t2, gh, gl, own, cross, after, field, u):
    small = whole(RHS, SKEL)
    square = whole(SKEL, SKEL)
    wide = pl.BlockSpec((RHS, WIDE), lambda i: (0, i))
    return pl.pallas_call(
        last_kernel,
        grid=(4,),
        in_specs=[
            whole(*got.shape),
            small,
            small,
            square,
            square,
            pl.BlockSpec((WIDE, SKEL), lambda i: (i, 0)),
            pl.BlockSpec((WIDE, SKEL), lambda i: (i, 0)),
            wide,
            pl.BlockSpec((RHS, WIDE), head_block),
            pl.BlockSpec((RHS, WIDE), tail_block),
            wide,
            wide,
        ],
        out_specs=(wide, wide),
        out_shape=(shape_of((RHS, 2 * LEAF), f32), shape_of((RHS, 2 * LEAF), f32)),
        scratch_shapes=[pltpu.VMEM((RHS, SKEL), f32), pltpu.VMEM((RHS, 128), f32)],
        compiler_params=params,
        cost_estimate=cost(250_000_000, 7_000_000),
        name="last",
    )(got, p1, p2, t1, t2, gh, gl, own, cross, after, field, u)


def exchange(sent, axis):
    return lax.all_to_all(sent, axis, 0, 0)


def shift_up(value):
    count = lax.axis_size(ALL)
    return lax.ppermute(value, ALL, [(i, i + 1) for i in range(count - 1)])


def shift_down(value):
    count = lax.axis_size(ALL)
    return lax.ppermute(value, ALL, [(i + 1, i) for i in range(count - 1)])


def shards(points, right_side, skel_sub, skel_group, skel_top, neighbors, counts):
    leaves, subs, groups = (lax.axis_size(axis) for axis in ("leaf", "sub", "group"))
    sent, gh, gl, t1, t2, halo = start_call(
        points, skel_sub, skel_group, skel_top, right_side, leaves
    )
    got = exchange(sent, "leaf")
    halo = shift_up(halo)
    tabs, own = tables_call(neighbors, counts, points, right_side, sent)
    up_one, sent = climb_call(got, t1, subs)
    got = exchange(sent, "sub")
    tab, cross, back = before_call(neighbors, counts, halo, points, right_side, sent)
    after = shift_down(back)
    up_two, sent = climb_call(got, t2, groups)
    got = exchange(sent, "group")
    second, edge = second_call(got, up_one, up_two, t1, t2, gh, gl, own, cross, after)

    edge = shift_up(edge)
    own, up, sums = third_call(neighbors, counts, second, right_side, tabs, gh, gl)
    sent, cross, back = finish_call(neighbors, counts, edge, tab, second, up, sums, leaves)
    got = exchange(sent, "leaf")
    after = shift_down(back)
    up_one, sent = climb_sums_call(got, t1, level_one, subs)
    got = exchange(sent, "sub")
    up_two, sent = climb_sums_call(got, t2, level_two, groups)
    got = exchange(sent, "group")
    return last_call(
        got, up_one, up_two, t1, t2, gh, gl, own, cross, after, right_side, second
    )


def solution(mesh):
    return jax.shard_map(
        shards,
        mesh=mesh,
        in_specs=(
            P(ALL, None),
            P(None, ALL),
            P(("group", "sub"), None),
            P("group", None),
            P(),
            P(ALL, None),
            P(ALL),
        ),
        out_specs=(P(None, ALL), P(None, ALL)),
        check_vma=False,
    )
```

```python
import math

import jax
import jax.numpy as jnp
from jax import lax
from jax.experimental import pallas as pl
from jax.experimental.pallas import tpu as pltpu
from jax.sharding import PartitionSpec as P

LEAF = 1024
SKEL = 256
RHS = 64
DIM = 256
ROWS = 256
STEPS = LEAF // ROWS
WIDE = 512
ALL = ("group", "sub", "leaf")

ridge_term = 3.0
level_one = 0.5
level_two = 0.25
level_top = 0.3

bf16 = jnp.bfloat16
f32 = jnp.float32
per_unit = 0.25 / DIM * math.log2(math.e)
vmem_bytes = 20 * 1024 * 1024


def shape_of(shape, dtype):
    return jax.ShapeDtypeStruct(shape, dtype)


def cost(flops, moved, exps=0):
    return pl.CostEstimate(flops=flops, bytes_accessed=moved, transcendentals=exps)


params = pltpu.CompilerParams(vmem_limit_bytes=vmem_bytes)


def nn(left, right, precision=None):
    return lax.dot_general(
        left, right, (((1,), (0,)), ((), ())), precision=precision, preferred_element_type=f32
    )


def nt(left, right, precision=None):
    return lax.dot_general(
        left, right, (((1,), (1,)), ((), ())), precision=precision, preferred_element_type=f32
    )


highest = lax.Precision.HIGHEST


def squares(rows):
    wide = rows.astype(f32)
    return wide * wide


def left_column(rows):
    return jnp.sum(squares(rows), axis=1, keepdims=True) * per_unit


def right_row(rows):
    square = squares(rows)
    high = square.astype(bf16)
    low = (square - high.astype(f32)).astype(bf16)
    ones = jnp.ones((8, rows.shape[1]), bf16)
    return (nt(ones, high) + nt(ones, low))[0:1] * per_unit


def gauss(left, column, right, row):
    return jnp.exp2(nt(left, right) * (2.0 * per_unit) - column - row)


def split(value):
    high = value.astype(bf16)
    low = (value - high.astype(f32)).astype(bf16)
    return high, low


def up_dot(field, table_high, table_low):
    high, low = split(field)
    both = nn(jnp.concatenate([high, low], axis=0), table_high)
    return both[:RHS] + both[RHS:] + nn(high, table_low)


def down_dot(weights, table_high, table_low):
    high, low = split(weights)
    both = nt(jnp.concatenate([high, low], axis=0), table_high)
    return both[:RHS] + both[RHS:] + nt(high, table_low)


def start_kernel(
    nb_ref, ct_ref, x_ref, z1_ref, z2_ref, z3_ref, b_ref,
    sent_ref, gh_ref, gl_ref, t1_ref, t2_ref, xv_ref, bv_ref, w_ref,
    z_ref, x_sem, b_sem, z_sem
):
    parts = x_ref.shape[0] // WIDE
    loads = []
    for k, source in enumerate((z1_ref, z2_ref, z3_ref)):
        loads.append(pltpu.make_async_copy(source, z_ref.at[k], z_sem.at[k]))
    x_loads, b_loads = [], []
    for k in range(parts):
        rows = pl.ds(k * WIDE, WIDE)
        x_loads.append(pltpu.make_async_copy(x_ref.at[rows, :], xv_ref.at[rows, :], x_sem.at[k]))
        b_loads.append(pltpu.make_async_copy(b_ref.at[:, rows], bv_ref.at[:, rows], b_sem.at[k]))
    loads[0].start()
    for k in range(parts):
        x_loads[k].start()
        b_loads[k].start()
    loads[1].start()
    loads[2].start()

    first = first_leaf_of()
    weights = (
        listed(nb_ref, ct_ref, 0, first - 1),
        listed(nb_ref, ct_ref, 0, first + 1),
        listed(nb_ref, ct_ref, 1, first),
        listed(nb_ref, ct_ref, 1, first + 2),
    )
    place = lax.broadcasted_iota(jnp.int32, (8, 128), 0)
    spread = jnp.zeros((8, 128), f32)
    for k in range(4):
        spread = jnp.where(place == k, weights[k], spread)
    w_ref[...] = spread

    loads[0].wait()
    z1 = z_ref[0]
    row = right_row(z1)
    total = jnp.zeros((RHS, SKEL), f32)
    for k in range(parts):
        rows = slice(k * WIDE, (k + 1) * WIDE)
        x_loads[k].wait()
        part = xv_ref[rows, :]
        high, low = split(gauss(part, left_column(part), z1, row))
        gh_ref[rows, :] = high
        gl_ref[rows, :] = low
        b_loads[k].wait()
        total += up_dot(bv_ref[:, rows], high, low)
    value = (total * (1.0 / LEAF)).astype(bf16)
    for k in range(sent_ref.shape[0]):
        sent_ref[k] = value
    loads[1].wait()
    loads[2].wait()
    z2, z3 = z_ref[1], z_ref[2]
    t1_ref[...] = gauss(z1, left_column(z1), z2, right_row(z2))
    t2_ref[...] = gauss(z2, left_column(z2), z3, right_row(z3))


def start_call(neighbors, counts, points, z1, z2, z3, field, peers):
    count = points.shape[0]
    parts = count // WIDE
    far_off = pl.BlockSpec(memory_space=pltpu.HBM)
    return pl.pallas_call(
        start_kernel,
        in_specs=[smem(), smem()] + [far_off] * 5,
        out_shape=(
            shape_of((peers, RHS, SKEL), bf16),
            shape_of((count, SKEL), bf16),
            shape_of((count, SKEL), bf16),
            shape_of((SKEL, SKEL), f32),
            shape_of((SKEL, SKEL), f32),
            shape_of((count, DIM), bf16),
            shape_of((RHS, count), f32),
            shape_of((8, 128), f32),
        ),
        scratch_shapes=[
            pltpu.VMEM((3, SKEL, DIM), bf16),
            pltpu.SemaphoreType.DMA((parts,)),
            pltpu.SemaphoreType.DMA((parts,)),
            pltpu.SemaphoreType.DMA((3,)),
        ],
        compiler_params=params,
        cost_estimate=cost(600_000_000, 5_000_000, 655_360),
        name="start",
    )(neighbors, counts, points, z1, z2, z3, field)


def smem():
    return pl.BlockSpec(memory_space=pltpu.SMEM)


def anywhere():
    return pl.BlockSpec(memory_space=pl.ANY)


def inside(count):
    return [pl.BlockSpec(memory_space=pltpu.VMEM)] * count


def listed(nb_ref, ct_ref, position, target):
    found = 0.0
    for k in range(nb_ref.shape[1]):
        hit = (k < ct_ref[position]) & (nb_ref[position, k] == target)
        found = found + jnp.where(hit, 1.0, 0.0)
    return found


def first_leaf_of():
    return lax.axis_index(ALL) * 2


def weight_of(w_ref, k):
    return w_ref[k : k + 1, 0:1]


def block(k):
    return slice(k * ROWS, (k + 1) * ROWS)


def make_symmetric(points, row, table_ref):
    for i in range(STEPS):
        rows = points[block(i), :]
        rest = slice(i * ROWS, LEAF)
        table_ref[block(i), rest] = gauss(
            rows, left_column(rows), points[rest, :], row[:, rest]
        ).astype(bf16)


def dot_symmetric(field, table_ref):
    out = [None] * STEPS

    def add(k, value):
        out[k] = value if out[k] is None else out[k] + value

    for i in range(STEPS):
        straight = nn(field[:, block(i)], table_ref[block(i), i * ROWS : LEAF])
        for j in range(i, STEPS):
            add(j, straight[:, block(j - i)])
        if i + 1 < STEPS:
            after = slice((i + 1) * ROWS, LEAF)
            add(i, nt(field[:, after], table_ref[block(i), after]))
    return jnp.concatenate(out, axis=1)


def make_block(left, points, row, table_ref):
    for i in range(STEPS):
        rows = left[block(i), :]
        table_ref[block(i), :] = gauss(rows, left_column(rows), points, row).astype(bf16)


def tables_a_kernel(
    x_ref, b_ref, after_ref, table_ref, own_ref, row_ref, up_ref, down_ref
):
    del after_ref
    for k in range(STEPS):
        place = slice(LEAF + k * RHS, LEAF + (k + 1) * RHS)
        up_ref[place, :] = b_ref[:, LEAF + k * ROWS : LEAF + (k + 1) * ROWS].astype(bf16)
        down_ref[place, :] = b_ref[:, k * ROWS : (k + 1) * ROWS].astype(bf16)
    up_ref[:LEAF, :] = x_ref[LEAF:, :]
    down_ref[:LEAF, :] = x_ref[:LEAF, :]
    row_ref[...] = right_row(x_ref[...])
    make_symmetric(x_ref[:LEAF, :], row_ref[:, :LEAF], table_ref)
    own_ref[...] = dot_symmetric(b_ref[:, :LEAF].astype(bf16), table_ref)


def tables_a_call(points, field, after):
    return pl.pallas_call(
        tables_a_kernel,
        in_specs=inside(2) + [anywhere()],
        out_shape=(
            shape_of((LEAF, LEAF), bf16),
            shape_of((RHS, LEAF), f32),
            shape_of((1, 2 * LEAF), f32),
            shape_of((LEAF + STEPS * RHS, DIM), bf16),
            shape_of((LEAF + STEPS * RHS, DIM), bf16),
        ),
        compiler_params=params,
        cost_estimate=cost(700_000_000, 5_000_000, 700_000),
        name="tables_a",
    )(points, field, after)


def tables_b_kernel(
    w_ref, x_ref, b_ref, row_ref, own_a_ref, after_ref, table_b_ref, table_ab_ref, own_ref
):
    del after_ref
    row_b = row_ref[:, LEAF:]
    make_symmetric(x_ref[LEAF:, :], row_b, table_b_ref)
    make_block(x_ref[:LEAF, :], x_ref[LEAF:, :], row_b, table_ab_ref)
    b_a, b_b = b_ref[:, :LEAF].astype(bf16), b_ref[:, LEAF:].astype(bf16)
    own_ref[:, :LEAF] = own_a_ref[...] + weight_of(w_ref, 1) * nt(b_b, table_ab_ref[...])
    own_ref[:, LEAF:] = dot_symmetric(b_b, table_b_ref) + weight_of(w_ref, 2) * nn(
        b_a, table_ab_ref[...]
    )


def tables_b_call(w, points, field, row, own_a, after):
    return pl.pallas_call(
        tables_b_kernel,
        in_specs=inside(5) + [anywhere()],
        out_shape=(
            shape_of((LEAF, LEAF), bf16),
            shape_of((LEAF, LEAF), bf16),
            shape_of((RHS, 2 * LEAF), f32),
        ),
        compiler_params=params,
        cost_estimate=cost(1_500_000_000, 7_000_000, 1_800_000),
        name="tables_b",
    )(w, points, field, row, own_a, after)


def unfold(halo_ref):
    parts = [halo_ref[LEAF + k * RHS : LEAF + (k + 1) * RHS, :] for k in range(STEPS)]
    return jnp.concatenate(parts, axis=1)


def around_kernel(
    w_ref, below_ref, above_ref, x_ref, row_ref, own_ref, below_table_ref, above_table_ref, out_ref
):
    make_block(below_ref[:LEAF, :], x_ref[:LEAF, :], row_ref[:, :LEAF], below_table_ref)
    out_ref[:, :LEAF] = own_ref[:, :LEAF] + weight_of(w_ref, 0) * nn(
        unfold(below_ref), below_table_ref[...]
    )
    make_block(above_ref[:LEAF, :], x_ref[LEAF:, :], row_ref[:, LEAF:], above_table_ref)
    out_ref[:, LEAF:] = own_ref[:, LEAF:] + weight_of(w_ref, 3) * nn(
        unfold(above_ref), above_table_ref[...]
    )


def around_call(w, below, above, points, row, own):
    return pl.pallas_call(
        around_kernel,
        in_specs=inside(6),
        out_shape=(
            shape_of((LEAF, LEAF), bf16),
            shape_of((LEAF, LEAF), bf16),
            shape_of((RHS, 2 * LEAF), f32),
        ),
        compiler_params=params,
        cost_estimate=cost(1_400_000_000, 7_000_000, 2_097_152),
        name="around",
    )(w, below, above, points, row, own)


def total_of(got_ref):
    total = got_ref[0].astype(f32)
    for k in range(1, got_ref.shape[0]):
        total += got_ref[k].astype(f32)
    return total


def climb_kernel(got_ref, table_ref, after_ref, up_ref, sent_ref):
    del after_ref
    total = total_of(got_ref)
    up_ref[...] = total
    value = (nn(total, table_ref[...], highest) * (1.0 / SKEL)).astype(bf16)
    for k in range(sent_ref.shape[0]):
        sent_ref[k] = value


def climb_call(got, table, peers, after):
    return pl.pallas_call(
        climb_kernel,
        in_specs=inside(2) + [anywhere()],
        out_shape=(shape_of((RHS, SKEL), f32), shape_of((peers, RHS, SKEL), bf16)),
        compiler_params=params,
        cost_estimate=cost(50_000_000, 900_000),
        name="climb",
    )(got, table, after)


def down_weights(up_one, up_two, up_top, low_table, high_table):
    down_top = level_top * up_top
    down_two = level_two * up_two + nt(down_top, high_table, highest) * (1.0 / SKEL)
    return level_one * up_one + nt(down_two, low_table, highest) * (1.0 / SKEL)


def second_kernel(
    got_ref, p1_ref, p2_ref, t1_ref, t2_ref, gh_ref, gl_ref, own_ref, u_ref, up_ref, down_ref
):
    weights = down_weights(p1_ref[...], p2_ref[...], total_of(got_ref), t1_ref[...], t2_ref[...])
    for k in range(2):
        part = slice(k * LEAF, (k + 1) * LEAF)
        far = down_dot(weights, gh_ref[part, :], gl_ref[part, :])
        value = (own_ref[:, part] + far) * (1.0 / LEAF)
        u_ref[:, part] = value
        (down_ref, up_ref)[k][...] = value.astype(bf16)


def second_call(got, p1, p2, t1, t2, gh, gl, own):
    return pl.pallas_call(
        second_kernel,
        in_specs=inside(8),
        out_shape=(
            shape_of((RHS, 2 * LEAF), f32),
            shape_of((RHS, LEAF), bf16),
            shape_of((RHS, LEAF), bf16),
        ),
        compiler_params=params,
        cost_estimate=cost(250_000_000, 5_000_000),
        name="second",
    )(got, p1, p2, t1, t2, gh, gl, own)


def row_sum(value):
    return jnp.sum(value, axis=1, keepdims=True)


def third_kernel(
    w_ref, u_ref, b_ref, u_a_ref, u_b_ref, table_a_ref, table_b_ref, table_ab_ref,
    gh_ref, gl_ref, out_ref, up_ref, sums_ref
):
    up_ref[...] = up_dot(u_ref[...], gh_ref[...], gl_ref[...])
    u_a, u_b = u_a_ref[...], u_b_ref[...]
    out_ref[:, :LEAF] = dot_symmetric(u_a, table_a_ref) + weight_of(w_ref, 1) * nt(
        u_b, table_ab_ref[...]
    )
    out_ref[:, LEAF:] = dot_symmetric(u_b, table_b_ref) + weight_of(w_ref, 2) * nn(
        u_a, table_ab_ref[...]
    )
    b, u = b_ref[...], u_ref[...]
    lane = lax.broadcasted_iota(jnp.int32, (RHS, 128), 1)
    sums = (row_sum(b * b), row_sum(b * u), row_sum(u * u))
    total = jnp.zeros((RHS, 128), f32)
    for k in range(3):
        total = jnp.where(lane == k, sums[k], total)
    sums_ref[...] = total


def third_call(w, u, field, u_a, u_b, table_a, table_b, table_ab, gh, gl):
    return pl.pallas_call(
        third_kernel,
        in_specs=inside(10),
        out_shape=(
            shape_of((RHS, 2 * LEAF), f32),
            shape_of((RHS, SKEL), f32),
            shape_of((RHS, 128), f32),
        ),
        compiler_params=params,
        cost_estimate=cost(700_000_000, 10_000_000),
        name="third",
    )(w, u, field, u_a, u_b, table_a, table_b, table_ab, gh, gl)


def rows_of(sums):
    high = sums.astype(bf16).astype(f32)
    rest = sums - high
    middle = rest.astype(bf16).astype(f32)
    low = rest - middle
    lane = lax.broadcasted_iota(jnp.int32, (RHS, 128), 1)
    packed = jnp.where(lane < 4, high, 0.0)
    packed += jnp.where((lane >= 4) & (lane < 8), pltpu.roll(middle, 4, 1), 0.0)
    packed += jnp.where((lane >= 8) & (lane < 12), pltpu.roll(low, 8, 1), 0.0)
    turned = packed.T[:16]
    return jnp.concatenate([turned, jnp.zeros((16, SKEL - RHS), f32)], axis=1)


def sums_of(rows):
    turned = jnp.concatenate([rows[:, :RHS], jnp.zeros((112, RHS), f32)], axis=0).T
    total = turned + (pltpu.roll(turned, 124, 1) + pltpu.roll(turned, 120, 1))
    lane = lax.broadcasted_iota(jnp.int32, (RHS, 128), 1)
    return jnp.where(lane < 4, total, 0.0)


def put_all(sent_ref, value, sums):
    message = jnp.concatenate([value, rows_of(sums)], axis=0).astype(bf16)
    for k in range(sent_ref.shape[0]):
        sent_ref[k] = message


def add_last(sums, column):
    lane = lax.broadcasted_iota(jnp.int32, (RHS, 128), 1)
    return sums + jnp.where(lane == 3, column, 0.0)


def finish_kernel(
    w_ref, below_ref, above_ref, below_table_ref, above_table_ref, u_ref, own_ref, up_ref,
    sums_ref, sent_ref, out_ref
):
    near_a = own_ref[:, :LEAF] + weight_of(w_ref, 0) * nn(below_ref[...], below_table_ref[...])
    near_b = own_ref[:, LEAF:] + weight_of(w_ref, 3) * nn(above_ref[...], above_table_ref[...])
    out_ref[:, :LEAF] = near_a
    out_ref[:, LEAF:] = near_b
    bend = row_sum(u_ref[:, :LEAF] * near_a) + row_sum(u_ref[:, LEAF:] * near_b)
    put_all(sent_ref, up_ref[...] * (1.0 / LEAF), add_last(sums_ref[...], bend * (1.0 / LEAF)))


def finish_call(w, below, above, below_table, above_table, u, own, up, sums, peers):
    return pl.pallas_call(
        finish_kernel,
        in_specs=inside(9),
        out_shape=(
            shape_of((peers, RHS + 16, SKEL), bf16),
            shape_of((RHS, 2 * LEAF), f32),
        ),
        compiler_params=params,
        cost_estimate=cost(270_000_000, 4_000_000),
        name="finish",
    )(w, below, above, below_table, above_table, u, own, up, sums)


def climb_sums_kernel(level, got_ref, table_ref, up_ref, sent_ref):
    total = total_of(got_ref)
    up = total[:RHS]
    up_ref[...] = up
    sums = add_last(sums_of(total[RHS:]), level * row_sum(up * up))
    put_all(sent_ref, nn(up, table_ref[...], highest) * (1.0 / SKEL), sums)


def climb_sums_call(got, table, level, peers):
    return pl.pallas_call(
        lambda *refs: climb_sums_kernel(level, *refs),
        out_shape=(shape_of((RHS, SKEL), f32), shape_of((peers, RHS + 16, SKEL), bf16)),
        compiler_params=params,
        cost_estimate=cost(50_000_000, 900_000),
        name="climb_sums",
    )(got, table)


def last_kernel(
    got_ref, p1_ref, p2_ref, t1_ref, t2_ref, gh_ref, gl_ref, near_ref, b_ref, u_ref, x_ref, r_ref
):
    total = total_of(got_ref)
    top = total[:RHS]
    weights = down_weights(p1_ref[...], p2_ref[...], top, t1_ref[...], t2_ref[...])
    sums = add_last(sums_of(total[RHS:]), level_top * row_sum(top * top))
    bb, bu, uu, uv = sums[:, 0:1], sums[:, 1:2], sums[:, 2:3], sums[:, 3:4]
    step_one = bb / (ridge_term * bb + bu)
    ratio = bu / bb
    norm_one = step_one * step_one * (uu - ratio * bu)
    beta = norm_one / bb
    bend_rr = step_one * step_one * (ratio * ratio * bu - 2.0 * ratio * uu + uv)
    bend_rb = step_one * (ratio * bu - uu)
    bending = (
        ridge_term * (norm_one + beta * beta * bb)
        + bend_rr
        + 2.0 * beta * bend_rb
        + beta * beta * bu
    )
    step_two = norm_one / bending
    for k in range(2):
        part = slice(k * LEAF, (k + 1) * LEAF)
        far = down_dot(weights, gh_ref[part, :], gl_ref[part, :])
        third = (near_ref[:, part] + far) * (1.0 / LEAF)
        first, second = b_ref[:, part], u_ref[:, part]
        residual_one = (step_one * ratio) * first - step_one * second
        direction = residual_one + beta * first
        applied = (
            ridge_term * direction + (step_one * ratio + beta) * second - step_one * third
        )
        x_ref[:, part] = step_one * first + step_two * direction
        r_ref[:, part] = residual_one - step_two * applied


def last_call(got, p1, p2, t1, t2, gh, gl, near, field, u):
    return pl.pallas_call(
        last_kernel,
        in_specs=inside(10),
        out_shape=(shape_of((RHS, 2 * LEAF), f32), shape_of((RHS, 2 * LEAF), f32)),
        compiler_params=params,
        cost_estimate=cost(250_000_000, 7_000_000),
        name="last",
    )(got, p1, p2, t1, t2, gh, gl, near, field, u)


def exchange(sent, axis):
    return lax.all_to_all(sent, axis, 0, 0)


def shift_up(value):
    count = lax.axis_size(ALL)
    return lax.ppermute(value, ALL, [(i, i + 1) for i in range(count - 1)])


def shift_down(value):
    count = lax.axis_size(ALL)
    return lax.ppermute(value, ALL, [(i + 1, i) for i in range(count - 1)])


def shards(points, right_side, skel_sub, skel_group, skel_top, neighbors, counts):
    leaves, subs, groups = (lax.axis_size(axis) for axis in ("leaf", "sub", "group"))
    sent, gh, gl, t1, t2, x, b, w = start_call(
        neighbors, counts, points, skel_sub, skel_group, skel_top, right_side, leaves
    )
    got = exchange(sent, "leaf")
    table_a, own_a, row, up, down = tables_a_call(x, b, sent)
    below, above = shift_up(up), shift_down(down)
    up_one, sent = climb_call(got, t1, subs, own_a)
    got = exchange(sent, "sub")
    table_b, table_ab, own = tables_b_call(w, x, b, row, own_a, sent)
    up_two, sent = climb_call(got, t2, groups, own)
    got = exchange(sent, "group")
    below_table, above_table, own = around_call(w, below, above, x, row, own)
    u, up, down = second_call(got, up_one, up_two, t1, t2, gh, gl, own)

    below, above = shift_up(up), shift_down(down)
    own, weights, sums = third_call(w, u, b, down, up, table_a, table_b, table_ab, gh, gl)
    sent, near = finish_call(
        w, below, above, below_table, above_table, u, own, weights, sums, leaves
    )
    got = exchange(sent, "leaf")
    up_one, sent = climb_sums_call(got, t1, level_one, subs)
    got = exchange(sent, "sub")
    up_two, sent = climb_sums_call(got, t2, level_two, groups)
    got = exchange(sent, "group")
    return last_call(got, up_one, up_two, t1, t2, gh, gl, near, b, u)


def solution(mesh):
    return jax.shard_map(
        shards,
        mesh=mesh,
        in_specs=(
            P(ALL, None),
            P(None, ALL),
            P(("group", "sub"), None),
            P("group", None),
            P(),
            P(ALL, None),
            P(ALL),
        ),
        out_specs=(P(None, ALL), P(None, ALL)),
        check_vma=False,
    )
```

```python
import math

import jax
import jax.numpy as jnp
from jax import lax
from jax.experimental import pallas as pl
from jax.experimental.pallas import tpu as pltpu
from jax.sharding import PartitionSpec as P

LEAF = 1024
SKEL = 256
RHS = 64
DIM = 256
ROWS = 256
STEPS = LEAF // ROWS
WIDE = 512
ALL = ("group", "sub", "leaf")

ridge_term = 3.0
level_one = 0.5
level_two = 0.25
level_top = 0.3

bf16 = jnp.bfloat16
f32 = jnp.float32
per_unit = 0.25 / DIM * math.log2(math.e)
vmem_bytes = 20 * 1024 * 1024


def shape_of(shape, dtype):
    return jax.ShapeDtypeStruct(shape, dtype)


def cost(flops, moved, exps=0):
    return pl.CostEstimate(flops=flops, bytes_accessed=moved, transcendentals=exps)


params = pltpu.CompilerParams(vmem_limit_bytes=vmem_bytes)


def nn(left, right, precision=None):
    return lax.dot_general(
        left, right, (((1,), (0,)), ((), ())), precision=precision, preferred_element_type=f32
    )


def nt(left, right, precision=None):
    return lax.dot_general(
        left, right, (((1,), (1,)), ((), ())), precision=precision, preferred_element_type=f32
    )


highest = lax.Precision.HIGHEST


def squares(rows):
    wide = rows.astype(f32)
    return wide * wide


def left_column(rows):
    return jnp.sum(squares(rows), axis=1, keepdims=True) * per_unit


def right_row(rows):
    square = squares(rows)
    high = square.astype(bf16)
    low = (square - high.astype(f32)).astype(bf16)
    ones = jnp.ones((8, rows.shape[1]), bf16)
    return (nt(ones, high) + nt(ones, low))[0:1] * per_unit


def gauss(left, column, right, row):
    return jnp.exp2(nt(left, right) * (2.0 * per_unit) - column - row)


def split(value):
    high = value.astype(bf16)
    low = (value - high.astype(f32)).astype(bf16)
    return high, low


def up_dot(field, table_high, table_low):
    high, low = split(field)
    both = nn(jnp.concatenate([high, low], axis=0), table_high)
    return both[:RHS] + both[RHS:] + nn(high, table_low)


def down_dot(weights, table_high, table_low):
    high, low = split(weights)
    both = nt(jnp.concatenate([high, low], axis=0), table_high)
    return both[:RHS] + both[RHS:] + nt(high, table_low)


def even_leaf():
    return lax.rem(lax.axis_index("leaf"), 2) == 0


def pack_kernel(x_ref, b_ref, odd_ref, even_ref, xv_ref, bv_ref, x_sem, b_sem):
    loads = []
    for k in range(2):
        part = pl.ds(k * LEAF, LEAF)
        loads.append(
            (
                pltpu.make_async_copy(b_ref.at[:, part], bv_ref.at[:, part], b_sem.at[k]),
                pltpu.make_async_copy(x_ref.at[part, :], xv_ref.at[part, :], x_sem.at[k]),
            )
        )
    for pair_of in loads:
        for load in pair_of:
            load.start()
    for pair_of in loads:
        for load in pair_of:
            load.wait()

    def fill(out_ref, first):
        out_ref[:LEAF, :] = xv_ref[first : first + LEAF, :]
        for k in range(STEPS):
            place = slice(LEAF + k * RHS, LEAF + (k + 1) * RHS)
            out_ref[place, :] = bv_ref[:, first + k * ROWS : first + (k + 1) * ROWS].astype(bf16)

    even = even_leaf()

    @pl.when(even)
    def _():
        fill(odd_ref, 0)
        fill(even_ref, LEAF)

    @pl.when(jnp.logical_not(even))
    def _():
        fill(odd_ref, LEAF)
        fill(even_ref, 0)


def in_hbm(value):
    return pltpu.with_memory_space_constraint(value, pltpu.HBM)


def pack_call(points, field):
    count = points.shape[0]
    return pl.pallas_call(
        pack_kernel,
        in_specs=[pl.BlockSpec(memory_space=pltpu.HBM)] * 2,
        out_shape=(
            shape_of((LEAF + STEPS * RHS, DIM), bf16),
            shape_of((LEAF + STEPS * RHS, DIM), bf16),
        ),
        scratch_shapes=[
            pltpu.VMEM((count, DIM), bf16),
            pltpu.VMEM((RHS, count), f32),
            pltpu.SemaphoreType.DMA((2,)),
            pltpu.SemaphoreType.DMA((2,)),
        ],
        compiler_params=params,
        cost_estimate=cost(1_000_000, 5_000_000),
        name="pack",
    )(in_hbm(points), in_hbm(field))


def start_kernel(
    x_ref, b_ref, z1_ref, z2_ref, z3_ref, sent_ref, gh_ref, gl_ref, t1_ref, t2_ref,
    xv_ref, bv_ref, z_ref, x_sem, b_sem, z_sem
):
    parts = x_ref.shape[0] // WIDE
    z_loads, x_loads, b_loads = [], [], []
    for k, source in enumerate((z1_ref, z2_ref, z3_ref)):
        z_loads.append(pltpu.make_async_copy(source, z_ref.at[k], z_sem.at[k]))
    for k in range(parts):
        rows = pl.ds(k * WIDE, WIDE)
        x_loads.append(pltpu.make_async_copy(x_ref.at[rows, :], xv_ref.at[rows, :], x_sem.at[k]))
        b_loads.append(pltpu.make_async_copy(b_ref.at[:, rows], bv_ref.at[:, rows], b_sem.at[k]))
    z_loads[0].start()
    for k in range(parts):
        x_loads[k].start()
        b_loads[k].start()
    z_loads[1].start()
    z_loads[2].start()
    z_loads[0].wait()
    z1 = z_ref[0]
    row = right_row(z1)
    total = jnp.zeros((RHS, SKEL), f32)
    for k in range(parts):
        rows = slice(k * WIDE, (k + 1) * WIDE)
        x_loads[k].wait()
        part = xv_ref[rows, :]
        high, low = split(gauss(part, left_column(part), z1, row))
        gh_ref[rows, :] = high
        gl_ref[rows, :] = low
        b_loads[k].wait()
        total += up_dot(bv_ref[:, rows], high, low)
    value = (total * (1.0 / LEAF)).astype(bf16)
    for k in range(sent_ref.shape[0]):
        sent_ref[k] = value
    z_loads[1].wait()
    z_loads[2].wait()
    z2, z3 = z_ref[1], z_ref[2]
    t1_ref[...] = gauss(z1, left_column(z1), z2, right_row(z2))
    t2_ref[...] = gauss(z2, left_column(z2), z3, right_row(z3))


def start_call(points, field, z1, z2, z3, peers):
    count = points.shape[0]
    parts = count // WIDE
    return pl.pallas_call(
        start_kernel,
        in_specs=[pl.BlockSpec(memory_space=pltpu.HBM)] * 5,
        out_shape=(
            shape_of((peers, RHS, SKEL), bf16),
            shape_of((count, SKEL), bf16),
            shape_of((count, SKEL), bf16),
            shape_of((SKEL, SKEL), f32),
            shape_of((SKEL, SKEL), f32),
        ),
        scratch_shapes=[
            pltpu.VMEM((count, DIM), bf16),
            pltpu.VMEM((RHS, count), f32),
            pltpu.VMEM((3, SKEL, DIM), bf16),
            pltpu.SemaphoreType.DMA((parts,)),
            pltpu.SemaphoreType.DMA((parts,)),
            pltpu.SemaphoreType.DMA((3,)),
        ],
        compiler_params=params,
        cost_estimate=cost(600_000_000, 5_000_000, 655_360),
        name="start",
    )(*(in_hbm(value) for value in (points, field, z1, z2, z3)))


def smem():
    return pl.BlockSpec(memory_space=pltpu.SMEM)


def anywhere():
    return pl.BlockSpec(memory_space=pl.ANY)


def inside(count):
    return [pl.BlockSpec(memory_space=pltpu.VMEM)] * count


def listed(nb_ref, ct_ref, position, target):
    found = 0.0
    for k in range(nb_ref.shape[1]):
        hit = (k < ct_ref[position]) & (nb_ref[position, k] == target)
        found = found + jnp.where(hit, 1.0, 0.0)
    return found


def first_leaf_of():
    return lax.axis_index(ALL) * 2


def weight_of(w_ref, k):
    return w_ref[k : k + 1, 0:1]


def block(k):
    return slice(k * ROWS, (k + 1) * ROWS)


def make_symmetric(points, row, table_ref):
    for i in range(STEPS):
        rows = points[block(i), :]
        rest = slice(i * ROWS, LEAF)
        table_ref[block(i), rest] = gauss(
            rows, left_column(rows), points[rest, :], row[:, rest]
        ).astype(bf16)


def dot_symmetric(field, table_ref):
    out = [None] * STEPS

    def add(k, value):
        out[k] = value if out[k] is None else out[k] + value

    for i in range(STEPS):
        straight = nn(field[:, block(i)], table_ref[block(i), i * ROWS : LEAF])
        for j in range(i, STEPS):
            add(j, straight[:, block(j - i)])
        if i + 1 < STEPS:
            after = slice((i + 1) * ROWS, LEAF)
            add(i, nt(field[:, after], table_ref[block(i), after]))
    return jnp.concatenate(out, axis=1)


def make_block(left, points, row, table_ref):
    for i in range(STEPS):
        rows = left[block(i), :]
        table_ref[block(i), :] = gauss(rows, left_column(rows), points, row).astype(bf16)


def tables_kernel(
    nb_ref, ct_ref, x_ref, b_ref, after_ref,
    table_a_ref, table_b_ref, table_ab_ref, own_ref, row_ref, w_ref, xv_ref, bv_ref,
    x_sem, b_sem
):
    del after_ref
    x_loads, b_loads = [], []
    for k in range(2):
        part = pl.ds(k * LEAF, LEAF)
        x_loads.append(pltpu.make_async_copy(x_ref.at[part, :], xv_ref.at[part, :], x_sem.at[k]))
        b_loads.append(pltpu.make_async_copy(b_ref.at[:, part], bv_ref.at[:, part], b_sem.at[k]))
    for load in x_loads + b_loads:
        load.start()
    first = first_leaf_of()
    weights = (
        listed(nb_ref, ct_ref, 0, first - 1),
        listed(nb_ref, ct_ref, 0, first + 1),
        listed(nb_ref, ct_ref, 1, first),
        listed(nb_ref, ct_ref, 1, first + 2),
    )
    place = lax.broadcasted_iota(jnp.int32, (8, 128), 0)
    spread = jnp.zeros((8, 128), f32)
    for k in range(4):
        spread = jnp.where(place == k, weights[k], spread)
    w_ref[...] = spread
    x_loads[0].wait()
    x_a = xv_ref[:LEAF, :]
    row_ref[:, :LEAF] = right_row(x_a)
    make_symmetric(x_a, row_ref[:, :LEAF], table_a_ref)
    x_loads[1].wait()
    x_b = xv_ref[LEAF:, :]
    row_ref[:, LEAF:] = right_row(x_b)
    make_symmetric(x_b, row_ref[:, LEAF:], table_b_ref)
    make_block(x_a, x_b, row_ref[:, LEAF:], table_ab_ref)
    b_loads[0].wait()
    b_loads[1].wait()
    b_a, b_b = bv_ref[:, :LEAF].astype(bf16), bv_ref[:, LEAF:].astype(bf16)
    own_ref[:, :LEAF] = dot_symmetric(b_a, table_a_ref) + weights[1] * nt(b_b, table_ab_ref[...])
    own_ref[:, LEAF:] = dot_symmetric(b_b, table_b_ref) + weights[2] * nn(b_a, table_ab_ref[...])


def tables_call(neighbors, counts, points, field, after):
    count = points.shape[0]
    return pl.pallas_call(
        tables_kernel,
        in_specs=[smem(), smem()]
        + [pl.BlockSpec(memory_space=pltpu.HBM)] * 2
        + [anywhere()],
        out_shape=(
            shape_of((LEAF, LEAF), bf16),
            shape_of((LEAF, LEAF), bf16),
            shape_of((LEAF, LEAF), bf16),
            shape_of((RHS, 2 * LEAF), f32),
            shape_of((1, 2 * LEAF), f32),
            shape_of((8, 128), f32),
            shape_of((count, DIM), bf16),
            shape_of((RHS, count), f32),
        ),
        scratch_shapes=[pltpu.SemaphoreType.DMA((2,)), pltpu.SemaphoreType.DMA((2,))],
        compiler_params=params,
        cost_estimate=cost(2_200_000_000, 9_000_000, 2_400_000),
        name="tables",
    )(neighbors, counts, in_hbm(points), in_hbm(field), after)


def unfold(halo):
    parts = [halo[LEAF + k * RHS : LEAF + (k + 1) * RHS, :] for k in range(STEPS)]
    return jnp.concatenate(parts, axis=1)


def in_order(odd_ref, even_ref):
    even = even_leaf()
    odd_got, even_got = odd_ref[...], even_ref[...]
    return jnp.where(even, odd_got, even_got), jnp.where(even, even_got, odd_got)


def around_kernel(
    w_ref, odd_ref, even_ref, x_ref, row_ref, own_ref, after_ref,
    below_table_ref, above_table_ref, out_ref
):
    del after_ref

    def build(below_ref, above_ref):
        make_block(below_ref, x_ref[:LEAF, :], row_ref[:, :LEAF], below_table_ref)
        out_ref[:, :LEAF] = own_ref[:, :LEAF] + weight_of(w_ref, 0) * nn(
            unfold(below_ref), below_table_ref[...]
        )
        make_block(above_ref, x_ref[LEAF:, :], row_ref[:, LEAF:], above_table_ref)
        out_ref[:, LEAF:] = own_ref[:, LEAF:] + weight_of(w_ref, 3) * nn(
            unfold(above_ref), above_table_ref[...]
        )

    even = even_leaf()

    @pl.when(even)
    def _():
        build(odd_ref, even_ref)

    @pl.when(jnp.logical_not(even))
    def _():
        build(even_ref, odd_ref)


def around_call(w, odd, even, points, row, own, after):
    return pl.pallas_call(
        around_kernel,
        in_specs=inside(6) + [anywhere()],
        out_shape=(
            shape_of((LEAF, LEAF), bf16),
            shape_of((LEAF, LEAF), bf16),
            shape_of((RHS, 2 * LEAF), f32),
        ),
        compiler_params=params,
        cost_estimate=cost(1_400_000_000, 7_000_000, 2_097_152),
        name="around",
    )(w, odd, even, points, row, own, after)


def total_of(got_ref):
    total = got_ref[0].astype(f32)
    for k in range(1, got_ref.shape[0]):
        total += got_ref[k].astype(f32)
    return total


def climb_kernel(got_ref, table_ref, after_ref, up_ref, sent_ref):
    del after_ref
    total = total_of(got_ref)
    up_ref[...] = total
    value = (nn(total, table_ref[...], highest) * (1.0 / SKEL)).astype(bf16)
    if len(sent_ref.shape) == 2:
        sent_ref[...] = value
    else:
        for k in range(sent_ref.shape[0]):
            sent_ref[k] = value


def climb_call(got, table, shape, after):
    return pl.pallas_call(
        climb_kernel,
        in_specs=inside(2) + [anywhere()],
        out_shape=(shape_of((RHS, SKEL), f32), shape_of(shape + (RHS, SKEL), bf16)),
        compiler_params=params,
        cost_estimate=cost(50_000_000, 900_000),
        name="climb",
    )(got, table, after)


def sum_of(refs):
    total = refs[0][...].astype(f32)
    for ref in refs[1:]:
        total += ref[...].astype(f32)
    return total


def down_weights(up_one, up_two, up_top, low_table, high_table):
    down_top = level_top * up_top
    down_two = level_two * up_two + nt(down_top, high_table, highest) * (1.0 / SKEL)
    return level_one * up_one + nt(down_two, low_table, highest) * (1.0 / SKEL)


def second_kernel(
    g0_ref, g1_ref, g2_ref, g3_ref, p1_ref, p2_ref, t1_ref, t2_ref, gh_ref, gl_ref, own_ref,
    u_ref, u16_ref, odd_ref, even_ref
):
    top = sum_of((g0_ref, g1_ref, g2_ref, g3_ref))
    weights = down_weights(p1_ref[...], p2_ref[...], top, t1_ref[...], t2_ref[...])
    for k in range(2):
        part = slice(k * LEAF, (k + 1) * LEAF)
        far = down_dot(weights, gh_ref[part, :], gl_ref[part, :])
        value = (own_ref[:, part] + far) * (1.0 / LEAF)
        u_ref[:, part] = value
        u16_ref[:, part] = value.astype(bf16)
    even = even_leaf()

    @pl.when(even)
    def _():
        odd_ref[...] = u16_ref[:, :LEAF]
        even_ref[...] = u16_ref[:, LEAF:]

    @pl.when(jnp.logical_not(even))
    def _():
        odd_ref[...] = u16_ref[:, LEAF:]
        even_ref[...] = u16_ref[:, :LEAF]


def second_call(parts, p1, p2, t1, t2, gh, gl, own):
    return pl.pallas_call(
        second_kernel,
        in_specs=inside(11),
        out_shape=(
            shape_of((RHS, 2 * LEAF), f32),
            shape_of((RHS, 2 * LEAF), bf16),
            shape_of((RHS, LEAF), bf16),
            shape_of((RHS, LEAF), bf16),
        ),
        compiler_params=params,
        cost_estimate=cost(250_000_000, 5_000_000),
        name="second",
    )(*parts, p1, p2, t1, t2, gh, gl, own)


def row_sum(value):
    return jnp.sum(value, axis=1, keepdims=True)


def third_kernel(
    w_ref, u_ref, b_ref, u16_ref, table_a_ref, table_b_ref, table_ab_ref,
    gh_ref, gl_ref, out_ref, up_ref, sums_ref
):
    up_ref[...] = up_dot(u_ref[...], gh_ref[...], gl_ref[...])
    u_a, u_b = u16_ref[:, :LEAF], u16_ref[:, LEAF:]
    out_ref[:, :LEAF] = dot_symmetric(u_a, table_a_ref) + weight_of(w_ref, 1) * nt(
        u_b, table_ab_ref[...]
    )
    out_ref[:, LEAF:] = dot_symmetric(u_b, table_b_ref) + weight_of(w_ref, 2) * nn(
        u_a, table_ab_ref[...]
    )
    b, u = b_ref[...], u_ref[...]
    lane = lax.broadcasted_iota(jnp.int32, (RHS, 128), 1)
    sums = (row_sum(b * b), row_sum(b * u), row_sum(u * u))
    total = jnp.zeros((RHS, 128), f32)
    for k in range(3):
        total = jnp.where(lane == k, sums[k], total)
    sums_ref[...] = total


def third_call(w, u, field, u16, table_a, table_b, table_ab, gh, gl):
    return pl.pallas_call(
        third_kernel,
        in_specs=inside(9),
        out_shape=(
            shape_of((RHS, 2 * LEAF), f32),
            shape_of((RHS, SKEL), f32),
            shape_of((RHS, 128), f32),
        ),
        compiler_params=params,
        cost_estimate=cost(700_000_000, 10_000_000),
        name="third",
    )(w, u, field, u16, table_a, table_b, table_ab, gh, gl)


def rows_of(sums):
    high = sums.astype(bf16).astype(f32)
    rest = sums - high
    middle = rest.astype(bf16).astype(f32)
    low = rest - middle
    lane = lax.broadcasted_iota(jnp.int32, (RHS, 128), 1)
    packed = jnp.where(lane < 4, high, 0.0)
    packed += jnp.where((lane >= 4) & (lane < 8), pltpu.roll(middle, 4, 1), 0.0)
    packed += jnp.where((lane >= 8) & (lane < 12), pltpu.roll(low, 8, 1), 0.0)
    turned = packed.T[:16]
    return jnp.concatenate([turned, jnp.zeros((16, SKEL - RHS), f32)], axis=1)


def sums_of(rows):
    turned = jnp.concatenate([rows[:, :RHS], jnp.zeros((112, RHS), f32)], axis=0).T
    total = turned + (pltpu.roll(turned, 124, 1) + pltpu.roll(turned, 120, 1))
    lane = lax.broadcasted_iota(jnp.int32, (RHS, 128), 1)
    return jnp.where(lane < 4, total, 0.0)


def put_all(sent_ref, value, sums):
    message = jnp.concatenate([value, rows_of(sums)], axis=0).astype(bf16)
    if len(sent_ref.shape) == 2:
        sent_ref[...] = message
    else:
        for k in range(sent_ref.shape[0]):
            sent_ref[k] = message


def add_last(sums, column):
    lane = lax.broadcasted_iota(jnp.int32, (RHS, 128), 1)
    return sums + jnp.where(lane == 3, column, 0.0)


def finish_kernel(
    w_ref, odd_ref, even_ref, below_table_ref, above_table_ref, u_ref, own_ref, up_ref,
    sums_ref, sent_ref, out_ref
):
    below, above = in_order(odd_ref, even_ref)
    near_a = own_ref[:, :LEAF] + weight_of(w_ref, 0) * nn(below, below_table_ref[...])
    near_b = own_ref[:, LEAF:] + weight_of(w_ref, 3) * nn(above, above_table_ref[...])
    out_ref[:, :LEAF] = near_a
    out_ref[:, LEAF:] = near_b
    bend = row_sum(u_ref[:, :LEAF] * near_a) + row_sum(u_ref[:, LEAF:] * near_b)
    put_all(sent_ref, up_ref[...] * (1.0 / LEAF), add_last(sums_ref[...], bend * (1.0 / LEAF)))


def finish_call(w, odd, even, below_table, above_table, u, own, up, sums, peers):
    return pl.pallas_call(
        finish_kernel,
        in_specs=inside(9),
        out_shape=(
            shape_of((peers, RHS + 16, SKEL), bf16),
            shape_of((RHS, 2 * LEAF), f32),
        ),
        compiler_params=params,
        cost_estimate=cost(270_000_000, 4_000_000),
        name="finish",
    )(w, odd, even, below_table, above_table, u, own, up, sums)


def climb_sums_kernel(level, got_ref, table_ref, up_ref, sent_ref):
    total = total_of(got_ref)
    up = total[:RHS]
    up_ref[...] = up
    sums = add_last(sums_of(total[RHS:]), level * row_sum(up * up))
    put_all(sent_ref, nn(up, table_ref[...], highest) * (1.0 / SKEL), sums)


def climb_sums_call(got, table, level, shape):
    return pl.pallas_call(
        lambda *refs: climb_sums_kernel(level, *refs),
        out_shape=(shape_of((RHS, SKEL), f32), shape_of(shape + (RHS + 16, SKEL), bf16)),
        compiler_params=params,
        cost_estimate=cost(50_000_000, 900_000),
        name="climb_sums",
    )(got, table)


def last_kernel(
    g0_ref, g1_ref, g2_ref, g3_ref, p1_ref, p2_ref, t1_ref, t2_ref, gh_ref, gl_ref, near_ref,
    b_ref, u_ref, x_ref, r_ref
):
    total = sum_of((g0_ref, g1_ref, g2_ref, g3_ref))
    top = total[:RHS]
    weights = down_weights(p1_ref[...], p2_ref[...], top, t1_ref[...], t2_ref[...])
    sums = add_last(sums_of(total[RHS:]), level_top * row_sum(top * top))
    bb, bu, uu, uv = sums[:, 0:1], sums[:, 1:2], sums[:, 2:3], sums[:, 3:4]
    step_one = bb / (ridge_term * bb + bu)
    ratio = bu / bb
    norm_one = step_one * step_one * (uu - ratio * bu)
    beta = norm_one / bb
    bend_rr = step_one * step_one * (ratio * ratio * bu - 2.0 * ratio * uu + uv)
    bend_rb = step_one * (ratio * bu - uu)
    bending = (
        ridge_term * (norm_one + beta * beta * bb)
        + bend_rr
        + 2.0 * beta * bend_rb
        + beta * beta * bu
    )
    step_two = norm_one / bending
    for k in range(2):
        part = slice(k * LEAF, (k + 1) * LEAF)
        far = down_dot(weights, gh_ref[part, :], gl_ref[part, :])
        third = (near_ref[:, part] + far) * (1.0 / LEAF)
        first, second = b_ref[:, part], u_ref[:, part]
        residual_one = (step_one * ratio) * first - step_one * second
        direction = residual_one + beta * first
        applied = (
            ridge_term * direction + (step_one * ratio + beta) * second - step_one * third
        )
        x_ref[:, part] = step_one * first + step_two * direction
        r_ref[:, part] = residual_one - step_two * applied


def last_call(parts, p1, p2, t1, t2, gh, gl, near, field, u):
    return pl.pallas_call(
        last_kernel,
        in_specs=inside(13),
        out_shape=(shape_of((RHS, 2 * LEAF), f32), shape_of((RHS, 2 * LEAF), f32)),
        compiler_params=params,
        cost_estimate=cost(250_000_000, 7_000_000),
        name="last",
    )(*parts, p1, p2, t1, t2, gh, gl, near, field, u)


def exchange(sent, axis):
    return lax.all_to_all(sent, axis, 0, 0)


def chain_swap(value, first):
    count = lax.axis_size(ALL)
    pairs = [(i, i + 1) for i in range(first, count - 1, 2)]
    return lax.ppermute(value, ALL, pairs + [(j, i) for i, j in pairs])


def swap_both(odd, even):
    return chain_swap(odd, 1), chain_swap(even, 0)


def turned(value, axis, shift):
    count = lax.axis_size(axis)
    return lax.ppermute(value, axis, [(i, (i + shift) % count) for i in range(count)])


def turns(value, axis):
    return [value] + [turned(value, axis, k) for k in range(1, lax.axis_size(axis))]


def shards(points, right_side, skel_sub, skel_group, skel_top, neighbors, counts):
    leaves, subs = (lax.axis_size(axis) for axis in ("leaf", "sub"))
    odd, even = swap_both(*pack_call(points, right_side))
    sent, gh, gl, t1, t2 = start_call(
        points, right_side, skel_sub, skel_group, skel_top, leaves
    )
    got = exchange(sent, "leaf")
    table_a, table_b, table_ab, own, row, w, x, b = tables_call(
        neighbors, counts, points, right_side, got
    )
    up_one, sent = climb_call(got, t1, (subs,), w)
    up_two, sent = climb_call(exchange(sent, "sub"), t2, (), w)
    parts = turns(sent, "group")
    below_table, above_table, own = around_call(w, odd, even, x, row, own, sent)
    u, u16, odd, even = second_call(parts, up_one, up_two, t1, t2, gh, gl, own)

    odd, even = swap_both(odd, even)
    own, weights, sums = third_call(w, u, b, u16, table_a, table_b, table_ab, gh, gl)
    sent, near = finish_call(
        w, odd, even, below_table, above_table, u, own, weights, sums, leaves
    )
    up_one, sent = climb_sums_call(exchange(sent, "leaf"), t1, level_one, (subs,))
    up_two, sent = climb_sums_call(exchange(sent, "sub"), t2, level_two, ())
    parts = turns(sent, "group")
    return last_call(parts, up_one, up_two, t1, t2, gh, gl, near, b, u)


def solution(mesh):
    return jax.shard_map(
        shards,
        mesh=mesh,
        in_specs=(
            P(ALL, None),
            P(None, ALL),
            P(("group", "sub"), None),
            P("group", None),
            P(),
            P(ALL, None),
            P(ALL),
        ),
        out_specs=(P(None, ALL), P(None, ALL)),
        check_vma=False,
    )
```

```python
import math

import jax
import jax.numpy as jnp
from jax import lax
from jax.experimental import pallas as pl
from jax.experimental.pallas import tpu as pltpu
from jax.sharding import PartitionSpec as P

LEAF = 1024
SKEL = 256
RHS = 64
DIM = 256
ROWS = 256
STEPS = LEAF // ROWS
WIDE = 512
ALL = ("group", "sub", "leaf")

ridge_term = 3.0
level_one = 0.5
level_two = 0.25
level_top = 0.3

bf16 = jnp.bfloat16
f32 = jnp.float32
per_unit = 0.25 / DIM * math.log2(math.e)
vmem_bytes = 20 * 1024 * 1024


def shape_of(shape, dtype):
    return jax.ShapeDtypeStruct(shape, dtype)


def cost(flops, moved, exps=0):
    return pl.CostEstimate(flops=flops, bytes_accessed=moved, transcendentals=exps)


params = pltpu.CompilerParams(vmem_limit_bytes=vmem_bytes)


def nn(left, right, precision=None):
    return lax.dot_general(
        left, right, (((1,), (0,)), ((), ())), precision=precision, preferred_element_type=f32
    )


def nt(left, right, precision=None):
    return lax.dot_general(
        left, right, (((1,), (1,)), ((), ())), precision=precision, preferred_element_type=f32
    )


highest = lax.Precision.HIGHEST


def squares(rows):
    wide = rows.astype(f32)
    return wide * wide


def left_column(rows):
    return jnp.sum(squares(rows), axis=1, keepdims=True) * per_unit


def right_row(rows):
    square = squares(rows)
    high = square.astype(bf16)
    low = (square - high.astype(f32)).astype(bf16)
    ones = jnp.ones((8, rows.shape[1]), bf16)
    return (nt(ones, high) + nt(ones, low))[0:1] * per_unit


def gauss(left, column, right, row):
    return jnp.exp2(nt(left, right) * (2.0 * per_unit) - column - row)


def split(value):
    high = value.astype(bf16)
    low = (value - high.astype(f32)).astype(bf16)
    return high, low


def up_dot(field, table_high, table_low):
    high, low = split(field)
    both = nn(jnp.concatenate([high, low], axis=0), table_high)
    return both[:RHS] + both[RHS:] + nn(high, table_low)


def down_dot(weights, table_high, table_low):
    high, low = split(weights)
    both = nt(jnp.concatenate([high, low], axis=0), table_high)
    return both[:RHS] + both[RHS:] + nt(high, table_low)


def even_leaf():
    return lax.rem(lax.axis_index("leaf"), 2) == 0


def in_hbm(value):
    return pltpu.with_memory_space_constraint(value, pltpu.HBM)


def outside(count):
    return [pl.BlockSpec(memory_space=pltpu.HBM)] * count


def start_kernel(
    x_ref, b_ref, z1_ref, z2_ref, z3_ref,
    sent_ref, gh_ref, gl_ref, t1_ref, t2_ref, odd_ref, even_ref,
    xv_ref, bv_ref, z_ref, fold_ref, x_sem, b_sem, z_sem, out_sem
):
    parts = x_ref.shape[0] // WIDE
    z_loads, x_loads, b_loads = [], [], []
    for k, source in enumerate((z1_ref, z2_ref, z3_ref)):
        z_loads.append(pltpu.make_async_copy(source, z_ref.at[k], z_sem.at[k]))
    for k in range(parts):
        rows = pl.ds(k * WIDE, WIDE)
        x_loads.append(pltpu.make_async_copy(x_ref.at[rows, :], xv_ref.at[rows, :], x_sem.at[k]))
        b_loads.append(pltpu.make_async_copy(b_ref.at[:, rows], bv_ref.at[:, rows], b_sem.at[k]))
    z_loads[0].start()
    for k in range(parts):
        x_loads[k].start()
        b_loads[k].start()
    z_loads[1].start()
    z_loads[2].start()
    parity = lax.rem(lax.axis_index("leaf"), 2)
    halves = (parity, 1 - parity)
    stores = []
    for k, out_ref in enumerate((odd_ref, even_ref)):
        rows = pl.ds(pl.multiple_of(halves[k] * LEAF, LEAF), LEAF)
        stores.append(
            pltpu.make_async_copy(x_ref.at[rows, :], out_ref.at[pl.ds(0, LEAF), :], out_sem.at[k])
        )
    for store in stores:
        store.start()
    z_loads[0].wait()
    z1 = z_ref[0]
    row = right_row(z1)
    total = jnp.zeros((RHS, SKEL), f32)
    for k in range(parts):
        rows = slice(k * WIDE, (k + 1) * WIDE)
        x_loads[k].wait()
        part = xv_ref[rows, :]
        high, low = split(gauss(part, left_column(part), z1, row))
        gh_ref[rows, :] = high
        gl_ref[rows, :] = low
        b_loads[k].wait()
        total += up_dot(bv_ref[:, rows], high, low)
    for half in range(2):
        for k in range(STEPS):
            fold_ref[half, k * RHS : (k + 1) * RHS, :] = bv_ref[
                :, half * LEAF + k * ROWS : half * LEAF + (k + 1) * ROWS
            ].astype(bf16)
    for k, out_ref in enumerate((odd_ref, even_ref)):
        stores.append(
            pltpu.make_async_copy(
                fold_ref.at[halves[k]], out_ref.at[pl.ds(LEAF, STEPS * RHS), :], out_sem.at[2 + k]
            )
        )
    for store in stores[2:]:
        store.start()
    value = (total * (1.0 / LEAF)).astype(bf16)
    for k in range(sent_ref.shape[0]):
        sent_ref[k] = value
    z_loads[1].wait()
    z_loads[2].wait()
    z2, z3 = z_ref[1], z_ref[2]
    t1_ref[...] = gauss(z1, left_column(z1), z2, right_row(z2))
    t2_ref[...] = gauss(z2, left_column(z2), z3, right_row(z3))
    for store in stores:
        store.wait()


def start_call(points, field, z1, z2, z3, peers):
    count = points.shape[0]
    parts = count // WIDE
    return pl.pallas_call(
        start_kernel,
        in_specs=outside(5),
        out_specs=tuple(inside(5) + outside(2)),
        out_shape=(
            shape_of((peers, RHS, SKEL), bf16),
            shape_of((count, SKEL), bf16),
            shape_of((count, SKEL), bf16),
            shape_of((SKEL, SKEL), f32),
            shape_of((SKEL, SKEL), f32),
            shape_of((LEAF + STEPS * RHS, DIM), bf16),
            shape_of((LEAF + STEPS * RHS, DIM), bf16),
        ),
        scratch_shapes=[
            pltpu.VMEM((count, DIM), bf16),
            pltpu.VMEM((RHS, count), f32),
            pltpu.VMEM((3, SKEL, DIM), bf16),
            pltpu.VMEM((2, STEPS * RHS, ROWS), bf16),
            pltpu.SemaphoreType.DMA((parts,)),
            pltpu.SemaphoreType.DMA((parts,)),
            pltpu.SemaphoreType.DMA((3,)),
            pltpu.SemaphoreType.DMA((4,)),
        ],
        compiler_params=params,
        cost_estimate=cost(600_000_000, 5_000_000, 655_360),
        name="start",
    )(*(in_hbm(value) for value in (points, field, z1, z2, z3)))


def smem():
    return pl.BlockSpec(memory_space=pltpu.SMEM)


def anywhere():
    return pl.BlockSpec(memory_space=pl.ANY)


def inside(count):
    return [pl.BlockSpec(memory_space=pltpu.VMEM)] * count


def listed(nb_ref, ct_ref, position, target):
    found = 0.0
    for k in range(nb_ref.shape[1]):
        hit = (k < ct_ref[position]) & (nb_ref[position, k] == target)
        found = found + jnp.where(hit, 1.0, 0.0)
    return found


def first_leaf_of():
    return lax.axis_index(ALL) * 2


def weight_of(w_ref, k):
    return w_ref[k : k + 1, 0:1]


def block(k):
    return slice(k * ROWS, (k + 1) * ROWS)


def make_symmetric(points, row, table_ref):
    for i in range(STEPS):
        rows = points[block(i), :]
        rest = slice(i * ROWS, LEAF)
        table_ref[block(i), rest] = gauss(
            rows, left_column(rows), points[rest, :], row[:, rest]
        ).astype(bf16)


def dot_symmetric(field, table_ref):
    out = [None] * STEPS

    def add(k, value):
        out[k] = value if out[k] is None else out[k] + value

    for i in range(STEPS):
        straight = nn(field[:, block(i)], table_ref[block(i), i * ROWS : LEAF])
        for j in range(i, STEPS):
            add(j, straight[:, block(j - i)])
        if i + 1 < STEPS:
            after = slice((i + 1) * ROWS, LEAF)
            add(i, nt(field[:, after], table_ref[block(i), after]))
    return jnp.concatenate(out, axis=1)


def make_block(left, points, row, table_ref):
    for i in range(STEPS):
        rows = left[block(i), :]
        table_ref[block(i), :] = gauss(rows, left_column(rows), points, row).astype(bf16)


def tables_a_kernel(
    nb_ref, ct_ref, x_ref, b_ref, after_ref,
    table_ref, own_ref, row_ref, w_ref, xv_ref, bv_ref, x_sem, b_sem
):
    del after_ref
    x_loads, b_loads = [], []
    for k in range(2):
        part = pl.ds(k * LEAF, LEAF)
        x_loads.append(pltpu.make_async_copy(x_ref.at[part, :], xv_ref.at[part, :], x_sem.at[k]))
        b_loads.append(pltpu.make_async_copy(b_ref.at[:, part], bv_ref.at[:, part], b_sem.at[k]))
    for load in (x_loads[0], b_loads[0], x_loads[1], b_loads[1]):
        load.start()
    first = first_leaf_of()
    weights = (
        listed(nb_ref, ct_ref, 0, first - 1),
        listed(nb_ref, ct_ref, 0, first + 1),
        listed(nb_ref, ct_ref, 1, first),
        listed(nb_ref, ct_ref, 1, first + 2),
    )
    place = lax.broadcasted_iota(jnp.int32, (8, 128), 0)
    spread = jnp.zeros((8, 128), f32)
    for k in range(4):
        spread = jnp.where(place == k, weights[k], spread)
    w_ref[...] = spread
    x_loads[0].wait()
    x_a = xv_ref[:LEAF, :]
    row_ref[:, :LEAF] = right_row(x_a)
    make_symmetric(x_a, row_ref[:, :LEAF], table_ref)
    b_loads[0].wait()
    own_ref[...] = dot_symmetric(bv_ref[:, :LEAF].astype(bf16), table_ref)
    x_loads[1].wait()
    row_ref[:, LEAF:] = right_row(xv_ref[LEAF:, :])
    b_loads[1].wait()


def tables_a_call(neighbors, counts, points, field, after):
    count = points.shape[0]
    return pl.pallas_call(
        tables_a_kernel,
        in_specs=[smem(), smem()] + outside(2) + [anywhere()],
        out_shape=(
            shape_of((LEAF, LEAF), bf16),
            shape_of((RHS, LEAF), f32),
            shape_of((1, 2 * LEAF), f32),
            shape_of((8, 128), f32),
            shape_of((count, DIM), bf16),
            shape_of((RHS, count), f32),
        ),
        scratch_shapes=[pltpu.SemaphoreType.DMA((2,)), pltpu.SemaphoreType.DMA((2,))],
        compiler_params=params,
        cost_estimate=cost(700_000_000, 5_000_000, 700_000),
        name="tables_a",
    )(neighbors, counts, in_hbm(points), in_hbm(field), after)


def tables_b_kernel(
    w_ref, x_ref, b_ref, row_ref, own_a_ref, after_ref, table_b_ref, table_ab_ref, own_ref
):
    del after_ref
    x_a, x_b = x_ref[:LEAF, :], x_ref[LEAF:, :]
    make_symmetric(x_b, row_ref[:, LEAF:], table_b_ref)
    make_block(x_a, x_b, row_ref[:, LEAF:], table_ab_ref)
    b_a, b_b = b_ref[:, :LEAF].astype(bf16), b_ref[:, LEAF:].astype(bf16)
    own_ref[:, :LEAF] = own_a_ref[...] + weight_of(w_ref, 1) * nt(b_b, table_ab_ref[...])
    own_ref[:, LEAF:] = dot_symmetric(b_b, table_b_ref) + weight_of(w_ref, 2) * nn(
        b_a, table_ab_ref[...]
    )


def tables_b_call(w, points, field, row, own_a, after):
    return pl.pallas_call(
        tables_b_kernel,
        in_specs=inside(5) + [anywhere()],
        out_shape=(
            shape_of((LEAF, LEAF), bf16),
            shape_of((LEAF, LEAF), bf16),
            shape_of((RHS, 2 * LEAF), f32),
        ),
        compiler_params=params,
        cost_estimate=cost(1_500_000_000, 7_000_000, 1_800_000),
        name="tables_b",
    )(w, points, field, row, own_a, after)


def unfold(halo):
    parts = [halo[LEAF + k * RHS : LEAF + (k + 1) * RHS, :] for k in range(STEPS)]
    return jnp.concatenate(parts, axis=1)


def in_order(odd_ref, even_ref):
    even = even_leaf()
    odd_got, even_got = odd_ref[...], even_ref[...]
    return jnp.where(even, odd_got, even_got), jnp.where(even, even_got, odd_got)


def around_kernel(
    w_ref, odd_ref, even_ref, x_ref, row_ref, own_ref, after_ref,
    below_table_ref, above_table_ref, out_ref
):
    del after_ref

    def build(below_ref, above_ref):
        make_block(below_ref, x_ref[:LEAF, :], row_ref[:, :LEAF], below_table_ref)
        out_ref[:, :LEAF] = own_ref[:, :LEAF] + weight_of(w_ref, 0) * nn(
            unfold(below_ref), below_table_ref[...]
        )
        make_block(above_ref, x_ref[LEAF:, :], row_ref[:, LEAF:], above_table_ref)
        out_ref[:, LEAF:] = own_ref[:, LEAF:] + weight_of(w_ref, 3) * nn(
            unfold(above_ref), above_table_ref[...]
        )

    even = even_leaf()

    @pl.when(even)
    def _():
        build(odd_ref, even_ref)

    @pl.when(jnp.logical_not(even))
    def _():
        build(even_ref, odd_ref)


def around_call(w, odd, even, points, row, own, after):
    return pl.pallas_call(
        around_kernel,
        in_specs=inside(6) + [anywhere()],
        out_shape=(
            shape_of((LEAF, LEAF), bf16),
            shape_of((LEAF, LEAF), bf16),
            shape_of((RHS, 2 * LEAF), f32),
        ),
        compiler_params=params,
        cost_estimate=cost(1_400_000_000, 7_000_000, 2_097_152),
        name="around",
    )(w, odd, even, points, row, own, after)


def total_of(got_ref):
    total = got_ref[0].astype(f32)
    for k in range(1, got_ref.shape[0]):
        total += got_ref[k].astype(f32)
    return total


def climb_kernel(got_ref, table_ref, up_ref, sent_ref):
    total = total_of(got_ref)
    up_ref[...] = total
    sent_ref[...] = (nn(total, table_ref[...], highest) * (1.0 / SKEL)).astype(bf16)


def climb_call(got, table):
    return pl.pallas_call(
        climb_kernel,
        in_specs=inside(2),
        out_shape=(shape_of((RHS, SKEL), f32), shape_of((RHS, SKEL), bf16)),
        compiler_params=params,
        cost_estimate=cost(50_000_000, 900_000),
        name="climb",
    )(got, table)


def join_kernel(left_ref, right_ref, after_ref, out_ref):
    del after_ref
    out_ref[...] = (left_ref[...].astype(f32) + right_ref[...].astype(f32)).astype(bf16)


def join_call(left, right, after):
    return pl.pallas_call(
        join_kernel,
        in_specs=inside(2) + [anywhere()],
        out_shape=shape_of((RHS, SKEL), bf16),
        compiler_params=params,
        cost_estimate=cost(100_000, 100_000),
        name="join",
    )(left, right, after)


def climb_four_kernel(g0_ref, g1_ref, g2_ref, g3_ref, table_ref, after_ref, up_ref, sent_ref):
    del after_ref
    total = sum_of((g0_ref, g1_ref, g2_ref, g3_ref))
    up_ref[...] = total
    sent_ref[...] = (nn(total, table_ref[...], highest) * (1.0 / SKEL)).astype(bf16)


def climb_four_call(parts, table, after):
    return pl.pallas_call(
        climb_four_kernel,
        in_specs=inside(5) + [anywhere()],
        out_shape=(shape_of((RHS, SKEL), f32), shape_of((RHS, SKEL), bf16)),
        compiler_params=params,
        cost_estimate=cost(50_000_000, 900_000),
        name="climb_four",
    )(*parts, table, after)


def sum_of(refs):
    total = refs[0][...].astype(f32)
    for ref in refs[1:]:
        total += ref[...].astype(f32)
    return total


def down_weights(up_one, up_two, up_top, low_table, high_table):
    down_top = level_top * up_top
    down_two = level_two * up_two + nt(down_top, high_table, highest) * (1.0 / SKEL)
    return level_one * up_one + nt(down_two, low_table, highest) * (1.0 / SKEL)


def second_kernel(
    g0_ref, g1_ref, g2_ref, g3_ref, p1_ref, p2_ref, t1_ref, t2_ref, gh_ref, gl_ref, own_ref,
    u_ref, u16_ref, odd_ref, even_ref
):
    top = sum_of((g0_ref, g1_ref, g2_ref, g3_ref))
    weights = down_weights(p1_ref[...], p2_ref[...], top, t1_ref[...], t2_ref[...])
    for k in range(2):
        part = slice(k * LEAF, (k + 1) * LEAF)
        far = down_dot(weights, gh_ref[part, :], gl_ref[part, :])
        value = (own_ref[:, part] + far) * (1.0 / LEAF)
        u_ref[:, part] = value
        u16_ref[:, part] = value.astype(bf16)
    even = even_leaf()

    @pl.when(even)
    def _():
        odd_ref[...] = u16_ref[:, :LEAF]
        even_ref[...] = u16_ref[:, LEAF:]

    @pl.when(jnp.logical_not(even))
    def _():
        odd_ref[...] = u16_ref[:, LEAF:]
        even_ref[...] = u16_ref[:, :LEAF]


def second_call(parts, p1, p2, t1, t2, gh, gl, own):
    return pl.pallas_call(
        second_kernel,
        in_specs=inside(11),
        out_shape=(
            shape_of((RHS, 2 * LEAF), f32),
            shape_of((RHS, 2 * LEAF), bf16),
            shape_of((RHS, LEAF), bf16),
            shape_of((RHS, LEAF), bf16),
        ),
        compiler_params=params,
        cost_estimate=cost(250_000_000, 5_000_000),
        name="second",
    )(*parts, p1, p2, t1, t2, gh, gl, own)


def row_sum(value):
    return jnp.sum(value, axis=1, keepdims=True)


def third_kernel(
    w_ref, u_ref, b_ref, u16_ref, table_a_ref, table_b_ref, table_ab_ref,
    gh_ref, gl_ref, out_ref, up_ref, sums_ref
):
    up_ref[...] = up_dot(u_ref[...], gh_ref[...], gl_ref[...])
    u_a, u_b = u16_ref[:, :LEAF], u16_ref[:, LEAF:]
    out_ref[:, :LEAF] = dot_symmetric(u_a, table_a_ref) + weight_of(w_ref, 1) * nt(
        u_b, table_ab_ref[...]
    )
    out_ref[:, LEAF:] = dot_symmetric(u_b, table_b_ref) + weight_of(w_ref, 2) * nn(
        u_a, table_ab_ref[...]
    )
    b, u = b_ref[...], u_ref[...]
    lane = lax.broadcasted_iota(jnp.int32, (RHS, 128), 1)
    sums = (row_sum(b * b), row_sum(b * u), row_sum(u * u))
    total = jnp.zeros((RHS, 128), f32)
    for k in range(3):
        total = jnp.where(lane == k, sums[k], total)
    sums_ref[...] = total


def third_call(w, u, field, u16, table_a, table_b, table_ab, gh, gl):
    return pl.pallas_call(
        third_kernel,
        in_specs=inside(9),
        out_shape=(
            shape_of((RHS, 2 * LEAF), f32),
            shape_of((RHS, SKEL), f32),
            shape_of((RHS, 128), f32),
        ),
        compiler_params=params,
        cost_estimate=cost(700_000_000, 10_000_000),
        name="third",
    )(w, u, field, u16, table_a, table_b, table_ab, gh, gl)


def rows_of(sums):
    high = sums.astype(bf16).astype(f32)
    rest = sums - high
    middle = rest.astype(bf16).astype(f32)
    low = rest - middle
    lane = lax.broadcasted_iota(jnp.int32, (RHS, 128), 1)
    packed = jnp.where(lane < 4, high, 0.0)
    packed += jnp.where((lane >= 4) & (lane < 8), pltpu.roll(middle, 4, 1), 0.0)
    packed += jnp.where((lane >= 8) & (lane < 12), pltpu.roll(low, 8, 1), 0.0)
    turned = packed.T[:16]
    return jnp.concatenate([turned, jnp.zeros((16, SKEL - RHS), f32)], axis=1)


def sums_of(rows):
    turned = jnp.concatenate([rows[:, :RHS], jnp.zeros((112, RHS), f32)], axis=0).T
    total = turned + (pltpu.roll(turned, 124, 1) + pltpu.roll(turned, 120, 1))
    lane = lax.broadcasted_iota(jnp.int32, (RHS, 128), 1)
    return jnp.where(lane < 4, total, 0.0)


def put_all(sent_ref, value, sums):
    message = jnp.concatenate([value, rows_of(sums)], axis=0).astype(bf16)
    if len(sent_ref.shape) == 2:
        sent_ref[...] = message
    else:
        for k in range(sent_ref.shape[0]):
            sent_ref[k] = message


def add_last(sums, column):
    lane = lax.broadcasted_iota(jnp.int32, (RHS, 128), 1)
    return sums + jnp.where(lane == 3, column, 0.0)


def finish_kernel(
    w_ref, odd_ref, even_ref, below_table_ref, above_table_ref, u_ref, own_ref, up_ref,
    sums_ref, sent_ref, out_ref
):
    below, above = in_order(odd_ref, even_ref)
    near_a = own_ref[:, :LEAF] + weight_of(w_ref, 0) * nn(below, below_table_ref[...])
    near_b = own_ref[:, LEAF:] + weight_of(w_ref, 3) * nn(above, above_table_ref[...])
    out_ref[:, :LEAF] = near_a
    out_ref[:, LEAF:] = near_b
    bend = row_sum(u_ref[:, :LEAF] * near_a) + row_sum(u_ref[:, LEAF:] * near_b)
    put_all(sent_ref, up_ref[...] * (1.0 / LEAF), add_last(sums_ref[...], bend * (1.0 / LEAF)))


def finish_call(w, odd, even, below_table, above_table, u, own, up, sums, peers):
    return pl.pallas_call(
        finish_kernel,
        in_specs=inside(9),
        out_shape=(
            shape_of((peers, RHS + 16, SKEL), bf16),
            shape_of((RHS, 2 * LEAF), f32),
        ),
        compiler_params=params,
        cost_estimate=cost(270_000_000, 4_000_000),
        name="finish",
    )(w, odd, even, below_table, above_table, u, own, up, sums)


def climb_sums(level, total, table_ref, up_ref, sent_ref):
    up = total[:RHS]
    up_ref[...] = up
    sums = add_last(sums_of(total[RHS:]), level * row_sum(up * up))
    put_all(sent_ref, nn(up, table_ref[...], highest) * (1.0 / SKEL), sums)


def climb_sums_kernel(level, got_ref, table_ref, up_ref, sent_ref):
    climb_sums(level, total_of(got_ref), table_ref, up_ref, sent_ref)


def climb_sums_four_kernel(level, g0_ref, g1_ref, g2_ref, g3_ref, table_ref, up_ref, sent_ref):
    climb_sums(level, sum_of((g0_ref, g1_ref, g2_ref, g3_ref)), table_ref, up_ref, sent_ref)


def climb_sums_call(got, table, level):
    several = isinstance(got, list)
    kernel = climb_sums_four_kernel if several else climb_sums_kernel
    inputs = got if several else [got]
    return pl.pallas_call(
        lambda *refs: kernel(level, *refs),
        in_specs=inside(len(inputs) + 1),
        out_shape=(shape_of((RHS, SKEL), f32), shape_of((RHS + 16, SKEL), bf16)),
        compiler_params=params,
        cost_estimate=cost(50_000_000, 900_000),
        name="climb_sums",
    )(*inputs, table)


def join_sums_kernel(left_ref, right_ref, out_ref):
    total = sum_of((left_ref, right_ref))
    put_all(out_ref, total[:RHS], sums_of(total[RHS:]))


def join_sums_call(left, right):
    return pl.pallas_call(
        join_sums_kernel,
        in_specs=inside(2),
        out_shape=shape_of((RHS + 16, SKEL), bf16),
        compiler_params=params,
        cost_estimate=cost(100_000, 100_000),
        name="join_sums",
    )(left, right)


def last_kernel(
    g0_ref, g1_ref, g2_ref, g3_ref, p1_ref, p2_ref, t1_ref, t2_ref, gh_ref, gl_ref, near_ref,
    b_ref, u_ref, x_ref, r_ref, xv_ref, rv_ref, x_sem, r_sem
):
    total = sum_of((g0_ref, g1_ref, g2_ref, g3_ref))
    top = total[:RHS]
    weights = down_weights(p1_ref[...], p2_ref[...], top, t1_ref[...], t2_ref[...])
    sums = add_last(sums_of(total[RHS:]), level_top * row_sum(top * top))
    bb, bu, uu, uv = sums[:, 0:1], sums[:, 1:2], sums[:, 2:3], sums[:, 3:4]
    step_one = bb / (ridge_term * bb + bu)
    ratio = bu / bb
    norm_one = step_one * step_one * (uu - ratio * bu)
    beta = norm_one / bb
    bend_rr = step_one * step_one * (ratio * ratio * bu - 2.0 * ratio * uu + uv)
    bend_rb = step_one * (ratio * bu - uu)
    bending = (
        ridge_term * (norm_one + beta * beta * bb)
        + bend_rr
        + 2.0 * beta * bend_rb
        + beta * beta * bu
    )
    step_two = norm_one / bending
    stores = []
    for k in range(4):
        part = slice(k * WIDE, (k + 1) * WIDE)
        far = down_dot(weights, gh_ref[part, :], gl_ref[part, :])
        third = (near_ref[:, part] + far) * (1.0 / LEAF)
        first, second = b_ref[:, part], u_ref[:, part]
        residual_one = (step_one * ratio) * first - step_one * second
        direction = residual_one + beta * first
        applied = (
            ridge_term * direction + (step_one * ratio + beta) * second - step_one * third
        )
        xv_ref[:, part] = step_one * first + step_two * direction
        rv_ref[:, part] = residual_one - step_two * applied
        place = pl.ds(k * WIDE, WIDE)
        for store in (
            pltpu.make_async_copy(xv_ref.at[:, place], x_ref.at[:, place], x_sem.at[k]),
            pltpu.make_async_copy(rv_ref.at[:, place], r_ref.at[:, place], r_sem.at[k]),
        ):
            store.start()
            stores.append(store)
    for store in stores:
        store.wait()


def last_call(parts, p1, p2, t1, t2, gh, gl, near, field, u):
    return pl.pallas_call(
        last_kernel,
        in_specs=inside(13),
        out_specs=tuple(outside(2)),
        out_shape=(shape_of((RHS, 2 * LEAF), f32), shape_of((RHS, 2 * LEAF), f32)),
        scratch_shapes=[
            pltpu.VMEM((RHS, 2 * LEAF), f32),
            pltpu.VMEM((RHS, 2 * LEAF), f32),
            pltpu.SemaphoreType.DMA((4,)),
            pltpu.SemaphoreType.DMA((4,)),
        ],
        compiler_params=params,
        cost_estimate=cost(250_000_000, 7_000_000),
        name="last",
    )(*parts, p1, p2, t1, t2, gh, gl, near, field, u)


def exchange(sent, axis):
    return lax.all_to_all(sent, axis, 0, 0)


def chain_swap(value, first):
    count = lax.axis_size(ALL)
    pairs = [(i, i + 1) for i in range(first, count - 1, 2)]
    return lax.ppermute(value, ALL, pairs + [(j, i) for i, j in pairs])


def swap_both(odd, even):
    return chain_swap(odd, 1), chain_swap(even, 0)


def turned(value, axis, shift):
    count = lax.axis_size(axis)
    return lax.ppermute(value, axis, [(i, (i + shift) % count) for i in range(count)])


def turns(value, axis, stride):
    return [value] + [turned(value, axis, k) for k in range(stride, lax.axis_size(axis), stride)]


def swapped(value, axis):
    count = lax.axis_size(axis)
    return lax.ppermute(value, axis, [(i, i ^ 1) for i in range(count)])


def shards(points, right_side, skel_sub, skel_group, skel_top, neighbors, counts):
    leaves = lax.axis_size("leaf")
    sent, gh, gl, t1, t2, odd, even = start_call(
        points, right_side, skel_sub, skel_group, skel_top, leaves
    )
    odd, even = swap_both(odd, even)
    up_one, sent = climb_call(exchange(sent, "leaf"), t1)
    other = swapped(sent, "sub")
    table_a, own_a, row, w, x, b = tables_a_call(neighbors, counts, points, right_side, sent)
    sent = join_call(sent, other, w)
    parts = turns(sent, "sub", 2)
    table_b, table_ab, own = tables_b_call(w, x, b, row, own_a, sent)
    up_two, sent = climb_four_call(parts, t2, own)
    parts = turns(sent, "group", 1)
    below_table, above_table, own = around_call(w, odd, even, x, row, own, sent)
    u, u16, odd, even = second_call(parts, up_one, up_two, t1, t2, gh, gl, own)

    odd, even = swap_both(odd, even)
    own, weights, sums = third_call(w, u, b, u16, table_a, table_b, table_ab, gh, gl)
    sent, near = finish_call(
        w, odd, even, below_table, above_table, u, own, weights, sums, leaves
    )
    up_one, sent = climb_sums_call(exchange(sent, "leaf"), t1, level_one)
    sent = join_sums_call(sent, swapped(sent, "sub"))
    up_two, sent = climb_sums_call(turns(sent, "sub", 2), t2, level_two)
    parts = turns(sent, "group", 1)
    return last_call(parts, up_one, up_two, t1, t2, gh, gl, near, b, u)


def solution(mesh):
    return jax.shard_map(
        shards,
        mesh=mesh,
        in_specs=(
            P(ALL, None),
            P(None, ALL),
            P(("group", "sub"), None),
            P("group", None),
            P(),
            P(ALL, None),
            P(ALL),
        ),
        out_specs=(P(None, ALL), P(None, ALL)),
        check_vma=False,
    )
```

```python
import math

import jax
import jax.numpy as jnp
from jax import lax
from jax.experimental import pallas as pl
from jax.experimental.pallas import tpu as pltpu
from jax.sharding import PartitionSpec as P

LEAF = 1024
SKEL = 256
RHS = 64
DIM = 256
ROWS = 256
STEPS = LEAF // ROWS
WIDE = 512
ALL = ("group", "sub", "leaf")

ridge_term = 3.0
level_one = 0.5
level_two = 0.25
level_top = 0.3

bf16 = jnp.bfloat16
f32 = jnp.float32
per_unit = 0.25 / DIM * math.log2(math.e)
vmem_bytes = 20 * 1024 * 1024


def shape_of(shape, dtype):
    return jax.ShapeDtypeStruct(shape, dtype)


def cost(flops, moved, exps=0):
    return pl.CostEstimate(flops=flops, bytes_accessed=moved, transcendentals=exps)


params = pltpu.CompilerParams(vmem_limit_bytes=vmem_bytes)


def nn(left, right, precision=None):
    return lax.dot_general(
        left, right, (((1,), (0,)), ((), ())), precision=precision, preferred_element_type=f32
    )


def nt(left, right, precision=None):
    return lax.dot_general(
        left, right, (((1,), (1,)), ((), ())), precision=precision, preferred_element_type=f32
    )


highest = lax.Precision.HIGHEST


def squares(rows):
    wide = rows.astype(f32)
    return wide * wide


def left_column(rows):
    return jnp.sum(squares(rows), axis=1, keepdims=True) * per_unit


def right_row(rows):
    square = squares(rows)
    high = square.astype(bf16)
    low = (square - high.astype(f32)).astype(bf16)
    ones = jnp.ones((8, rows.shape[1]), bf16)
    return (nt(ones, high) + nt(ones, low))[0:1] * per_unit


def gauss(left, column, right, row):
    return jnp.exp2(nt(left, right) * (2.0 * per_unit) - column - row)


def split(value):
    high = value.astype(bf16)
    low = (value - high.astype(f32)).astype(bf16)
    return high, low


def up_dot(field, table):
    both = nn(jnp.concatenate(split(field), axis=0), table)
    return both[:RHS] + both[RHS:]


def down_dot(weights, table):
    both = nt(jnp.concatenate(split(weights), axis=0), table)
    return both[:RHS] + both[RHS:]


def even_leaf():
    return lax.rem(lax.axis_index("leaf"), 2) == 0


def in_hbm(value):
    return pltpu.with_memory_space_constraint(value, pltpu.HBM)


def outside(count):
    return [pl.BlockSpec(memory_space=pltpu.HBM)] * count


def start_kernel(
    x_ref, b_ref, z1_ref, z2_ref,
    sent_ref, g_ref, t1_ref, xv_ref, bv_ref, gv_ref, z_ref, x_sem, b_sem, z_sem, g_sem
):
    parts = x_ref.shape[0] // WIDE
    z_loads, x_loads, b_loads = [], [], []
    for k, source in enumerate((z1_ref, z2_ref)):
        z_loads.append(pltpu.make_async_copy(source, z_ref.at[k], z_sem.at[k]))
    for k in range(parts):
        rows = pl.ds(k * WIDE, WIDE)
        x_loads.append(pltpu.make_async_copy(x_ref.at[rows, :], xv_ref.at[rows, :], x_sem.at[k]))
        b_loads.append(pltpu.make_async_copy(b_ref.at[:, rows], bv_ref.at[:, rows], b_sem.at[k]))
    z_loads[0].start()
    for k in range(parts):
        x_loads[k].start()
        b_loads[k].start()
    z_loads[1].start()
    stores = []
    z_loads[0].wait()
    z1 = z_ref[0]
    row = right_row(z1)
    total = jnp.zeros((RHS, SKEL), f32)
    for k in range(parts):
        rows = slice(k * WIDE, (k + 1) * WIDE)
        x_loads[k].wait()
        part = xv_ref[rows, :]
        table = gauss(part, left_column(part), z1, row).astype(bf16)
        gv_ref[rows, :] = table
        place = pl.ds(k * WIDE, WIDE)
        store = pltpu.make_async_copy(gv_ref.at[place, :], g_ref.at[place, :], g_sem.at[k])
        store.start()
        stores.append(store)
        b_loads[k].wait()
        total += up_dot(bv_ref[:, rows], table)
    value = (total * (1.0 / LEAF)).astype(bf16)
    for k in range(sent_ref.shape[0]):
        sent_ref[k] = value
    z_loads[1].wait()
    z2 = z_ref[1]
    t1_ref[...] = gauss(z1, left_column(z1), z2, right_row(z2))
    for store in stores:
        store.wait()


def start_call(points, field, z1, z2, peers):
    count = points.shape[0]
    parts = count // WIDE
    return pl.pallas_call(
        start_kernel,
        in_specs=outside(4),
        out_specs=tuple(inside(1) + outside(1) + inside(3)),
        out_shape=(
            shape_of((peers, RHS, SKEL), bf16),
            pltpu.HBM((count, SKEL), bf16),
            shape_of((SKEL, SKEL), f32),
            shape_of((count, DIM), bf16),
            shape_of((RHS, count), f32),
        ),
        scratch_shapes=[
            pltpu.VMEM((count, SKEL), bf16),
            pltpu.VMEM((2, SKEL, DIM), bf16),
            pltpu.SemaphoreType.DMA((parts,)),
            pltpu.SemaphoreType.DMA((parts,)),
            pltpu.SemaphoreType.DMA((2,)),
            pltpu.SemaphoreType.DMA((parts,)),
        ],
        compiler_params=params,
        cost_estimate=cost(600_000_000, 5_000_000, 655_360),
        name="start",
    )(*(in_hbm(value) for value in (points, field, z1, z2)))


def pack_kernel(x_ref, b_ref, odd_ref, even_ref, fold_ref, out_sem):
    parity = lax.rem(lax.axis_index("leaf"), 2)
    halves = (parity, 1 - parity)
    stores = []
    for k, out_ref in enumerate((odd_ref, even_ref)):
        rows = pl.ds(pl.multiple_of(halves[k] * LEAF, LEAF), LEAF)
        stores.append(
            pltpu.make_async_copy(x_ref.at[rows, :], out_ref.at[pl.ds(0, LEAF), :], out_sem.at[k])
        )
    for store in stores:
        store.start()
    for half in range(2):
        for k in range(STEPS):
            fold_ref[half, k * RHS : (k + 1) * RHS, :] = b_ref[
                :, half * LEAF + k * ROWS : half * LEAF + (k + 1) * ROWS
            ].astype(bf16)
    for k, out_ref in enumerate((odd_ref, even_ref)):
        stores.append(
            pltpu.make_async_copy(
                fold_ref.at[halves[k]], out_ref.at[pl.ds(LEAF, STEPS * RHS), :], out_sem.at[2 + k]
            )
        )
    for store in stores[2:]:
        store.start()
    for store in stores:
        store.wait()


def pack_call(points, field):
    return pl.pallas_call(
        pack_kernel,
        in_specs=inside(2),
        out_specs=tuple(outside(2)),
        out_shape=(
            pltpu.HBM((LEAF + STEPS * RHS, DIM), bf16),
            pltpu.HBM((LEAF + STEPS * RHS, DIM), bf16),
        ),
        scratch_shapes=[
            pltpu.VMEM((2, STEPS * RHS, ROWS), bf16),
            pltpu.SemaphoreType.DMA((4,)),
        ],
        compiler_params=params,
        cost_estimate=cost(1_000_000, 5_000_000),
        name="pack",
    )(points, field)


def smem():
    return pl.BlockSpec(memory_space=pltpu.SMEM)


def anywhere():
    return pl.BlockSpec(memory_space=pl.ANY)


def inside(count):
    return [pl.BlockSpec(memory_space=pltpu.VMEM)] * count


def listed(nb_ref, ct_ref, position, target):
    found = 0.0
    for k in range(nb_ref.shape[1]):
        hit = (k < ct_ref[position]) & (nb_ref[position, k] == target)
        found = found + jnp.where(hit, 1.0, 0.0)
    return found


def first_leaf_of():
    return lax.axis_index(ALL) * 2


def weight_of(w_ref, k):
    return w_ref[k : k + 1, 0:1]


def block(k):
    return slice(k * ROWS, (k + 1) * ROWS)


def make_symmetric(points, row, table_ref):
    for i in range(STEPS):
        rows = points[block(i), :]
        rest = slice(i * ROWS, LEAF)
        table_ref[block(i), rest] = gauss(
            rows, left_column(rows), points[rest, :], row[:, rest]
        ).astype(bf16)


def dot_symmetric(field, table_ref):
    out = [None] * STEPS

    def add(k, value):
        out[k] = value if out[k] is None else out[k] + value

    for i in range(STEPS):
        straight = nn(field[:, block(i)], table_ref[block(i), i * ROWS : LEAF])
        for j in range(i, STEPS):
            add(j, straight[:, block(j - i)])
        if i + 1 < STEPS:
            after = slice((i + 1) * ROWS, LEAF)
            add(i, nt(field[:, after], table_ref[block(i), after]))
    return jnp.concatenate(out, axis=1)


def make_block(left, points, row, table_ref):
    for i in range(STEPS):
        rows = left[block(i), :]
        table_ref[block(i), :] = gauss(rows, left_column(rows), points, row).astype(bf16)


def prepare_kernel(
    nb_ref, ct_ref, x_ref, z2_ref, z3_ref, after_ref, row_ref, w_ref, t2_ref, z_ref, z_sem
):
    del after_ref
    loads = []
    for k, source in enumerate((z2_ref, z3_ref)):
        loads.append(pltpu.make_async_copy(source, z_ref.at[k], z_sem.at[k]))
        loads[k].start()
    first = first_leaf_of()
    weights = (
        listed(nb_ref, ct_ref, 0, first - 1),
        listed(nb_ref, ct_ref, 0, first + 1),
        listed(nb_ref, ct_ref, 1, first),
        listed(nb_ref, ct_ref, 1, first + 2),
    )
    place = lax.broadcasted_iota(jnp.int32, (8, 128), 0)
    spread = jnp.zeros((8, 128), f32)
    for k in range(4):
        spread = jnp.where(place == k, weights[k], spread)
    w_ref[...] = spread
    row_ref[...] = right_row(x_ref[...])
    for load in loads:
        load.wait()
    z2, z3 = z_ref[0], z_ref[1]
    t2_ref[...] = gauss(z2, left_column(z2), z3, right_row(z3))


def prepare_call(neighbors, counts, points, z2, z3, after):
    return pl.pallas_call(
        prepare_kernel,
        in_specs=[smem(), smem()] + inside(1) + outside(2) + [anywhere()],
        out_shape=(
            shape_of((1, 2 * LEAF), f32),
            shape_of((8, 128), f32),
            shape_of((SKEL, SKEL), f32),
        ),
        scratch_shapes=[pltpu.VMEM((2, SKEL, DIM), bf16), pltpu.SemaphoreType.DMA((2,))],
        compiler_params=params,
        cost_estimate=cost(50_000_000, 2_000_000, 65_536),
        name="prepare",
    )(neighbors, counts, points, in_hbm(z2), in_hbm(z3), after)


def tables_kernel(x_ref, b_ref, row_ref, after_ref, table_a_ref, table_b_ref, own_ref):
    del after_ref
    make_symmetric(x_ref[:LEAF, :], row_ref[:, :LEAF], table_a_ref)
    make_symmetric(x_ref[LEAF:, :], row_ref[:, LEAF:], table_b_ref)
    own_ref[:, :LEAF] = dot_symmetric(b_ref[:, :LEAF].astype(bf16), table_a_ref)
    own_ref[:, LEAF:] = dot_symmetric(b_ref[:, LEAF:].astype(bf16), table_b_ref)


def tables_call(points, field, row, after):
    return pl.pallas_call(
        tables_kernel,
        in_specs=inside(3) + [anywhere()],
        out_shape=(
            shape_of((LEAF, LEAF), bf16),
            shape_of((LEAF, LEAF), bf16),
            shape_of((RHS, 2 * LEAF), f32),
        ),
        compiler_params=params,
        cost_estimate=cost(2_200_000_000, 9_000_000, 2_400_000),
        name="tables",
    )(points, field, row, after)


def unfold(halo):
    parts = [halo[LEAF + k * RHS : LEAF + (k + 1) * RHS, :] for k in range(STEPS)]
    return jnp.concatenate(parts, axis=1)


def in_order(odd_ref, even_ref):
    even = even_leaf()
    odd_got, even_got = odd_ref[...], even_ref[...]
    return jnp.where(even, odd_got, even_got), jnp.where(even, even_got, odd_got)


def around_kernel(
    w_ref, odd_ref, even_ref, x_ref, b_ref, row_ref, own_ref, after_ref,
    table_ab_ref, below_table_ref, above_table_ref, out_ref
):
    del after_ref
    x_a, x_b = x_ref[:LEAF, :], x_ref[LEAF:, :]
    row_a, row_b = row_ref[:, :LEAF], row_ref[:, LEAF:]
    b_a, b_b = b_ref[:, :LEAF].astype(bf16), b_ref[:, LEAF:].astype(bf16)
    make_block(x_a, x_b, row_b, table_ab_ref)
    near_a = own_ref[:, :LEAF] + weight_of(w_ref, 1) * nt(b_b, table_ab_ref[...])
    near_b = own_ref[:, LEAF:] + weight_of(w_ref, 2) * nn(b_a, table_ab_ref[...])

    def build(below_ref, above_ref):
        make_block(below_ref, x_a, row_a, below_table_ref)
        out_ref[:, :LEAF] = near_a + weight_of(w_ref, 0) * nn(
            unfold(below_ref), below_table_ref[...]
        )
        make_block(above_ref, x_b, row_b, above_table_ref)
        out_ref[:, LEAF:] = near_b + weight_of(w_ref, 3) * nn(
            unfold(above_ref), above_table_ref[...]
        )

    even = even_leaf()

    @pl.when(even)
    def _():
        build(odd_ref, even_ref)

    @pl.when(jnp.logical_not(even))
    def _():
        build(even_ref, odd_ref)


def around_call(w, odd, even, points, field, row, own, after):
    return pl.pallas_call(
        around_kernel,
        in_specs=inside(7) + [anywhere()],
        out_shape=(
            shape_of((LEAF, LEAF), bf16),
            shape_of((LEAF, LEAF), bf16),
            shape_of((LEAF, LEAF), bf16),
            shape_of((RHS, 2 * LEAF), f32),
        ),
        compiler_params=params,
        cost_estimate=cost(2_200_000_000, 9_000_000, 3_145_728),
        name="around",
    )(w, odd, even, points, field, row, own, after)


def total_of(got_ref):
    total = got_ref[0].astype(f32)
    for k in range(1, got_ref.shape[0]):
        total += got_ref[k].astype(f32)
    return total


def climb_kernel(got_ref, table_ref, up_ref, sent_ref):
    total = total_of(got_ref)
    up_ref[...] = total
    sent_ref[...] = (nn(total, table_ref[...], highest) * (1.0 / SKEL)).astype(bf16)


def climb_call(got, table):
    return pl.pallas_call(
        climb_kernel,
        in_specs=inside(2),
        out_shape=(shape_of((RHS, SKEL), f32), shape_of((RHS, SKEL), bf16)),
        compiler_params=params,
        cost_estimate=cost(50_000_000, 900_000),
        name="climb",
    )(got, table)


def join_kernel(left_ref, right_ref, after_ref, out_ref):
    del after_ref
    out_ref[...] = (left_ref[...].astype(f32) + right_ref[...].astype(f32)).astype(bf16)


def join_call(left, right, after):
    return pl.pallas_call(
        join_kernel,
        in_specs=inside(2) + [anywhere()],
        out_shape=shape_of((RHS, SKEL), bf16),
        compiler_params=params,
        cost_estimate=cost(100_000, 100_000),
        name="join",
    )(left, right, after)


def climb_four_kernel(g0_ref, g1_ref, g2_ref, g3_ref, table_ref, after_ref, up_ref, sent_ref):
    del after_ref
    total = sum_of((g0_ref, g1_ref, g2_ref, g3_ref))
    up_ref[...] = total
    sent_ref[...] = (nn(total, table_ref[...], highest) * (1.0 / SKEL)).astype(bf16)


def climb_four_call(parts, table, after):
    return pl.pallas_call(
        climb_four_kernel,
        in_specs=inside(5) + [anywhere()],
        out_shape=(shape_of((RHS, SKEL), f32), shape_of((RHS, SKEL), bf16)),
        compiler_params=params,
        cost_estimate=cost(50_000_000, 900_000),
        name="climb_four",
    )(*parts, table, after)


def sum_of(refs):
    total = refs[0][...].astype(f32)
    for ref in refs[1:]:
        total += ref[...].astype(f32)
    return total


def down_weights(up_one, up_two, up_top, low_table, high_table):
    down_top = level_top * up_top
    down_two = level_two * up_two + nt(down_top, high_table, highest) * (1.0 / SKEL)
    return level_one * up_one + nt(down_two, low_table, highest) * (1.0 / SKEL)


def second_kernel(
    g0_ref, g1_ref, g2_ref, g3_ref, p1_ref, p2_ref, t1_ref, t2_ref, g_ref, own_ref,
    u_ref, u16_ref, odd_ref, even_ref
):
    top = sum_of((g0_ref, g1_ref, g2_ref, g3_ref))
    weights = down_weights(p1_ref[...], p2_ref[...], top, t1_ref[...], t2_ref[...])
    for k in range(2):
        part = slice(k * LEAF, (k + 1) * LEAF)
        far = down_dot(weights, g_ref[part, :])
        value = (own_ref[:, part] + far) * (1.0 / LEAF)
        u_ref[:, part] = value
        u16_ref[:, part] = value.astype(bf16)
    even = even_leaf()

    @pl.when(even)
    def _():
        odd_ref[...] = u16_ref[:, :LEAF]
        even_ref[...] = u16_ref[:, LEAF:]

    @pl.when(jnp.logical_not(even))
    def _():
        odd_ref[...] = u16_ref[:, LEAF:]
        even_ref[...] = u16_ref[:, :LEAF]


def second_call(parts, p1, p2, t1, t2, table, own):
    return pl.pallas_call(
        second_kernel,
        in_specs=inside(10),
        out_shape=(
            shape_of((RHS, 2 * LEAF), f32),
            shape_of((RHS, 2 * LEAF), bf16),
            shape_of((RHS, LEAF), bf16),
            shape_of((RHS, LEAF), bf16),
        ),
        compiler_params=params,
        cost_estimate=cost(250_000_000, 5_000_000),
        name="second",
    )(*parts, p1, p2, t1, t2, table, own)


def row_sum(value):
    return jnp.sum(value, axis=1, keepdims=True)


def third_kernel(
    w_ref, u_ref, b_ref, u16_ref, table_a_ref, table_b_ref, table_ab_ref,
    g_ref, out_ref, up_ref, sums_ref
):
    up_ref[...] = up_dot(u_ref[...], g_ref[...])
    u_a, u_b = u16_ref[:, :LEAF], u16_ref[:, LEAF:]
    out_ref[:, :LEAF] = dot_symmetric(u_a, table_a_ref) + weight_of(w_ref, 1) * nt(
        u_b, table_ab_ref[...]
    )
    out_ref[:, LEAF:] = dot_symmetric(u_b, table_b_ref) + weight_of(w_ref, 2) * nn(
        u_a, table_ab_ref[...]
    )
    b, u = b_ref[...], u_ref[...]
    lane = lax.broadcasted_iota(jnp.int32, (RHS, 128), 1)
    sums = (row_sum(b * b), row_sum(b * u), row_sum(u * u))
    total = jnp.zeros((RHS, 128), f32)
    for k in range(3):
        total = jnp.where(lane == k, sums[k], total)
    sums_ref[...] = total


def third_call(w, u, field, u16, table_a, table_b, table_ab, table):
    return pl.pallas_call(
        third_kernel,
        in_specs=inside(8),
        out_shape=(
            shape_of((RHS, 2 * LEAF), f32),
            shape_of((RHS, SKEL), f32),
            shape_of((RHS, 128), f32),
        ),
        compiler_params=params,
        cost_estimate=cost(700_000_000, 10_000_000),
        name="third",
    )(w, u, field, u16, table_a, table_b, table_ab, table)


def rows_of(sums):
    high = sums.astype(bf16).astype(f32)
    rest = sums - high
    middle = rest.astype(bf16).astype(f32)
    low = rest - middle
    lane = lax.broadcasted_iota(jnp.int32, (RHS, 128), 1)
    packed = jnp.where(lane < 4, high, 0.0)
    packed += jnp.where((lane >= 4) & (lane < 8), pltpu.roll(middle, 4, 1), 0.0)
    packed += jnp.where((lane >= 8) & (lane < 12), pltpu.roll(low, 8, 1), 0.0)
    turned = packed.T[:16]
    pieces = [turned[4 * k : 4 * k + 4] for k in range(4)]
    row = jnp.concatenate(pieces, axis=1)
    return jnp.concatenate([row, jnp.zeros((4, SKEL), f32)], axis=0)


def sums_of(rows):
    high, middle, low = (rows[:4, k * RHS : (k + 1) * RHS] for k in range(3))
    total = high + (middle + low)
    return jnp.concatenate([total, jnp.zeros((124, RHS), f32)], axis=0).T


def put_all(sent_ref, value, sums):
    message = jnp.concatenate([value, rows_of(sums)], axis=0).astype(bf16)
    if len(sent_ref.shape) == 2:
        sent_ref[...] = message
    else:
        for k in range(sent_ref.shape[0]):
            sent_ref[k] = message


def add_last(sums, column):
    lane = lax.broadcasted_iota(jnp.int32, (RHS, 128), 1)
    return sums + jnp.where(lane == 3, column, 0.0)


def finish_kernel(
    w_ref, odd_ref, even_ref, below_table_ref, above_table_ref, u_ref, own_ref, up_ref,
    sums_ref, sent_ref, out_ref
):
    below, above = in_order(odd_ref, even_ref)
    near_a = own_ref[:, :LEAF] + weight_of(w_ref, 0) * nn(below, below_table_ref[...])
    near_b = own_ref[:, LEAF:] + weight_of(w_ref, 3) * nn(above, above_table_ref[...])
    out_ref[:, :LEAF] = near_a
    out_ref[:, LEAF:] = near_b
    bend = row_sum(u_ref[:, :LEAF] * near_a) + row_sum(u_ref[:, LEAF:] * near_b)
    put_all(sent_ref, up_ref[...] * (1.0 / LEAF), add_last(sums_ref[...], bend * (1.0 / LEAF)))


def finish_call(w, odd, even, below_table, above_table, u, own, up, sums, peers):
    return pl.pallas_call(
        finish_kernel,
        in_specs=inside(9),
        out_shape=(
            shape_of((peers, RHS + 8, SKEL), bf16),
            shape_of((RHS, 2 * LEAF), f32),
        ),
        compiler_params=params,
        cost_estimate=cost(270_000_000, 4_000_000),
        name="finish",
    )(w, odd, even, below_table, above_table, u, own, up, sums)


def climb_sums(level, total, table_ref, up_ref, sent_ref):
    up = total[:RHS]
    up_ref[...] = up
    sums = add_last(sums_of(total[RHS:]), level * row_sum(up * up))
    put_all(sent_ref, nn(up, table_ref[...], highest) * (1.0 / SKEL), sums)


def climb_sums_kernel(level, got_ref, table_ref, up_ref, sent_ref):
    climb_sums(level, total_of(got_ref), table_ref, up_ref, sent_ref)


def climb_sums_four_kernel(level, g0_ref, g1_ref, g2_ref, g3_ref, table_ref, up_ref, sent_ref):
    climb_sums(level, sum_of((g0_ref, g1_ref, g2_ref, g3_ref)), table_ref, up_ref, sent_ref)


def climb_sums_call(got, table, level):
    several = isinstance(got, list)
    kernel = climb_sums_four_kernel if several else climb_sums_kernel
    inputs = got if several else [got]
    return pl.pallas_call(
        lambda *refs: kernel(level, *refs),
        in_specs=inside(len(inputs) + 1),
        out_shape=(shape_of((RHS, SKEL), f32), shape_of((RHS + 8, SKEL), bf16)),
        compiler_params=params,
        cost_estimate=cost(50_000_000, 900_000),
        name="climb_sums",
    )(*inputs, table)


def join_sums_kernel(left_ref, right_ref, out_ref):
    total = sum_of((left_ref, right_ref))
    put_all(out_ref, total[:RHS], sums_of(total[RHS:]))


def join_sums_call(left, right):
    return pl.pallas_call(
        join_sums_kernel,
        in_specs=inside(2),
        out_shape=shape_of((RHS + 8, SKEL), bf16),
        compiler_params=params,
        cost_estimate=cost(100_000, 100_000),
        name="join_sums",
    )(left, right)


def last_kernel(
    g0_ref, g1_ref, g2_ref, g3_ref, p1_ref, p2_ref, t1_ref, t2_ref, g_ref, near_ref,
    b_ref, u_ref, x_ref, r_ref, xv_ref, rv_ref, x_sem, r_sem
):
    total = sum_of((g0_ref, g1_ref, g2_ref, g3_ref))
    top = total[:RHS]
    weights = down_weights(p1_ref[...], p2_ref[...], top, t1_ref[...], t2_ref[...])
    sums = add_last(sums_of(total[RHS:]), level_top * row_sum(top * top))
    bb, bu, uu, uv = sums[:, 0:1], sums[:, 1:2], sums[:, 2:3], sums[:, 3:4]
    step_one = bb / (ridge_term * bb + bu)
    ratio = bu / bb
    norm_one = step_one * step_one * (uu - ratio * bu)
    beta = norm_one / bb
    bend_rr = step_one * step_one * (ratio * ratio * bu - 2.0 * ratio * uu + uv)
    bend_rb = step_one * (ratio * bu - uu)
    bending = (
        ridge_term * (norm_one + beta * beta * bb)
        + bend_rr
        + 2.0 * beta * bend_rb
        + beta * beta * bu
    )
    step_two = norm_one / bending
    stores = []
    for k in range(4):
        part = slice(k * WIDE, (k + 1) * WIDE)
        far = down_dot(weights, g_ref[part, :])
        third = (near_ref[:, part] + far) * (1.0 / LEAF)
        first, second = b_ref[:, part], u_ref[:, part]
        residual_one = (step_one * ratio) * first - step_one * second
        direction = residual_one + beta * first
        applied = (
            ridge_term * direction + (step_one * ratio + beta) * second - step_one * third
        )
        xv_ref[:, part] = step_one * first + step_two * direction
        rv_ref[:, part] = residual_one - step_two * applied
        place = pl.ds(k * WIDE, WIDE)
        for store in (
            pltpu.make_async_copy(xv_ref.at[:, place], x_ref.at[:, place], x_sem.at[k]),
            pltpu.make_async_copy(rv_ref.at[:, place], r_ref.at[:, place], r_sem.at[k]),
        ):
            store.start()
            stores.append(store)
    for store in stores:
        store.wait()


def last_call(parts, p1, p2, t1, t2, table, near, field, u):
    return pl.pallas_call(
        last_kernel,
        in_specs=inside(12),
        out_specs=tuple(outside(2)),
        out_shape=(shape_of((RHS, 2 * LEAF), f32), shape_of((RHS, 2 * LEAF), f32)),
        scratch_shapes=[
            pltpu.VMEM((RHS, 2 * LEAF), f32),
            pltpu.VMEM((RHS, 2 * LEAF), f32),
            pltpu.SemaphoreType.DMA((4,)),
            pltpu.SemaphoreType.DMA((4,)),
        ],
        compiler_params=params,
        cost_estimate=cost(250_000_000, 7_000_000),
        name="last",
    )(*parts, p1, p2, t1, t2, table, near, field, u)


def exchange(sent, axis):
    return lax.all_to_all(sent, axis, 0, 0)


def chain_swap(value, first):
    count = lax.axis_size(ALL)
    pairs = [(i, i + 1) for i in range(first, count - 1, 2)]
    return lax.ppermute(value, ALL, pairs + [(j, i) for i, j in pairs])


def swap_both(odd, even):
    return chain_swap(odd, 1), chain_swap(even, 0)


def turned(value, axis, shift):
    count = lax.axis_size(axis)
    return lax.ppermute(value, axis, [(i, (i + shift) % count) for i in range(count)])


def turns(value, axis, stride):
    return [value] + [turned(value, axis, k) for k in range(stride, lax.axis_size(axis), stride)]


def swapped(value, axis):
    count = lax.axis_size(axis)
    return lax.ppermute(value, axis, [(i, i ^ 1) for i in range(count)])


def shards(points, right_side, skel_sub, skel_group, skel_top, neighbors, counts):
    leaves = lax.axis_size("leaf")
    sent, g, t1, x, b = start_call(points, right_side, skel_sub, skel_group, leaves)
    odd, even = swap_both(*pack_call(x, b))
    up_one, sent = climb_call(exchange(sent, "leaf"), t1)
    other = swapped(sent, "sub")
    row, w, t2 = prepare_call(neighbors, counts, x, skel_group, skel_top, sent)
    sent = join_call(sent, other, w)
    parts = turns(sent, "sub", 2)
    table_a, table_b, own = tables_call(x, b, row, sent)
    up_two, sent = climb_four_call(parts, t2, own)
    parts = turns(sent, "group", 1)
    table_ab, below_table, above_table, own = around_call(
        w, odd, even, x, b, row, own, sent
    )
    u, u16, odd, even = second_call(parts, up_one, up_two, t1, t2, g, own)

    odd, even = swap_both(odd, even)
    own, weights, sums = third_call(w, u, b, u16, table_a, table_b, table_ab, g)
    sent, near = finish_call(
        w, odd, even, below_table, above_table, u, own, weights, sums, leaves
    )
    up_one, sent = climb_sums_call(exchange(sent, "leaf"), t1, level_one)
    sent = join_sums_call(sent, swapped(sent, "sub"))
    up_two, sent = climb_sums_call(turns(sent, "sub", 2), t2, level_two)
    parts = turns(sent, "group", 1)
    return last_call(parts, up_one, up_two, t1, t2, g, near, b, u)


def solution(mesh):
    return jax.shard_map(
        shards,
        mesh=mesh,
        in_specs=(
            P(ALL, None),
            P(None, ALL),
            P(("group", "sub"), None),
            P("group", None),
            P(),
            P(ALL, None),
            P(ALL),
        ),
        out_specs=(P(None, ALL), P(None, ALL)),
        check_vma=False,
    )
```

```python
import math

import jax
import jax.numpy as jnp
from jax import lax
from jax.experimental import pallas as pl
from jax.experimental.pallas import tpu as pltpu
from jax.sharding import PartitionSpec as P

LEAF = 1024
SKEL = 256
RHS = 64
DIM = 256
ROWS = 256
STEPS = LEAF // ROWS
WIDE = 512
ALL = ("group", "sub", "leaf")

ridge_term = 3.0
level_one = 0.5
level_two = 0.25
level_top = 0.3

bf16 = jnp.bfloat16
f32 = jnp.float32
per_unit = 0.25 / DIM * math.log2(math.e)
vmem_bytes = 20 * 1024 * 1024


def shape_of(shape, dtype):
    return jax.ShapeDtypeStruct(shape, dtype)


def cost(flops, moved, exps=0):
    return pl.CostEstimate(flops=flops, bytes_accessed=moved, transcendentals=exps)


params = pltpu.CompilerParams(vmem_limit_bytes=vmem_bytes)


def nn(left, right, precision=None):
    return lax.dot_general(
        left, right, (((1,), (0,)), ((), ())), precision=precision, preferred_element_type=f32
    )


def nt(left, right, precision=None):
    return lax.dot_general(
        left, right, (((1,), (1,)), ((), ())), precision=precision, preferred_element_type=f32
    )


highest = lax.Precision.HIGHEST


def squares(rows):
    wide = rows.astype(f32)
    return wide * wide


def left_column(rows):
    return jnp.sum(squares(rows), axis=1, keepdims=True) * per_unit


def right_row(rows):
    square = squares(rows)
    high = square.astype(bf16)
    low = (square - high.astype(f32)).astype(bf16)
    ones = jnp.ones((8, rows.shape[1]), bf16)
    return (nt(ones, high) + nt(ones, low))[0:1] * per_unit


def gauss(left, column, right, row):
    return jnp.exp2(nt(left, right) * (2.0 * per_unit) - column - row)


def split(value):
    high = value.astype(bf16)
    low = (value - high.astype(f32)).astype(bf16)
    return high, low


def up_dot(field, table):
    both = nn(jnp.concatenate(split(field), axis=0), table)
    return both[:RHS] + both[RHS:]


def down_dot(weights, table):
    both = nt(jnp.concatenate(split(weights), axis=0), table)
    return both[:RHS] + both[RHS:]


def even_leaf():
    return lax.rem(lax.axis_index("leaf"), 2) == 0


def in_hbm(value):
    return pltpu.with_memory_space_constraint(value, pltpu.HBM)


def outside(count):
    return [pl.BlockSpec(memory_space=pltpu.HBM)] * count


def start_kernel(
    x_ref, b_ref, z1_ref, z2_ref,
    sent_ref, g_ref, t1_ref, xv_ref, bv_ref, gv_ref, z_ref, x_sem, b_sem, z_sem, g_sem
):
    parts = x_ref.shape[0] // WIDE
    z_loads, x_loads, b_loads = [], [], []
    for k, source in enumerate((z1_ref, z2_ref)):
        z_loads.append(pltpu.make_async_copy(source, z_ref.at[k], z_sem.at[k]))
    for k in range(parts):
        rows = pl.ds(k * WIDE, WIDE)
        x_loads.append(pltpu.make_async_copy(x_ref.at[rows, :], xv_ref.at[rows, :], x_sem.at[k]))
        b_loads.append(pltpu.make_async_copy(b_ref.at[:, rows], bv_ref.at[:, rows], b_sem.at[k]))
    z_loads[0].start()
    for k in range(parts):
        x_loads[k].start()
        b_loads[k].start()
    z_loads[1].start()
    stores = []
    z_loads[0].wait()
    z1 = z_ref[0]
    row = right_row(z1)
    total = jnp.zeros((RHS, SKEL), f32)
    for k in range(parts):
        rows = slice(k * WIDE, (k + 1) * WIDE)
        x_loads[k].wait()
        part = xv_ref[rows, :]
        table = gauss(part, left_column(part), z1, row).astype(bf16)
        gv_ref[rows, :] = table
        place = pl.ds(k * WIDE, WIDE)
        store = pltpu.make_async_copy(gv_ref.at[place, :], g_ref.at[place, :], g_sem.at[k])
        store.start()
        stores.append(store)
        b_loads[k].wait()
        total += up_dot(bv_ref[:, rows], table)
    value = (total * (1.0 / LEAF)).astype(bf16)
    for k in range(sent_ref.shape[0]):
        sent_ref[k] = value
    z_loads[1].wait()
    z2 = z_ref[1]
    t1_ref[...] = gauss(z1, left_column(z1), z2, right_row(z2))
    for store in stores:
        store.wait()


def start_call(points, field, z1, z2, peers):
    count = points.shape[0]
    parts = count // WIDE
    return pl.pallas_call(
        start_kernel,
        in_specs=outside(4),
        out_specs=tuple(inside(1) + outside(1) + inside(3)),
        out_shape=(
            shape_of((peers, RHS, SKEL), bf16),
            pltpu.HBM((count, SKEL), bf16),
            shape_of((SKEL, SKEL), f32),
            shape_of((count, DIM), bf16),
            shape_of((RHS, count), f32),
        ),
        scratch_shapes=[
            pltpu.VMEM((count, SKEL), bf16),
            pltpu.VMEM((2, SKEL, DIM), bf16),
            pltpu.SemaphoreType.DMA((parts,)),
            pltpu.SemaphoreType.DMA((parts,)),
            pltpu.SemaphoreType.DMA((2,)),
            pltpu.SemaphoreType.DMA((parts,)),
        ],
        compiler_params=params,
        cost_estimate=cost(600_000_000, 5_000_000, 655_360),
        name="start",
    )(*(in_hbm(value) for value in (points, field, z1, z2)))


def pack_kernel(x_ref, b_ref, odd_ref, even_ref, fold_ref, out_sem):
    parity = lax.rem(lax.axis_index("leaf"), 2)
    halves = (parity, 1 - parity)
    stores = []
    for k, out_ref in enumerate((odd_ref, even_ref)):
        rows = pl.ds(pl.multiple_of(halves[k] * LEAF, LEAF), LEAF)
        stores.append(
            pltpu.make_async_copy(x_ref.at[rows, :], out_ref.at[pl.ds(0, LEAF), :], out_sem.at[k])
        )
    for store in stores:
        store.start()
    for half in range(2):
        for k in range(STEPS):
            fold_ref[half, k * RHS : (k + 1) * RHS, :] = b_ref[
                :, half * LEAF + k * ROWS : half * LEAF + (k + 1) * ROWS
            ].astype(bf16)
    for k, out_ref in enumerate((odd_ref, even_ref)):
        stores.append(
            pltpu.make_async_copy(
                fold_ref.at[halves[k]], out_ref.at[pl.ds(LEAF, STEPS * RHS), :], out_sem.at[2 + k]
            )
        )
    for store in stores[2:]:
        store.start()
    for store in stores:
        store.wait()


def pack_call(points, field):
    return pl.pallas_call(
        pack_kernel,
        in_specs=inside(2),
        out_specs=tuple(outside(2)),
        out_shape=(
            pltpu.HBM((LEAF + STEPS * RHS, DIM), bf16),
            pltpu.HBM((LEAF + STEPS * RHS, DIM), bf16),
        ),
        scratch_shapes=[
            pltpu.VMEM((2, STEPS * RHS, ROWS), bf16),
            pltpu.SemaphoreType.DMA((4,)),
        ],
        compiler_params=params,
        cost_estimate=cost(1_000_000, 5_000_000),
        name="pack",
    )(points, field)


def smem():
    return pl.BlockSpec(memory_space=pltpu.SMEM)


def anywhere():
    return pl.BlockSpec(memory_space=pl.ANY)


def inside(count):
    return [pl.BlockSpec(memory_space=pltpu.VMEM)] * count


def listed(nb_ref, ct_ref, position, target):
    found = 0.0
    for k in range(nb_ref.shape[1]):
        hit = (k < ct_ref[position]) & (nb_ref[position, k] == target)
        found = found + jnp.where(hit, 1.0, 0.0)
    return found


def first_leaf_of():
    return lax.axis_index(ALL) * 2


def weight_of(w_ref, k):
    return w_ref[k : k + 1, 0:1]


def block(k):
    return slice(k * ROWS, (k + 1) * ROWS)


def make_symmetric(points, row, table_ref):
    for i in range(STEPS):
        rows = points[block(i), :]
        rest = slice(i * ROWS, LEAF)
        table_ref[block(i), rest] = gauss(
            rows, left_column(rows), points[rest, :], row[:, rest]
        ).astype(bf16)


def dot_symmetric(field, table_ref):
    out = [None] * STEPS

    def add(k, value):
        out[k] = value if out[k] is None else out[k] + value

    for i in range(STEPS):
        straight = nn(field[:, block(i)], table_ref[block(i), i * ROWS : LEAF])
        for j in range(i, STEPS):
            add(j, straight[:, block(j - i)])
        if i + 1 < STEPS:
            after = slice((i + 1) * ROWS, LEAF)
            add(i, nt(field[:, after], table_ref[block(i), after]))
    return jnp.concatenate(out, axis=1)


def make_block(left, points, row, table_ref):
    for i in range(STEPS):
        rows = left[block(i), :]
        table_ref[block(i), :] = gauss(rows, left_column(rows), points, row).astype(bf16)


def prepare_kernel(
    nb_ref, ct_ref, x_ref, z2_ref, z3_ref, after_ref, row_ref, w_ref, t2_ref, z_ref, z_sem
):
    del after_ref
    loads = []
    for k, source in enumerate((z2_ref, z3_ref)):
        loads.append(pltpu.make_async_copy(source, z_ref.at[k], z_sem.at[k]))
        loads[k].start()
    first = first_leaf_of()
    weights = (
        listed(nb_ref, ct_ref, 0, first - 1),
        listed(nb_ref, ct_ref, 0, first + 1),
        listed(nb_ref, ct_ref, 1, first),
        listed(nb_ref, ct_ref, 1, first + 2),
    )
    place = lax.broadcasted_iota(jnp.int32, (8, 128), 0)
    spread = jnp.zeros((8, 128), f32)
    for k in range(4):
        spread = jnp.where(place == k, weights[k], spread)
    w_ref[...] = spread
    row_ref[...] = right_row(x_ref[...])
    for load in loads:
        load.wait()
    z2, z3 = z_ref[0], z_ref[1]
    t2_ref[...] = gauss(z2, left_column(z2), z3, right_row(z3))


def prepare_call(neighbors, counts, points, z2, z3, after):
    return pl.pallas_call(
        prepare_kernel,
        in_specs=[smem(), smem()] + inside(1) + outside(2) + [anywhere()],
        out_shape=(
            shape_of((1, 2 * LEAF), f32),
            shape_of((8, 128), f32),
            shape_of((SKEL, SKEL), f32),
        ),
        scratch_shapes=[pltpu.VMEM((2, SKEL, DIM), bf16), pltpu.SemaphoreType.DMA((2,))],
        compiler_params=params,
        cost_estimate=cost(50_000_000, 2_000_000, 65_536),
        name="prepare",
    )(neighbors, counts, points, in_hbm(z2), in_hbm(z3), after)


def inner_kernel(x_ref, b_ref, after_ref, table_ref, out_ref, tv_ref, sem):
    del after_ref
    x_a, x_b = x_ref[:LEAF, :], x_ref[LEAF:, :]
    row_b = right_row(x_b)
    stores = []
    for i in range(STEPS):
        rows = x_a[block(i), :]
        tv_ref[block(i), :] = gauss(rows, left_column(rows), x_b, row_b).astype(bf16)
        place = pl.ds(i * ROWS, ROWS)
        store = pltpu.make_async_copy(tv_ref.at[place, :], table_ref.at[place, :], sem.at[i])
        store.start()
        stores.append(store)
    out_ref[:, :LEAF] = nt(b_ref[:, LEAF:].astype(bf16), tv_ref[...])
    out_ref[:, LEAF:] = nn(b_ref[:, :LEAF].astype(bf16), tv_ref[...])
    for store in stores:
        store.wait()


def inner_call(points, field, after):
    return pl.pallas_call(
        inner_kernel,
        in_specs=inside(2) + [anywhere()],
        out_specs=tuple(outside(1) + inside(1)),
        out_shape=(pltpu.HBM((LEAF, LEAF), bf16), shape_of((RHS, 2 * LEAF), f32)),
        scratch_shapes=[pltpu.VMEM((LEAF, LEAF), bf16), pltpu.SemaphoreType.DMA((STEPS,))],
        compiler_params=params,
        cost_estimate=cost(100_000_000, 1_000_000, 100_000),
        name="inner",
    )(points, field, after)


def tables_kernel(x_ref, b_ref, row_ref, after_ref, table_a_ref, table_b_ref, own_ref):
    del after_ref
    make_symmetric(x_ref[:LEAF, :], row_ref[:, :LEAF], table_a_ref)
    make_symmetric(x_ref[LEAF:, :], row_ref[:, LEAF:], table_b_ref)
    own_ref[:, :LEAF] = dot_symmetric(b_ref[:, :LEAF].astype(bf16), table_a_ref)
    own_ref[:, LEAF:] = dot_symmetric(b_ref[:, LEAF:].astype(bf16), table_b_ref)


def tables_call(points, field, row, after):
    return pl.pallas_call(
        tables_kernel,
        in_specs=inside(3) + [anywhere()],
        out_shape=(
            shape_of((LEAF, LEAF), bf16),
            shape_of((LEAF, LEAF), bf16),
            shape_of((RHS, 2 * LEAF), f32),
        ),
        compiler_params=params,
        cost_estimate=cost(3_000_000_000, 9_000_000, 2_400_000),
        name="tables",
    )(points, field, row, after)


def unfold(halo):
    parts = [halo[LEAF + k * RHS : LEAF + (k + 1) * RHS, :] for k in range(STEPS)]
    return jnp.concatenate(parts, axis=1)


def in_order(odd_ref, even_ref):
    even = even_leaf()
    odd_got, even_got = odd_ref[...], even_ref[...]
    return jnp.where(even, odd_got, even_got), jnp.where(even, even_got, odd_got)


def around_kernel(
    w_ref, odd_ref, even_ref, x_ref, inner_ref, row_ref, own_ref, after_ref,
    below_table_ref, above_table_ref, out_ref
):
    del after_ref
    x_a, x_b = x_ref[:LEAF, :], x_ref[LEAF:, :]
    row_a, row_b = row_ref[:, :LEAF], row_ref[:, LEAF:]
    near_a = own_ref[:, :LEAF] + weight_of(w_ref, 1) * inner_ref[:, :LEAF]
    near_b = own_ref[:, LEAF:] + weight_of(w_ref, 2) * inner_ref[:, LEAF:]

    def build(below_ref, above_ref):
        make_block(below_ref, x_a, row_a, below_table_ref)
        out_ref[:, :LEAF] = near_a + weight_of(w_ref, 0) * nn(
            unfold(below_ref), below_table_ref[...]
        )
        make_block(above_ref, x_b, row_b, above_table_ref)
        out_ref[:, LEAF:] = near_b + weight_of(w_ref, 3) * nn(
            unfold(above_ref), above_table_ref[...]
        )

    even = even_leaf()

    @pl.when(even)
    def _():
        build(odd_ref, even_ref)

    @pl.when(jnp.logical_not(even))
    def _():
        build(even_ref, odd_ref)


def around_call(w, odd, even, points, inner, row, own, after):
    return pl.pallas_call(
        around_kernel,
        in_specs=inside(7) + [anywhere()],
        out_shape=(
            shape_of((LEAF, LEAF), bf16),
            shape_of((LEAF, LEAF), bf16),
            shape_of((RHS, 2 * LEAF), f32),
        ),
        compiler_params=params,
        cost_estimate=cost(2_200_000_000, 9_000_000, 3_145_728),
        name="around",
    )(w, odd, even, points, inner, row, own, after)


def total_of(got_ref):
    total = got_ref[0].astype(f32)
    for k in range(1, got_ref.shape[0]):
        total += got_ref[k].astype(f32)
    return total


def climb_kernel(got_ref, table_ref, after_ref, up_ref, sent_ref):
    del after_ref
    total = total_of(got_ref)
    up_ref[...] = total
    sent_ref[...] = (nn(total, table_ref[...], highest) * (1.0 / SKEL)).astype(bf16)


def climb_call(got, table, after):
    return pl.pallas_call(
        climb_kernel,
        in_specs=inside(2) + [anywhere()],
        out_shape=(shape_of((RHS, SKEL), f32), shape_of((RHS, SKEL), bf16)),
        compiler_params=params,
        cost_estimate=cost(50_000_000, 900_000),
        name="climb",
    )(got, table, after)


def join_kernel(left_ref, right_ref, after_ref, out_ref):
    del after_ref
    out_ref[...] = (left_ref[...].astype(f32) + right_ref[...].astype(f32)).astype(bf16)


def join_call(left, right, after):
    return pl.pallas_call(
        join_kernel,
        in_specs=inside(2) + [anywhere()],
        out_shape=shape_of((RHS, SKEL), bf16),
        compiler_params=params,
        cost_estimate=cost(100_000, 100_000),
        name="join",
    )(left, right, after)


def climb_four_kernel(g0_ref, g1_ref, g2_ref, g3_ref, table_ref, after_ref, up_ref, sent_ref):
    del after_ref
    total = sum_of((g0_ref, g1_ref, g2_ref, g3_ref))
    up_ref[...] = total
    sent_ref[...] = (nn(total, table_ref[...], highest) * (1.0 / SKEL)).astype(bf16)


def climb_four_call(parts, table, after):
    return pl.pallas_call(
        climb_four_kernel,
        in_specs=inside(5) + [anywhere()],
        out_shape=(shape_of((RHS, SKEL), f32), shape_of((RHS, SKEL), bf16)),
        compiler_params=params,
        cost_estimate=cost(50_000_000, 900_000),
        name="climb_four",
    )(*parts, table, after)


def sum_of(refs):
    total = refs[0][...].astype(f32)
    for ref in refs[1:]:
        total += ref[...].astype(f32)
    return total


def down_weights(up_one, up_two, up_top, low_table, high_table):
    down_top = level_top * up_top
    down_two = level_two * up_two + nt(down_top, high_table, highest) * (1.0 / SKEL)
    return level_one * up_one + nt(down_two, low_table, highest) * (1.0 / SKEL)


def second_kernel(
    g0_ref, g1_ref, g2_ref, g3_ref, p1_ref, p2_ref, t1_ref, t2_ref, g_ref, own_ref,
    u_ref, u16_ref, odd_ref, even_ref
):
    top = sum_of((g0_ref, g1_ref, g2_ref, g3_ref))
    weights = down_weights(p1_ref[...], p2_ref[...], top, t1_ref[...], t2_ref[...])
    for k in range(2):
        part = slice(k * LEAF, (k + 1) * LEAF)
        far = down_dot(weights, g_ref[part, :])
        value = (own_ref[:, part] + far) * (1.0 / LEAF)
        u_ref[:, part] = value
        u16_ref[:, part] = value.astype(bf16)
    even = even_leaf()

    @pl.when(even)
    def _():
        odd_ref[...] = u16_ref[:, :LEAF]
        even_ref[...] = u16_ref[:, LEAF:]

    @pl.when(jnp.logical_not(even))
    def _():
        odd_ref[...] = u16_ref[:, LEAF:]
        even_ref[...] = u16_ref[:, :LEAF]


def second_call(parts, p1, p2, t1, t2, table, own):
    return pl.pallas_call(
        second_kernel,
        in_specs=inside(10),
        out_shape=(
            shape_of((RHS, 2 * LEAF), f32),
            shape_of((RHS, 2 * LEAF), bf16),
            shape_of((RHS, LEAF), bf16),
            shape_of((RHS, LEAF), bf16),
        ),
        compiler_params=params,
        cost_estimate=cost(250_000_000, 5_000_000),
        name="second",
    )(*parts, p1, p2, t1, t2, table, own)


def row_sum(value):
    return jnp.sum(value, axis=1, keepdims=True)


def third_kernel(
    w_ref, u_ref, b_ref, u16_ref, table_a_ref, table_b_ref, table_ab_ref,
    g_ref, out_ref, up_ref, sums_ref
):
    up_ref[...] = up_dot(u_ref[...], g_ref[...])
    u_a, u_b = u16_ref[:, :LEAF], u16_ref[:, LEAF:]
    out_ref[:, :LEAF] = dot_symmetric(u_a, table_a_ref) + weight_of(w_ref, 1) * nt(
        u_b, table_ab_ref[...]
    )
    out_ref[:, LEAF:] = dot_symmetric(u_b, table_b_ref) + weight_of(w_ref, 2) * nn(
        u_a, table_ab_ref[...]
    )
    b, u = b_ref[...], u_ref[...]
    lane = lax.broadcasted_iota(jnp.int32, (RHS, 128), 1)
    sums = (row_sum(b * b), row_sum(b * u), row_sum(u * u))
    total = jnp.zeros((RHS, 128), f32)
    for k in range(3):
        total = jnp.where(lane == k, sums[k], total)
    sums_ref[...] = total


def third_call(w, u, field, u16, table_a, table_b, table_ab, table):
    return pl.pallas_call(
        third_kernel,
        in_specs=inside(8),
        out_shape=(
            shape_of((RHS, 2 * LEAF), f32),
            shape_of((RHS, SKEL), f32),
            shape_of((RHS, 128), f32),
        ),
        compiler_params=params,
        cost_estimate=cost(700_000_000, 10_000_000),
        name="third",
    )(w, u, field, u16, table_a, table_b, table_ab, table)


def rows_of(sums):
    high = sums.astype(bf16).astype(f32)
    rest = sums - high
    middle = rest.astype(bf16).astype(f32)
    low = rest - middle
    lane = lax.broadcasted_iota(jnp.int32, (RHS, 128), 1)
    packed = jnp.where(lane < 4, high, 0.0)
    packed += jnp.where((lane >= 4) & (lane < 8), pltpu.roll(middle, 4, 1), 0.0)
    packed += jnp.where((lane >= 8) & (lane < 12), pltpu.roll(low, 8, 1), 0.0)
    turned = packed.T[:16]
    pieces = [turned[4 * k : 4 * k + 4] for k in range(4)]
    row = jnp.concatenate(pieces, axis=1)
    return jnp.concatenate([row, jnp.zeros((4, SKEL), f32)], axis=0)


def sums_of(rows):
    high, middle, low = (rows[:4, k * RHS : (k + 1) * RHS] for k in range(3))
    total = high + (middle + low)
    return jnp.concatenate([total, jnp.zeros((124, RHS), f32)], axis=0).T


def put_all(sent_ref, value, sums):
    message = jnp.concatenate([value, rows_of(sums)], axis=0).astype(bf16)
    if len(sent_ref.shape) == 2:
        sent_ref[...] = message
    else:
        for k in range(sent_ref.shape[0]):
            sent_ref[k] = message


def add_last(sums, column):
    lane = lax.broadcasted_iota(jnp.int32, (RHS, 128), 1)
    return sums + jnp.where(lane == 3, column, 0.0)


def finish_kernel(
    w_ref, odd_ref, even_ref, below_table_ref, above_table_ref, u_ref, own_ref, up_ref,
    sums_ref, sent_ref, out_ref
):
    below, above = in_order(odd_ref, even_ref)
    near_a = own_ref[:, :LEAF] + weight_of(w_ref, 0) * nn(below, below_table_ref[...])
    near_b = own_ref[:, LEAF:] + weight_of(w_ref, 3) * nn(above, above_table_ref[...])
    out_ref[:, :LEAF] = near_a
    out_ref[:, LEAF:] = near_b
    bend = row_sum(u_ref[:, :LEAF] * near_a) + row_sum(u_ref[:, LEAF:] * near_b)
    put_all(sent_ref, up_ref[...] * (1.0 / LEAF), add_last(sums_ref[...], bend * (1.0 / LEAF)))


def finish_call(w, odd, even, below_table, above_table, u, own, up, sums, peers):
    return pl.pallas_call(
        finish_kernel,
        in_specs=inside(9),
        out_shape=(
            shape_of((peers, RHS + 8, SKEL), bf16),
            shape_of((RHS, 2 * LEAF), f32),
        ),
        compiler_params=params,
        cost_estimate=cost(270_000_000, 4_000_000),
        name="finish",
    )(w, odd, even, below_table, above_table, u, own, up, sums)


def climb_sums(level, total, table_ref, up_ref, sent_ref):
    up = total[:RHS]
    up_ref[...] = up
    sums = add_last(sums_of(total[RHS:]), level * row_sum(up * up))
    put_all(sent_ref, nn(up, table_ref[...], highest) * (1.0 / SKEL), sums)


def climb_sums_kernel(level, got_ref, table_ref, up_ref, sent_ref):
    climb_sums(level, total_of(got_ref), table_ref, up_ref, sent_ref)


def climb_sums_four_kernel(level, g0_ref, g1_ref, g2_ref, g3_ref, table_ref, up_ref, sent_ref):
    climb_sums(level, sum_of((g0_ref, g1_ref, g2_ref, g3_ref)), table_ref, up_ref, sent_ref)


def climb_sums_call(got, table, level):
    several = isinstance(got, list)
    kernel = climb_sums_four_kernel if several else climb_sums_kernel
    inputs = got if several else [got]
    return pl.pallas_call(
        lambda *refs: kernel(level, *refs),
        in_specs=inside(len(inputs) + 1),
        out_shape=(shape_of((RHS, SKEL), f32), shape_of((RHS + 8, SKEL), bf16)),
        compiler_params=params,
        cost_estimate=cost(50_000_000, 900_000),
        name="climb_sums",
    )(*inputs, table)


def join_sums_kernel(left_ref, right_ref, out_ref):
    total = sum_of((left_ref, right_ref))
    put_all(out_ref, total[:RHS], sums_of(total[RHS:]))


def join_sums_call(left, right):
    return pl.pallas_call(
        join_sums_kernel,
        in_specs=inside(2),
        out_shape=shape_of((RHS + 8, SKEL), bf16),
        compiler_params=params,
        cost_estimate=cost(100_000, 100_000),
        name="join_sums",
    )(left, right)


def last_kernel(
    g0_ref, g1_ref, g2_ref, g3_ref, p1_ref, p2_ref, t1_ref, t2_ref, g_ref, near_ref,
    b_ref, u_ref, x_ref, r_ref, xv_ref, rv_ref, x_sem, r_sem
):
    total = sum_of((g0_ref, g1_ref, g2_ref, g3_ref))
    top = total[:RHS]
    weights = down_weights(p1_ref[...], p2_ref[...], top, t1_ref[...], t2_ref[...])
    sums = add_last(sums_of(total[RHS:]), level_top * row_sum(top * top))
    bb, bu, uu, uv = sums[:, 0:1], sums[:, 1:2], sums[:, 2:3], sums[:, 3:4]
    step_one = bb / (ridge_term * bb + bu)
    ratio = bu / bb
    norm_one = step_one * step_one * (uu - ratio * bu)
    beta = norm_one / bb
    bend_rr = step_one * step_one * (ratio * ratio * bu - 2.0 * ratio * uu + uv)
    bend_rb = step_one * (ratio * bu - uu)
    bending = (
        ridge_term * (norm_one + beta * beta * bb)
        + bend_rr
        + 2.0 * beta * bend_rb
        + beta * beta * bu
    )
    step_two = norm_one / bending
    stores = []
    for k in range(4):
        part = slice(k * WIDE, (k + 1) * WIDE)
        far = down_dot(weights, g_ref[part, :])
        third = (near_ref[:, part] + far) * (1.0 / LEAF)
        first, second = b_ref[:, part], u_ref[:, part]
        residual_one = (step_one * ratio) * first - step_one * second
        direction = residual_one + beta * first
        applied = (
            ridge_term * direction + (step_one * ratio + beta) * second - step_one * third
        )
        xv_ref[:, part] = step_one * first + step_two * direction
        rv_ref[:, part] = residual_one - step_two * applied
        place = pl.ds(k * WIDE, WIDE)
        for store in (
            pltpu.make_async_copy(xv_ref.at[:, place], x_ref.at[:, place], x_sem.at[k]),
            pltpu.make_async_copy(rv_ref.at[:, place], r_ref.at[:, place], r_sem.at[k]),
        ):
            store.start()
            stores.append(store)
    for store in stores:
        store.wait()


def last_call(parts, p1, p2, t1, t2, table, near, field, u):
    return pl.pallas_call(
        last_kernel,
        in_specs=inside(12),
        out_specs=tuple(outside(2)),
        out_shape=(shape_of((RHS, 2 * LEAF), f32), shape_of((RHS, 2 * LEAF), f32)),
        scratch_shapes=[
            pltpu.VMEM((RHS, 2 * LEAF), f32),
            pltpu.VMEM((RHS, 2 * LEAF), f32),
            pltpu.SemaphoreType.DMA((4,)),
            pltpu.SemaphoreType.DMA((4,)),
        ],
        compiler_params=params,
        cost_estimate=cost(250_000_000, 7_000_000),
        name="last",
    )(*parts, p1, p2, t1, t2, table, near, field, u)


def exchange(sent, axis):
    return lax.all_to_all(sent, axis, 0, 0)


def chain_swap(value, first):
    count = lax.axis_size(ALL)
    pairs = [(i, i + 1) for i in range(first, count - 1, 2)]
    return lax.ppermute(value, ALL, pairs + [(j, i) for i, j in pairs])


def swap_both(odd, even):
    return chain_swap(odd, 1), chain_swap(even, 0)


def turned(value, axis, shift):
    count = lax.axis_size(axis)
    return lax.ppermute(value, axis, [(i, (i + shift) % count) for i in range(count)])


def turns(value, axis, stride):
    return [value] + [turned(value, axis, k) for k in range(stride, lax.axis_size(axis), stride)]


def swapped(value, axis):
    count = lax.axis_size(axis)
    return lax.ppermute(value, axis, [(i, i ^ 1) for i in range(count)])


def shards(points, right_side, skel_sub, skel_group, skel_top, neighbors, counts):
    leaves = lax.axis_size("leaf")
    sent, g, t1, x, b = start_call(points, right_side, skel_sub, skel_group, leaves)
    odd, even = swap_both(*pack_call(x, b))
    table_ab, inner = inner_call(x, b, sent)
    up_one, sent = climb_call(exchange(sent, "leaf"), t1, inner)
    other = swapped(sent, "sub")
    row, w, t2 = prepare_call(neighbors, counts, x, skel_group, skel_top, sent)
    sent = join_call(sent, other, w)
    parts = turns(sent, "sub", 2)
    table_a, table_b, own = tables_call(x, b, row, sent)
    up_two, sent = climb_four_call(parts, t2, own)
    parts = turns(sent, "group", 1)
    below_table, above_table, own = around_call(w, odd, even, x, inner, row, own, sent)
    u, u16, odd, even = second_call(parts, up_one, up_two, t1, t2, g, own)

    odd, even = swap_both(odd, even)
    own, weights, sums = third_call(w, u, b, u16, table_a, table_b, table_ab, g)
    sent, near = finish_call(
        w, odd, even, below_table, above_table, u, own, weights, sums, leaves
    )
    up_one, sent = climb_sums_call(exchange(sent, "leaf"), t1, level_one)
    sent = join_sums_call(sent, swapped(sent, "sub"))
    up_two, sent = climb_sums_call(turns(sent, "sub", 2), t2, level_two)
    parts = turns(sent, "group", 1)
    return last_call(parts, up_one, up_two, t1, t2, g, near, b, u)


def solution(mesh):
    return jax.shard_map(
        shards,
        mesh=mesh,
        in_specs=(
            P(ALL, None),
            P(None, ALL),
            P(("group", "sub"), None),
            P("group", None),
            P(),
            P(ALL, None),
            P(ALL),
        ),
        out_specs=(P(None, ALL), P(None, ALL)),
        check_vma=False,
    )
```

```python
import math

import jax
import jax.numpy as jnp
from jax import lax
from jax.experimental import pallas as pl
from jax.experimental.pallas import tpu as pltpu
from jax.sharding import PartitionSpec as P

LEAF = 1024
SKEL = 256
RHS = 64
DIM = 256
ROWS = 256
STEPS = LEAF // ROWS
WIDE = 512
ALL = ("group", "sub", "leaf")

ridge_term = 3.0
level_one = 0.5
level_two = 0.25
level_top = 0.3

bf16 = jnp.bfloat16
f32 = jnp.float32
per_unit = 0.25 / DIM * math.log2(math.e)
vmem_bytes = 20 * 1024 * 1024


def shape_of(shape, dtype):
    return jax.ShapeDtypeStruct(shape, dtype)


def cost(flops, moved, exps=0):
    return pl.CostEstimate(flops=flops, bytes_accessed=moved, transcendentals=exps)


params = pltpu.CompilerParams(vmem_limit_bytes=vmem_bytes)


def nn(left, right, precision=None):
    return lax.dot_general(
        left, right, (((1,), (0,)), ((), ())), precision=precision, preferred_element_type=f32
    )


def nt(left, right, precision=None):
    return lax.dot_general(
        left, right, (((1,), (1,)), ((), ())), precision=precision, preferred_element_type=f32
    )


highest = lax.Precision.HIGHEST


def squares(rows):
    wide = rows.astype(f32)
    return wide * wide


def left_column(rows):
    return jnp.sum(squares(rows), axis=1, keepdims=True) * per_unit


def right_row(rows):
    square = squares(rows)
    high = square.astype(bf16)
    low = (square - high.astype(f32)).astype(bf16)
    ones = jnp.ones((8, rows.shape[1]), bf16)
    return (nt(ones, high) + nt(ones, low))[0:1] * per_unit


def gauss(left, column, right, row):
    return jnp.exp2(nt(left, right) * (2.0 * per_unit) - column - row)


def split(value):
    high = value.astype(bf16)
    low = (value - high.astype(f32)).astype(bf16)
    return high, low


def up_dot(field, table):
    both = nn(jnp.concatenate(split(field), axis=0), table)
    return both[:RHS] + both[RHS:]


def down_dot(weights, table):
    both = nt(jnp.concatenate(split(weights), axis=0), table)
    return both[:RHS] + both[RHS:]


def even_leaf():
    return lax.rem(lax.axis_index("leaf"), 2) == 0


def in_hbm(value):
    return pltpu.with_memory_space_constraint(value, pltpu.HBM)


def outside(count):
    return [pl.BlockSpec(memory_space=pltpu.HBM)] * count


def start_kernel(
    x_ref, b_ref, z1_ref, z2_ref,
    sent_ref, g_ref, t1_ref, xv_ref, bv_ref, gv_ref, z_ref, x_sem, b_sem, z_sem, g_sem
):
    parts = x_ref.shape[0] // WIDE
    z_loads, x_loads, b_loads = [], [], []
    for k, source in enumerate((z1_ref, z2_ref)):
        z_loads.append(pltpu.make_async_copy(source, z_ref.at[k], z_sem.at[k]))
    for k in range(parts):
        rows = pl.ds(k * WIDE, WIDE)
        x_loads.append(pltpu.make_async_copy(x_ref.at[rows, :], xv_ref.at[rows, :], x_sem.at[k]))
        b_loads.append(pltpu.make_async_copy(b_ref.at[:, rows], bv_ref.at[:, rows], b_sem.at[k]))
    z_loads[0].start()
    for k in range(parts):
        x_loads[k].start()
        b_loads[k].start()
    z_loads[1].start()
    stores = []
    z_loads[0].wait()
    z1 = z_ref[0]
    row = right_row(z1)
    total = jnp.zeros((RHS, SKEL), f32)
    for k in range(parts):
        rows = slice(k * WIDE, (k + 1) * WIDE)
        x_loads[k].wait()
        part = xv_ref[rows, :]
        table = gauss(part, left_column(part), z1, row).astype(bf16)
        gv_ref[rows, :] = table
        place = pl.ds(k * WIDE, WIDE)
        store = pltpu.make_async_copy(gv_ref.at[place, :], g_ref.at[place, :], g_sem.at[k])
        store.start()
        stores.append(store)
        b_loads[k].wait()
        total += up_dot(bv_ref[:, rows], table)
    value = (total * (1.0 / LEAF)).astype(bf16)
    for k in range(sent_ref.shape[0]):
        sent_ref[k] = value
    z_loads[1].wait()
    z2 = z_ref[1]
    t1_ref[...] = gauss(z1, left_column(z1), z2, right_row(z2))
    for store in stores:
        store.wait()


def start_call(points, field, z1, z2, peers):
    count = points.shape[0]
    parts = count // WIDE
    return pl.pallas_call(
        start_kernel,
        in_specs=outside(4),
        out_specs=tuple(inside(1) + outside(1) + inside(3)),
        out_shape=(
            shape_of((peers, RHS, SKEL), bf16),
            pltpu.HBM((count, SKEL), bf16),
            shape_of((SKEL, SKEL), f32),
            shape_of((count, DIM), bf16),
            shape_of((RHS, count), f32),
        ),
        scratch_shapes=[
            pltpu.VMEM((count, SKEL), bf16),
            pltpu.VMEM((2, SKEL, DIM), bf16),
            pltpu.SemaphoreType.DMA((parts,)),
            pltpu.SemaphoreType.DMA((parts,)),
            pltpu.SemaphoreType.DMA((2,)),
            pltpu.SemaphoreType.DMA((parts,)),
        ],
        compiler_params=params,
        cost_estimate=cost(600_000_000, 5_000_000, 655_360),
        name="start",
    )(*(in_hbm(value) for value in (points, field, z1, z2)))


def pack_kernel(x_ref, b_ref, odd_ref, even_ref, fold_ref, out_sem):
    parity = lax.rem(lax.axis_index("leaf"), 2)
    halves = (parity, 1 - parity)
    stores = []
    for k, out_ref in enumerate((odd_ref, even_ref)):
        rows = pl.ds(pl.multiple_of(halves[k] * LEAF, LEAF), LEAF)
        stores.append(
            pltpu.make_async_copy(x_ref.at[rows, :], out_ref.at[pl.ds(0, LEAF), :], out_sem.at[k])
        )
    for store in stores:
        store.start()
    for half in range(2):
        for k in range(STEPS):
            fold_ref[half, k * RHS : (k + 1) * RHS, :] = b_ref[
                :, half * LEAF + k * ROWS : half * LEAF + (k + 1) * ROWS
            ].astype(bf16)
    for k, out_ref in enumerate((odd_ref, even_ref)):
        stores.append(
            pltpu.make_async_copy(
                fold_ref.at[halves[k]], out_ref.at[pl.ds(LEAF, STEPS * RHS), :], out_sem.at[2 + k]
            )
        )
    for store in stores[2:]:
        store.start()
    for store in stores:
        store.wait()


def pack_call(points, field):
    return pl.pallas_call(
        pack_kernel,
        in_specs=inside(2),
        out_specs=tuple(outside(2)),
        out_shape=(
            pltpu.HBM((LEAF + STEPS * RHS, DIM), bf16),
            pltpu.HBM((LEAF + STEPS * RHS, DIM), bf16),
        ),
        scratch_shapes=[
            pltpu.VMEM((2, STEPS * RHS, ROWS), bf16),
            pltpu.SemaphoreType.DMA((4,)),
        ],
        compiler_params=params,
        cost_estimate=cost(1_000_000, 5_000_000),
        name="pack",
    )(points, field)


def smem():
    return pl.BlockSpec(memory_space=pltpu.SMEM)


def anywhere():
    return pl.BlockSpec(memory_space=pl.ANY)


def inside(count):
    return [pl.BlockSpec(memory_space=pltpu.VMEM)] * count


def listed(nb_ref, ct_ref, position, target):
    found = 0.0
    for k in range(nb_ref.shape[1]):
        hit = (k < ct_ref[position]) & (nb_ref[position, k] == target)
        found = found + jnp.where(hit, 1.0, 0.0)
    return found


def first_leaf_of():
    return lax.axis_index(ALL) * 2


def weight_of(w_ref, k):
    return w_ref[k : k + 1, 0:1]


def block(k):
    return slice(k * ROWS, (k + 1) * ROWS)


def make_symmetric(points, row, table_ref):
    for i in range(STEPS):
        rows = points[block(i), :]
        rest = slice(i * ROWS, LEAF)
        table_ref[block(i), rest] = gauss(
            rows, left_column(rows), points[rest, :], row[:, rest]
        ).astype(bf16)


def dot_symmetric(field, table_ref):
    out = [None] * STEPS

    def add(k, value):
        out[k] = value if out[k] is None else out[k] + value

    for i in range(STEPS):
        straight = nn(field[:, block(i)], table_ref[block(i), i * ROWS : LEAF])
        for j in range(i, STEPS):
            add(j, straight[:, block(j - i)])
        if i + 1 < STEPS:
            after = slice((i + 1) * ROWS, LEAF)
            add(i, nt(field[:, after], table_ref[block(i), after]))
    return jnp.concatenate(out, axis=1)


def make_block(left, points, row, table_ref):
    for i in range(STEPS):
        rows = left[block(i), :]
        table_ref[block(i), :] = gauss(rows, left_column(rows), points, row).astype(bf16)


def prepare_kernel(nb_ref, ct_ref, after_ref, w_ref):
    del after_ref
    first = first_leaf_of()
    weights = (
        listed(nb_ref, ct_ref, 0, first - 1),
        listed(nb_ref, ct_ref, 0, first + 1),
        listed(nb_ref, ct_ref, 1, first),
        listed(nb_ref, ct_ref, 1, first + 2),
    )
    place = lax.broadcasted_iota(jnp.int32, (8, 128), 0)
    spread = jnp.zeros((8, 128), f32)
    for k in range(4):
        spread = jnp.where(place == k, weights[k], spread)
    w_ref[...] = spread


def prepare_call(neighbors, counts, after):
    return pl.pallas_call(
        prepare_kernel,
        in_specs=[smem(), smem(), anywhere()],
        out_shape=shape_of((8, 128), f32),
        compiler_params=params,
        cost_estimate=cost(50_000_000, 2_000_000, 65_536),
        name="prepare",
    )(neighbors, counts, after)


def inner_kernel(x_ref, b_ref, after_ref, table_ref, out_ref, tv_ref, sem):
    del after_ref
    x_a, x_b = x_ref[:LEAF, :], x_ref[LEAF:, :]
    row_b = right_row(x_b)
    stores = []
    for i in range(STEPS):
        rows = x_a[block(i), :]
        tv_ref[block(i), :] = gauss(rows, left_column(rows), x_b, row_b).astype(bf16)
        place = pl.ds(i * ROWS, ROWS)
        store = pltpu.make_async_copy(tv_ref.at[place, :], table_ref.at[place, :], sem.at[i])
        store.start()
        stores.append(store)
    out_ref[:, :LEAF] = nt(b_ref[:, LEAF:].astype(bf16), tv_ref[...])
    out_ref[:, LEAF:] = nn(b_ref[:, :LEAF].astype(bf16), tv_ref[...])
    for store in stores:
        store.wait()


def inner_call(points, field, after):
    return pl.pallas_call(
        inner_kernel,
        in_specs=inside(2) + [anywhere()],
        out_specs=tuple(outside(1) + inside(1)),
        out_shape=(pltpu.HBM((LEAF, LEAF), bf16), shape_of((RHS, 2 * LEAF), f32)),
        scratch_shapes=[pltpu.VMEM((LEAF, LEAF), bf16), pltpu.SemaphoreType.DMA((STEPS,))],
        compiler_params=params,
        cost_estimate=cost(100_000_000, 1_000_000, 100_000),
        name="inner",
    )(points, field, after)


def tables_kernel(
    x_ref, b_ref, z2_ref, z3_ref, after_ref, table_ref, own_ref, row_ref, t2_ref, z_ref, z_sem
):
    del after_ref
    loads = []
    for k, source in enumerate((z2_ref, z3_ref)):
        loads.append(pltpu.make_async_copy(source, z_ref.at[k], z_sem.at[k]))
        loads[k].start()
    row_ref[...] = right_row(x_ref[...])
    make_symmetric(x_ref[:LEAF, :], row_ref[:, :LEAF], table_ref)
    own_ref[...] = dot_symmetric(b_ref[:, :LEAF].astype(bf16), table_ref)
    for load in loads:
        load.wait()
    z2, z3 = z_ref[0], z_ref[1]
    t2_ref[...] = gauss(z2, left_column(z2), z3, right_row(z3))


def tables_call(points, field, z2, z3, after):
    return pl.pallas_call(
        tables_kernel,
        in_specs=inside(2) + outside(2) + [anywhere()],
        out_shape=(
            shape_of((LEAF, LEAF), bf16),
            shape_of((RHS, LEAF), f32),
            shape_of((1, 2 * LEAF), f32),
            shape_of((SKEL, SKEL), f32),
        ),
        scratch_shapes=[pltpu.VMEM((2, SKEL, DIM), bf16), pltpu.SemaphoreType.DMA((2,))],
        compiler_params=params,
        cost_estimate=cost(3_000_000_000, 9_000_000, 2_400_000),
        name="tables",
    )(points, field, in_hbm(z2), in_hbm(z3), after)


def unfold(halo):
    parts = [halo[LEAF + k * RHS : LEAF + (k + 1) * RHS, :] for k in range(STEPS)]
    return jnp.concatenate(parts, axis=1)


def in_order(odd_ref, even_ref):
    even = even_leaf()
    odd_got, even_got = odd_ref[...], even_ref[...]
    return jnp.where(even, odd_got, even_got), jnp.where(even, even_got, odd_got)


def around_kernel(
    w_ref, odd_ref, even_ref, x_ref, b_ref, inner_ref, row_ref, own_ref, after_ref,
    table_b_ref, below_table_ref, above_table_ref, out_ref, halo_ref, sem
):
    del after_ref
    parity = lax.rem(lax.axis_index("leaf"), 2)
    loads = []
    for k, source in enumerate((odd_ref, even_ref)):
        slot = parity if k == 0 else 1 - parity
        loads.append(pltpu.make_async_copy(source, halo_ref.at[slot], sem.at[k]))
    for load in loads:
        load.start()
    x_a, x_b = x_ref[:LEAF, :], x_ref[LEAF:, :]
    row_a, row_b = row_ref[:, :LEAF], row_ref[:, LEAF:]
    make_symmetric(x_b, row_b, table_b_ref)
    own_b = dot_symmetric(b_ref[:, LEAF:].astype(bf16), table_b_ref)
    near_a = own_ref[...] + weight_of(w_ref, 1) * inner_ref[:, :LEAF]
    near_b = own_b + weight_of(w_ref, 2) * inner_ref[:, LEAF:]
    for load in loads:
        load.wait()
    below_ref, above_ref = halo_ref.at[0], halo_ref.at[1]
    make_block(below_ref, x_a, row_a, below_table_ref)
    out_ref[:, :LEAF] = near_a + weight_of(w_ref, 0) * nn(
        unfold(below_ref), below_table_ref[...]
    )
    make_block(above_ref, x_b, row_b, above_table_ref)
    out_ref[:, LEAF:] = near_b + weight_of(w_ref, 3) * nn(
        unfold(above_ref), above_table_ref[...]
    )


def around_call(w, odd, even, points, field, inner, row, own, after):
    return pl.pallas_call(
        around_kernel,
        in_specs=inside(1) + [anywhere()] * 2 + inside(5) + [anywhere()],
        out_shape=(
            shape_of((LEAF, LEAF), bf16),
            shape_of((LEAF, LEAF), bf16),
            shape_of((LEAF, LEAF), bf16),
            shape_of((RHS, 2 * LEAF), f32),
        ),
        scratch_shapes=[
            pltpu.VMEM((2, LEAF + STEPS * RHS, DIM), bf16),
            pltpu.SemaphoreType.DMA((2,)),
        ],
        compiler_params=params,
        cost_estimate=cost(2_200_000_000, 9_000_000, 3_145_728),
        name="around",
    )(w, odd, even, points, field, inner, row, own, after)


def total_of(got_ref):
    total = got_ref[0].astype(f32)
    for k in range(1, got_ref.shape[0]):
        total += got_ref[k].astype(f32)
    return total


def climb_kernel(got_ref, table_ref, after_ref, up_ref, sent_ref):
    del after_ref
    total = total_of(got_ref)
    up_ref[...] = total
    sent_ref[...] = (nn(total, table_ref[...], highest) * (1.0 / SKEL)).astype(bf16)


def climb_call(got, table, after):
    return pl.pallas_call(
        climb_kernel,
        in_specs=inside(2) + [anywhere()],
        out_shape=(shape_of((RHS, SKEL), f32), shape_of((RHS, SKEL), bf16)),
        compiler_params=params,
        cost_estimate=cost(50_000_000, 900_000),
        name="climb",
    )(got, table, after)


def join_kernel(left_ref, right_ref, after_ref, out_ref):
    del after_ref
    out_ref[...] = (left_ref[...].astype(f32) + right_ref[...].astype(f32)).astype(bf16)


def join_call(left, right, after):
    return pl.pallas_call(
        join_kernel,
        in_specs=inside(2) + [anywhere()],
        out_shape=shape_of((RHS, SKEL), bf16),
        compiler_params=params,
        cost_estimate=cost(100_000, 100_000),
        name="join",
    )(left, right, after)


def climb_four_kernel(g0_ref, g1_ref, g2_ref, g3_ref, table_ref, after_ref, up_ref, sent_ref):
    del after_ref
    total = sum_of((g0_ref, g1_ref, g2_ref, g3_ref))
    up_ref[...] = total
    sent_ref[...] = (nn(total, table_ref[...], highest) * (1.0 / SKEL)).astype(bf16)


def climb_four_call(parts, table, after):
    return pl.pallas_call(
        climb_four_kernel,
        in_specs=inside(5) + [anywhere()],
        out_shape=(shape_of((RHS, SKEL), f32), shape_of((RHS, SKEL), bf16)),
        compiler_params=params,
        cost_estimate=cost(50_000_000, 900_000),
        name="climb_four",
    )(*parts, table, after)


def sum_of(refs):
    total = refs[0][...].astype(f32)
    for ref in refs[1:]:
        total += ref[...].astype(f32)
    return total


def down_weights(up_one, up_two, up_top, low_table, high_table):
    down_top = level_top * up_top
    down_two = level_two * up_two + nt(down_top, high_table, highest) * (1.0 / SKEL)
    return level_one * up_one + nt(down_two, low_table, highest) * (1.0 / SKEL)


def second_kernel(
    g0_ref, g1_ref, g2_ref, g3_ref, p1_ref, p2_ref, t1_ref, t2_ref, g_ref, own_ref,
    u_ref, u16_ref, odd_ref, even_ref
):
    top = sum_of((g0_ref, g1_ref, g2_ref, g3_ref))
    weights = down_weights(p1_ref[...], p2_ref[...], top, t1_ref[...], t2_ref[...])
    for k in range(2):
        part = slice(k * LEAF, (k + 1) * LEAF)
        far = down_dot(weights, g_ref[part, :])
        value = (own_ref[:, part] + far) * (1.0 / LEAF)
        u_ref[:, part] = value
        u16_ref[:, part] = value.astype(bf16)
    even = even_leaf()

    @pl.when(even)
    def _():
        odd_ref[...] = u16_ref[:, :LEAF]
        even_ref[...] = u16_ref[:, LEAF:]

    @pl.when(jnp.logical_not(even))
    def _():
        odd_ref[...] = u16_ref[:, LEAF:]
        even_ref[...] = u16_ref[:, :LEAF]


def second_call(parts, p1, p2, t1, t2, table, own):
    return pl.pallas_call(
        second_kernel,
        in_specs=inside(10),
        out_shape=(
            shape_of((RHS, 2 * LEAF), f32),
            shape_of((RHS, 2 * LEAF), bf16),
            shape_of((RHS, LEAF), bf16),
            shape_of((RHS, LEAF), bf16),
        ),
        compiler_params=params,
        cost_estimate=cost(250_000_000, 5_000_000),
        name="second",
    )(*parts, p1, p2, t1, t2, table, own)


def row_sum(value):
    return jnp.sum(value, axis=1, keepdims=True)


def third_kernel(
    w_ref, u_ref, b_ref, u16_ref, table_a_ref, table_b_ref, table_ab_ref,
    g_ref, out_ref, up_ref, sums_ref
):
    up_ref[...] = up_dot(u_ref[...], g_ref[...])
    u_a, u_b = u16_ref[:, :LEAF], u16_ref[:, LEAF:]
    out_ref[:, :LEAF] = dot_symmetric(u_a, table_a_ref) + weight_of(w_ref, 1) * nt(
        u_b, table_ab_ref[...]
    )
    out_ref[:, LEAF:] = dot_symmetric(u_b, table_b_ref) + weight_of(w_ref, 2) * nn(
        u_a, table_ab_ref[...]
    )
    b, u = b_ref[...], u_ref[...]
    lane = lax.broadcasted_iota(jnp.int32, (RHS, 128), 1)
    sums = (row_sum(b * b), row_sum(b * u), row_sum(u * u))
    total = jnp.zeros((RHS, 128), f32)
    for k in range(3):
        total = jnp.where(lane == k, sums[k], total)
    sums_ref[...] = total


def third_call(w, u, field, u16, table_a, table_b, table_ab, table):
    return pl.pallas_call(
        third_kernel,
        in_specs=inside(8),
        out_shape=(
            shape_of((RHS, 2 * LEAF), f32),
            shape_of((RHS, SKEL), f32),
            shape_of((RHS, 128), f32),
        ),
        compiler_params=params,
        cost_estimate=cost(700_000_000, 10_000_000),
        name="third",
    )(w, u, field, u16, table_a, table_b, table_ab, table)


def rows_of(sums):
    high = sums.astype(bf16).astype(f32)
    rest = sums - high
    middle = rest.astype(bf16).astype(f32)
    low = rest - middle
    lane = lax.broadcasted_iota(jnp.int32, (RHS, 128), 1)
    packed = jnp.where(lane < 4, high, 0.0)
    packed += jnp.where((lane >= 4) & (lane < 8), pltpu.roll(middle, 4, 1), 0.0)
    packed += jnp.where((lane >= 8) & (lane < 12), pltpu.roll(low, 8, 1), 0.0)
    turned = packed.T[:16]
    pieces = [turned[4 * k : 4 * k + 4] for k in range(4)]
    row = jnp.concatenate(pieces, axis=1)
    return jnp.concatenate([row, jnp.zeros((4, SKEL), f32)], axis=0)


def sums_of(rows):
    high, middle, low = (rows[:4, k * RHS : (k + 1) * RHS] for k in range(3))
    total = high + (middle + low)
    return jnp.concatenate([total, jnp.zeros((124, RHS), f32)], axis=0).T


def put_all(sent_ref, value, sums):
    message = jnp.concatenate([value, rows_of(sums)], axis=0).astype(bf16)
    if len(sent_ref.shape) == 2:
        sent_ref[...] = message
    else:
        for k in range(sent_ref.shape[0]):
            sent_ref[k] = message


def add_last(sums, column):
    lane = lax.broadcasted_iota(jnp.int32, (RHS, 128), 1)
    return sums + jnp.where(lane == 3, column, 0.0)


def finish_kernel(
    w_ref, odd_ref, even_ref, below_table_ref, above_table_ref, u_ref, own_ref, up_ref,
    sums_ref, sent_ref, out_ref
):
    below, above = in_order(odd_ref, even_ref)
    near_a = own_ref[:, :LEAF] + weight_of(w_ref, 0) * nn(below, below_table_ref[...])
    near_b = own_ref[:, LEAF:] + weight_of(w_ref, 3) * nn(above, above_table_ref[...])
    out_ref[:, :LEAF] = near_a
    out_ref[:, LEAF:] = near_b
    bend = row_sum(u_ref[:, :LEAF] * near_a) + row_sum(u_ref[:, LEAF:] * near_b)
    put_all(sent_ref, up_ref[...] * (1.0 / LEAF), add_last(sums_ref[...], bend * (1.0 / LEAF)))


def finish_call(w, odd, even, below_table, above_table, u, own, up, sums, peers):
    return pl.pallas_call(
        finish_kernel,
        in_specs=inside(9),
        out_shape=(
            shape_of((peers, RHS + 8, SKEL), bf16),
            shape_of((RHS, 2 * LEAF), f32),
        ),
        compiler_params=params,
        cost_estimate=cost(270_000_000, 4_000_000),
        name="finish",
    )(w, odd, even, below_table, above_table, u, own, up, sums)


def climb_sums(level, total, table_ref, up_ref, sent_ref):
    up = total[:RHS]
    up_ref[...] = up
    sums = add_last(sums_of(total[RHS:]), level * row_sum(up * up))
    put_all(sent_ref, nn(up, table_ref[...], highest) * (1.0 / SKEL), sums)


def climb_sums_kernel(level, got_ref, table_ref, up_ref, sent_ref):
    climb_sums(level, total_of(got_ref), table_ref, up_ref, sent_ref)


def climb_sums_four_kernel(level, g0_ref, g1_ref, g2_ref, g3_ref, table_ref, up_ref, sent_ref):
    climb_sums(level, sum_of((g0_ref, g1_ref, g2_ref, g3_ref)), table_ref, up_ref, sent_ref)


def climb_sums_call(got, table, level):
    several = isinstance(got, list)
    kernel = climb_sums_four_kernel if several else climb_sums_kernel
    inputs = got if several else [got]
    return pl.pallas_call(
        lambda *refs: kernel(level, *refs),
        in_specs=inside(len(inputs) + 1),
        out_shape=(shape_of((RHS, SKEL), f32), shape_of((RHS + 8, SKEL), bf16)),
        compiler_params=params,
        cost_estimate=cost(50_000_000, 900_000),
        name="climb_sums",
    )(*inputs, table)


def join_sums_kernel(left_ref, right_ref, out_ref):
    total = sum_of((left_ref, right_ref))
    put_all(out_ref, total[:RHS], sums_of(total[RHS:]))


def join_sums_call(left, right):
    return pl.pallas_call(
        join_sums_kernel,
        in_specs=inside(2),
        out_shape=shape_of((RHS + 8, SKEL), bf16),
        compiler_params=params,
        cost_estimate=cost(100_000, 100_000),
        name="join_sums",
    )(left, right)


def last_kernel(
    g0_ref, g1_ref, g2_ref, g3_ref, p1_ref, p2_ref, t1_ref, t2_ref, g_ref, near_ref,
    b_ref, u_ref, x_ref, r_ref, xv_ref, rv_ref, x_sem, r_sem
):
    total = sum_of((g0_ref, g1_ref, g2_ref, g3_ref))
    top = total[:RHS]
    weights = down_weights(p1_ref[...], p2_ref[...], top, t1_ref[...], t2_ref[...])
    sums = add_last(sums_of(total[RHS:]), level_top * row_sum(top * top))
    bb, bu, uu, uv = sums[:, 0:1], sums[:, 1:2], sums[:, 2:3], sums[:, 3:4]
    step_one = bb / (ridge_term * bb + bu)
    ratio = bu / bb
    norm_one = step_one * step_one * (uu - ratio * bu)
    beta = norm_one / bb
    bend_rr = step_one * step_one * (ratio * ratio * bu - 2.0 * ratio * uu + uv)
    bend_rb = step_one * (ratio * bu - uu)
    bending = (
        ridge_term * (norm_one + beta * beta * bb)
        + bend_rr
        + 2.0 * beta * bend_rb
        + beta * beta * bu
    )
    step_two = norm_one / bending
    stores = []
    for k in range(4):
        part = slice(k * WIDE, (k + 1) * WIDE)
        far = down_dot(weights, g_ref[part, :])
        third = (near_ref[:, part] + far) * (1.0 / LEAF)
        first, second = b_ref[:, part], u_ref[:, part]
        residual_one = (step_one * ratio) * first - step_one * second
        direction = residual_one + beta * first
        applied = (
            ridge_term * direction + (step_one * ratio + beta) * second - step_one * third
        )
        xv_ref[:, part] = step_one * first + step_two * direction
        rv_ref[:, part] = residual_one - step_two * applied
        place = pl.ds(k * WIDE, WIDE)
        for store in (
            pltpu.make_async_copy(xv_ref.at[:, place], x_ref.at[:, place], x_sem.at[k]),
            pltpu.make_async_copy(rv_ref.at[:, place], r_ref.at[:, place], r_sem.at[k]),
        ):
            store.start()
            stores.append(store)
    for store in stores:
        store.wait()


def last_call(parts, p1, p2, t1, t2, table, near, field, u):
    return pl.pallas_call(
        last_kernel,
        in_specs=inside(12),
        out_specs=tuple(outside(2)),
        out_shape=(shape_of((RHS, 2 * LEAF), f32), shape_of((RHS, 2 * LEAF), f32)),
        scratch_shapes=[
            pltpu.VMEM((RHS, 2 * LEAF), f32),
            pltpu.VMEM((RHS, 2 * LEAF), f32),
            pltpu.SemaphoreType.DMA((4,)),
            pltpu.SemaphoreType.DMA((4,)),
        ],
        compiler_params=params,
        cost_estimate=cost(250_000_000, 7_000_000),
        name="last",
    )(*parts, p1, p2, t1, t2, table, near, field, u)


def exchange(sent, axis):
    return lax.all_to_all(sent, axis, 0, 0)


def chain_swap(value, first):
    count = lax.axis_size(ALL)
    pairs = [(i, i + 1) for i in range(first, count - 1, 2)]
    return lax.ppermute(value, ALL, pairs + [(j, i) for i, j in pairs])


def swap_both(odd, even):
    return chain_swap(odd, 1), chain_swap(even, 0)


def turned(value, axis, shift):
    count = lax.axis_size(axis)
    return lax.ppermute(value, axis, [(i, (i + shift) % count) for i in range(count)])


def turns(value, axis, stride):
    return [value] + [turned(value, axis, k) for k in range(stride, lax.axis_size(axis), stride)]


def swapped(value, axis):
    count = lax.axis_size(axis)
    return lax.ppermute(value, axis, [(i, i ^ 1) for i in range(count)])


def shards(points, right_side, skel_sub, skel_group, skel_top, neighbors, counts):
    leaves = lax.axis_size("leaf")
    sent, g, t1, x, b = start_call(points, right_side, skel_sub, skel_group, leaves)
    odd, even = swap_both(*pack_call(x, b))
    table_ab, inner = inner_call(x, b, sent)
    up_one, sent = climb_call(exchange(sent, "leaf"), t1, inner)
    other = swapped(sent, "sub")
    w = prepare_call(neighbors, counts, sent)
    sent = join_call(sent, other, w)
    parts = turns(sent, "sub", 2)
    table_a, own, row, t2 = tables_call(x, b, skel_group, skel_top, sent)
    up_two, sent = climb_four_call(parts, t2, own)
    parts = turns(sent, "group", 1)
    table_b, below_table, above_table, own = around_call(
        w, odd, even, x, b, inner, row, own, sent
    )
    u, u16, odd, even = second_call(parts, up_one, up_two, t1, t2, g, own)

    odd, even = swap_both(odd, even)
    own, weights, sums = third_call(w, u, b, u16, table_a, table_b, table_ab, g)
    sent, near = finish_call(
        w, odd, even, below_table, above_table, u, own, weights, sums, leaves
    )
    up_one, sent = climb_sums_call(exchange(sent, "leaf"), t1, level_one)
    sent = join_sums_call(sent, swapped(sent, "sub"))
    up_two, sent = climb_sums_call(turns(sent, "sub", 2), t2, level_two)
    parts = turns(sent, "group", 1)
    return last_call(parts, up_one, up_two, t1, t2, g, near, b, u)


def solution(mesh):
    return jax.shard_map(
        shards,
        mesh=mesh,
        in_specs=(
            P(ALL, None),
            P(None, ALL),
            P(("group", "sub"), None),
            P("group", None),
            P(),
            P(ALL, None),
            P(ALL),
        ),
        out_specs=(P(None, ALL), P(None, ALL)),
        check_vma=False,
    )
```
